128 devices in a mesh: ptg: 8 (over y_lo, z), img: 16 (over y_hi, x, core).
Axes of the slice: x: 4, y: 4 (y_hi: 2, y_lo: 2; y = y_hi * 2 + y_lo), z: 4, core: 2. Of those that a mesh axis runs over, the one named last changes fastest.
Arguments:
- image: bfloat16 [2048, 8192], P(None, 'img'), may hold values from -6 to 6
- beam: float32 [8, 2048, 2048], P('ptg', 'img'), may hold values from 0.2 to 1
- counts: int32 [8, 2048, 2048], P('ptg', None, 'img'), may hold values from 0 to 15
- offsets: int32 [8], P('ptg'), may hold values from 0 to 6144, as said below
Outputs:
- hessian_image: float32 [2048, 8192], P('ptg', 'img')
The draws below stay inside these ranges and needn't reach their ends.
Inputs may be any that keep to these rules, and one draw needn't show every extreme that they name: offsets rise with the pointing; the first is 0 and the last is 6144.
All inputs are finite; a program needn't handle non-finite values.
Results may differ from the reference program's by a relative error of at most 0.0095.
Values may be sent and summed in bfloat16 or wider, within the bound.
No kernel may reach another device: no remote copies, remote signals or barrier semaphores. Data moves between devices by JAX's collectives and lax.ppermute only.
A program may use at most 64 MiB of HBM per device.

```python
import math
import jax
import jax.numpy as jnp
from jax import lax

POINT = 2048
NPTG = 8
WIDTH = 8192


def draw_offsets(key, part):
    key = jax.random.fold_in(key, 5)
    span = WIDTH - POINT
    index_ptg = jnp.arange(NPTG, dtype=jnp.int32)
    base = index_ptg * span // (NPTG - 1)
    reach = span // (4 * (NPTG - 1))
    jitter = jax.random.randint(key, (NPTG,), -reach, reach + 1, dtype=jnp.int32)
    inner = (index_ptg > 0) & (index_ptg < NPTG - 1)
    return jnp.clip(base + jnp.where(inner, jitter, 0), 0, span).astype(jnp.int32)


def set_ends(entries, own_key, least, largest):
    extent = entries.shape
    place = [jax.random.randint(jax.random.fold_in(own_key, axis), (), 0, extent[axis]) for axis in range(len(extent))]
    entries = entries.at[tuple(place)].set(least)
    longest = extent.index(max(extent))
    place[longest] = (place[longest] + 1) % extent[longest]
    return entries.at[tuple(place)].set(largest)


def level_of(key, dims, split, least, high):
    def one(dim, shards_of):
        heights = jax.random.uniform(jax.random.fold_in(jax.random.fold_in(key, 6), dim), (shards_of,), jnp.float32, least / len(split), high / len(split))
        return jnp.repeat(jnp.exp(heights), dims[dim] // shards_of).reshape((-1,) + (1,) * (len(dims) - dim - 1))

    gain = one(*split[0])
    for cut in split[1:]:
        gain = gain * one(*cut)
    return gain


def noise(stream_key, extent, spread, bound, split=(), held_as=jnp.bfloat16):
    gain = level_of(stream_key, extent, split, -0.22, 0.18) if split else 1.0
    values = jax.random.normal(stream_key, extent, jnp.float32) * spread * gain
    return jnp.minimum(jnp.maximum(values, -bound), bound).astype(held_as)


def setup_inputs(seed: int = 0) -> dict:
    key_list = jax.random.split(jax.random.key(seed), 5)
    image = noise(key_list[0], (POINT, WIDTH), 1.0, 6.0, ((1, 16),))
    beam = jnp.clip(0.2 + 0.8 * jax.random.uniform(key_list[1], (NPTG, POINT, POINT), jnp.float32) ** level_of(key_list[1], (NPTG, POINT, POINT), ((0, 8), (1, 16)), -0.2, 0.2), 0.2, 1.0)
    counts = set_ends(jax.random.randint(key_list[2], (NPTG, POINT, POINT), 0, 16), jax.random.fold_in(key_list[2], 1), 0, 15).astype(jnp.int32)
    offsets = draw_offsets(jax.random.fold_in(key_list[4], 71), 0)
    return {"image": image, "beam": beam, "counts": counts, "offsets": offsets}


def tables(points):
    index_row = jnp.arange(points, dtype=jnp.int32)
    phase = (index_row[:, None] * index_row[None, :]) % points
    angle = phase.astype(jnp.float32) * (2.0 * math.pi / points)
    return jnp.cos(angle).astype(jnp.bfloat16), (-jnp.sin(angle)).astype(jnp.bfloat16)


def reference(image, beam, counts, offsets):
    cosine, sine_table = tables(POINT)
    total = jnp.zeros((POINT, WIDTH), jnp.float32)
    for pointing in range(NPTG):
        start = offsets[pointing].astype(jnp.int32)
        window = lax.dynamic_slice_in_dim(image, start, POINT, 1)
        beamed = (beam[pointing] * window.astype(jnp.float32)).astype(jnp.bfloat16)
        row_real = jnp.dot(beamed, cosine, preferred_element_type=jnp.float32).astype(jnp.bfloat16)
        row_imag = jnp.dot(beamed, sine_table, preferred_element_type=jnp.float32).astype(jnp.bfloat16)
        spec_real = jnp.dot(cosine, row_real, preferred_element_type=jnp.float32) - jnp.dot(sine_table, row_imag, preferred_element_type=jnp.float32)
        spec_imag = jnp.dot(sine_table, row_real, preferred_element_type=jnp.float32) + jnp.dot(cosine, row_imag, preferred_element_type=jnp.float32)
        weight = counts[pointing].astype(jnp.float32) / float(POINT * POINT)
        weighted_real = (weight * spec_real).astype(jnp.bfloat16)
        weighted_imag = (weight * spec_imag).astype(jnp.bfloat16)
        back_real = (jnp.dot(cosine, weighted_real, preferred_element_type=jnp.float32) + jnp.dot(sine_table, weighted_imag, preferred_element_type=jnp.float32)).astype(jnp.bfloat16)
        back_imag = (jnp.dot(cosine, weighted_imag, preferred_element_type=jnp.float32) - jnp.dot(sine_table, weighted_real, preferred_element_type=jnp.float32)).astype(jnp.bfloat16)
        image_real = jnp.dot(back_real, cosine, preferred_element_type=jnp.float32) + jnp.dot(back_imag, sine_table, preferred_element_type=jnp.float32)
        contribution = (beam[pointing] * image_real).astype(jnp.bfloat16)
        current = lax.dynamic_slice_in_dim(total, start, POINT, 1)
        total = lax.dynamic_update_slice_in_dim(total, current + contribution.astype(jnp.float32), start, 1)
    return total
```

```python
import numpy as np

import jax
import jax.numpy as jnp
from jax import lax
from jax.sharding import PartitionSpec as P


def first_frequency(device, devices, points):
    half = points // devices // 2
    low = device < devices // 2
    return np.where(low, 2 * half * device, 2 * half * (devices - 1 - device) + half)


def tables(points, devices):
    index = np.arange(points)
    angle = 2.0 * np.pi / points * np.arange(points)
    cos_of, sin_of = np.cos(angle), -np.sin(angle)
    phase = index[:, None] * index[None, :] % points
    half = points // devices // 2
    device = np.arange(devices)
    freq = first_frequency(device, devices, points)[:, None] + np.arange(half)[None, :]
    row_phase = index[:, None, None] * freq[None] % points
    row_imag = sin_of[row_phase]
    row_imag[:, 0, 0] = cos_of[index * (points // 2) % points]
    row = np.concatenate([cos_of[row_phase], row_imag], axis=2).reshape(points, points)
    as_bf16 = lambda t: jnp.asarray(t.astype(np.float32)).astype(jnp.bfloat16)
    return as_bf16(cos_of[phase]), as_bf16(sin_of[phase]), as_bf16(row)


def dot(a, b, dims=((1,), (0,))):
    return lax.dot_general(a, b, (dims, ((), ())), preferred_element_type=jnp.float32)


def paired_weights(counts, devices):
    points = counts.shape[0]
    me = lax.axis_index("img")
    low = me < devices // 2
    held = counts.astype(jnp.bfloat16)
    half = held.shape[1] // 2
    lower, upper = held[:, :half], held[:, half:]
    other = lax.ppermute(upper, "img", [(i, devices - 1 - i) for i in range(devices)])
    edge = lax.ppermute(
        held[:, 0].reshape(points // 128, 128),
        "img",
        [(i, (devices - i) % (devices // 2)) for i in range(devices // 2, devices)],
    ).reshape(points, 1)
    direct = jnp.where(low, lower, other).astype(jnp.float32)
    mirror = jnp.where(low, other, lower)
    first = jnp.where(low, jnp.where(me == 0, held[:, :1], edge), upper[:, :1])
    mirror = jnp.concatenate([first, jnp.flip(mirror, 1)[:, : half - 1], edge], 1)
    mirror = jnp.concatenate([mirror[:1], jnp.flip(mirror[1:], 0)], 0).astype(jnp.float32)
    nyquist = 0.5 * (edge.astype(jnp.float32) + mirror[:, half:])
    weight = direct + mirror[:, :half]
    zero = me == 0
    left = jnp.where(zero, 0.5, 1.0) * weight[:, :1]
    right = jnp.where(zero, nyquist, weight[:, :1])
    return jnp.concatenate([left, weight[:, 1:], right, weight[:, 1:]], 1)


def shards(image, beam, counts, offsets):
    points = counts.shape[1]
    devices = lax.axis_size("img")
    pointings = lax.axis_size("ptg")
    rows = points // devices
    start = offsets[0]
    me = lax.axis_index("img")
    ptg = lax.axis_index("ptg")
    cosine, sine_table, row_table = tables(points, devices)
    starts = lax.all_gather(offsets, "ptg", axis=0, tiled=True)
    strip = lax.all_to_all(image, "img", split_axis=0, concat_axis=1, tiled=True)
    weight = paired_weights(counts[0], devices) * (1.0 / float(points * points))
    window = lax.dynamic_slice_in_dim(strip, start, points, 1)
    beamed = (beam[0] * window.astype(jnp.float32)).astype(jnp.bfloat16)
    row = dot(beamed, row_table).astype(jnp.bfloat16)
    col = lax.all_to_all(row, "img", split_axis=1, concat_axis=0, tiled=True)
    by_cos, by_sin = dot(cosine, col), dot(sine_table, col)
    half = col.shape[1] // 2
    sign = jnp.where(jnp.arange(2 * half) < half, -1.0, 1.0)
    packed = (me == 0) & (jnp.arange(2 * half) % half == 0)
    swap = lambda t: jnp.concatenate([t[:, half:], t[:, :half]], 1)
    upper = weight * (by_cos + jnp.where(packed, 0.0, sign * swap(by_sin)))
    lower = jnp.where(packed, weight * by_sin, -sign * swap(upper))
    back = (
        dot(cosine, upper.astype(jnp.bfloat16)) + dot(sine_table, lower.astype(jnp.bfloat16))
    ).astype(jnp.bfloat16)
    spectrum_rows = lax.all_to_all(back, "img", split_axis=0, concat_axis=1, tiled=True)
    pixels = dot(spectrum_rows, row_table, ((1,), (1,)))
    contribution = (beam[0] * pixels).astype(jnp.bfloat16)
    twice = jnp.concatenate([contribution, contribution], 1)
    by_class = lax.dynamic_slice_in_dim(twice, (points - start % points) % points, points, 1)
    share = points // pointings
    terms = lax.all_to_all(by_class, "ptg", split_axis=1, concat_axis=0, tiled=True)
    terms = terms.reshape(pointings, rows, share).astype(jnp.float32)
    laps = strip.shape[1] // points
    column = jnp.arange(laps)[:, None] * points + ptg * share + jnp.arange(share)[None, :]
    sums = 0.0
    for p in range(pointings):
        inside = (column >= starts[p]) & (column < starts[p] + points)
        sums = sums + jnp.where(inside[:, None, :], terms[p][None], 0.0)
    sums = sums.astype(jnp.bfloat16).reshape(2, laps // 2, rows, share)
    core = me % 2
    mine = lax.dynamic_index_in_dim(sums, core, 0, keepdims=False)
    theirs = lax.dynamic_index_in_dim(sums, 1 - core, 0, keepdims=False)
    got = lax.ppermute(theirs, "img", [(i, i ^ 1) for i in range(devices)])
    both = jnp.where(
        core == 0, jnp.concatenate([mine, got], 1), jnp.concatenate([got, mine], 1)
    )
    tile = strip.shape[1] // devices
    per_lap = points // tile
    halves = tile // share
    received = []
    for turn in range(2):
        pairs = []
        for q in range(pointings):
            for i in range(devices):
                lap = 2 * (i % 2) + (turn ^ (q % 2))
                pairs.append((q * devices + i, (i // 2) * devices + per_lap * lap + q // halves))
        block = lax.dynamic_index_in_dim(both, turn ^ (ptg % 2), 0, keepdims=False)
        received.append(lax.ppermute(block, ("ptg", "img"), pairs))
    odd = (me // per_lap) % 2 == 1
    out = jnp.where(
        odd,
        jnp.concatenate([received[1], received[0]], 1),
        jnp.concatenate([received[0], received[1]], 1),
    )
    return out.astype(jnp.float32)


def solution(mesh):
    return jax.shard_map(
        shards,
        mesh=mesh,
        in_specs=(P(None, "img"), P("ptg", "img", None), P("ptg", None, "img"), P("ptg")),
        out_specs=P("ptg", "img"),
        check_vma=False,
    )
```

```python
import functools

import numpy as np

import jax
import jax.numpy as jnp
from jax import lax
from jax.experimental import pallas as pl
from jax.experimental.pallas import tpu as pltpu
from jax.sharding import PartitionSpec as P

F32, BF16 = jnp.float32, jnp.bfloat16
NT = (((1,), (1,)), ((), ()))
NN = (((1,), (0,)), ((), ()))
VMEM = pl.BlockSpec(memory_space=pltpu.VMEM)
SMEM = pl.BlockSpec(memory_space=pltpu.SMEM)


def dot(a, b, dims=NN):
    return lax.dot_general(a, b, dims, preferred_element_type=F32)


def row_tables(points, devices):
    half, lanes = points // 2, points // devices
    index = np.arange(half)
    turn = 2.0 * np.pi / points * np.arange(points)
    cos_of, sin_of = np.cos(turn), -np.sin(turn)
    made = []
    for odd in (0, 1):
        blocks = np.arange(devices // 2)
        if odd:
            blocks = blocks[::-1]
        freq = lanes * blocks[:, None] + 2 * np.arange(lanes // 2)[None, :] + odd
        phase = index[:, None, None] * freq[None] % points
        imag = sin_of[phase]
        if not odd:
            imag[:, 0, 0] = cos_of[index * half % points]
        made.append(np.concatenate([cos_of[phase], imag], axis=2).reshape(half, half))
    return np.stack(made)


def column_tables(points):
    half = points // 2
    index = np.arange(half)
    turn = 2.0 * np.pi / points * np.arange(points)
    cos_of, sin_of = np.cos(turn), -np.sin(turn)
    even = index[:, None] * (2 * index[None, :]) % points
    odd = index[:, None] * (2 * index[None, :] + 1) % points
    return [
        cos_of[even].T,
        sin_of[even].T,
        cos_of[odd].T,
        sin_of[odd].T,
        cos_of[odd],
        sin_of[odd],
    ]


def bf16(table):
    return jnp.asarray(np.asarray(table, np.float32).astype(jnp.bfloat16))


def lane_choice(lanes):
    half = lanes // 2
    k = np.arange(half)
    chosen = np.zeros((2, lanes, 2, 2, half), np.float32)
    for copy in (0, 1):
        chosen[0, 2 * k, 0, copy, k] = 1
        chosen[0, 2 * k + 1, 1, copy, k] = 1
        chosen[1, lanes - 1 - 2 * k, 0, copy, k] = 1
        chosen[1, lanes - 2 * k[1:], 1, copy, k[1:]] = 1
    return chosen.reshape(2, lanes, 4 * half)


def row_choice():
    k = np.arange(128)
    direct, negated = np.zeros((256, 256), np.float32), np.zeros((256, 256), np.float32)
    direct[k, 2 * k] = 1
    direct[128 + k, 2 * k + 1] = 1
    negated[k[1:], 256 - 2 * k[1:]] = 1
    negated[128 + k, 255 - 2 * k] = 1
    return direct, negated


def choose_kernel(counts_ref, choice_ref, first_ref, own_ref, send_ref, edge_ref):
    points = counts_ref.shape[0]
    lane = lax.broadcasted_iota(jnp.int32, (256, 128), 1)
    for b in range(points // 512):
        low = counts_ref[pl.ds(256 * b, 256)].astype(F32).astype(BF16)
        high = counts_ref[pl.ds(256 * b + points // 2, 256)].astype(F32).astype(BF16)
        got_low, got_high = dot(low, choice_ref[...]), dot(high, choice_ref[...])
        own_ref[pl.ds(256 * b, 256)] = got_low[:, :128].astype(BF16)
        own_ref[pl.ds(256 * b + points // 2, 256)] = got_high[:, :128].astype(BF16)
        send_ref[pl.ds(256 * b, 256)] = jnp.where(
            lane < 64, got_low[:, 128:], got_high[:, 128:]
        ).astype(BF16)
    edges = []
    for b in range(points // 128):
        block = counts_ref[pl.ds(128 * b, 128)].astype(F32).astype(BF16)
        edges.append(dot(first_ref[...], block, NT)[:1])
    edge_ref[...] = jnp.concatenate(edges, 0).astype(BF16)


def weight_kernel(me_ref, own_ref, got_ref, edge_ref, eye_ref, direct_ref, negated_ref, out_ref, plus, minus):
    points = own_ref.shape[0]
    me = me_ref[0]
    low, zero = me < 8, me == 0
    edge = dot(eye_ref[...], edge_ref[...], NT)
    lane = lax.broadcasted_iota(jnp.int32, (128, 128), 1)
    for b in range(points // 128):
        rows = pl.ds(128 * b, 128)
        own = own_ref[rows].astype(F32)
        packed = got_ref[pl.ds(128 * b % (points // 2), 128)].astype(F32)
        moved = pltpu.roll(packed, 64, 1)
        in_left = 128 * b < points // 2
        got = jnp.where((lane < 64) == in_left, packed, moved)
        column = jnp.broadcast_to(edge[:, b : b + 1], (128, 128))
        straight = jnp.where(low, own, got)
        mirrored = jnp.where(low, got, own)
        first = jnp.where(zero, jnp.where(lane == 0, own, column), column)
        mirrored = jnp.where(low & (lane % 64 == 0), first, mirrored)
        straight = jnp.where(zero & (lane == 64), column, straight)
        plus[rows] = straight.astype(BF16)
        minus[rows] = mirrored
    blocks = points // 256
    row = lax.broadcasted_iota(jnp.int32, (256, 128), 0)
    wide = lax.broadcasted_iota(jnp.int32, (256, 128), 1)
    scale = jnp.where(zero & (wide % 64 == 0), 0.5, 1.0)
    for b in range(blocks):
        taken = dot(direct_ref[...], plus[pl.ds(256 * b, 256)])
        taken += dot(negated_ref[...], minus[pl.ds(256 * (blocks - 1 - b), 256)].astype(BF16))
        wrapped = minus[pl.ds(256 * ((blocks - b) % blocks), 1)]
        taken = scale * (taken + jnp.where(row == 0, wrapped, 0.0))
        out_ref[pl.ds(128 * b, 128)] = taken[:128].astype(BF16)
        out_ref[pl.ds(points // 2 + 128 * b, 128)] = taken[128:].astype(BF16)


def row_kernel(start_ref, tiles_ref, beam_ref, table_ref, out_ref):
    tiles, rows, wide = tiles_ref.shape
    points = beam_ref.shape[1]
    start = start_ref[0]
    per_lap = points // wide
    lane = lax.broadcasted_iota(jnp.int32, (rows, wide), 1)
    beamed = []
    for block in range(per_lap):
        window = jnp.zeros((rows, wide), F32)
        for lap in range(tiles // per_lap):
            column = lane + (lap * points + block * wide)
            inside = (column >= start) & (column < start + points)
            window = jnp.where(inside, tiles_ref[lap * per_lap + block].astype(F32), window)
        beamed.append(window * beam_ref[:, pl.ds(block * wide, wide)])
    left = jnp.concatenate(beamed[: per_lap // 2], 1)
    right = jnp.concatenate(beamed[per_lap // 2 :], 1)
    blocks = out_ref.shape[0] // 2
    for odd in (0, 1):
        folded = (left - right if odd else left + right).astype(BF16)
        for part in range(blocks // 2):
            spectrum = dot(folded, table_ref[odd, :, pl.ds(256 * part, 256)]).astype(BF16)
            out_ref[odd * blocks + 2 * part] = spectrum[:, :128]
            out_ref[odd * blocks + 2 * part + 1] = spectrum[:, 128:]


def column_kernel(me_ref, x_ref, weight_ref, c0, s0, c1, s1, c1t, s1t, out_ref, upper, lower):
    points = x_ref.shape[0]
    half = points // 2
    scale = 1.0 / float(points * points)
    lane = lax.broadcasted_iota(jnp.int32, (256, 128), 1)
    sign = jnp.where(lane < 64, -1.0, 1.0)
    packed = (me_ref[0] == 0) & (lane % 64 == 0)
    first, second = x_ref[:half].astype(F32), x_ref[half:].astype(F32)
    for odd in (0, 1):
        folded = (first - second if odd else first + second).astype(BF16)
        for m in range(half // 256):
            rows = pl.ds(256 * m, 256)
            by_cos = dot((c1 if odd else c0)[rows], folded)
            by_sin = dot((s1 if odd else s0)[rows], folded)
            weight = weight_ref[pl.ds(odd * half + 256 * m, 256)].astype(F32) * scale
            up = weight * (by_cos + jnp.where(packed, 0.0, sign * pltpu.roll(by_sin, 64, 1)))
            down = jnp.where(packed, weight * by_sin, -sign * pltpu.roll(up, 64, 1))
            upper[odd, rows] = up.astype(BF16)
            lower[odd, rows] = down.astype(BF16)
    for m in range(half // 256):
        rows = pl.ds(256 * m, 256)
        even = dot(c0[rows], upper[0]) + dot(s0[rows], lower[0])
        odd = dot(c1t[rows], upper[1]) + dot(s1t[rows], lower[1])
        out_ref[rows] = (even + odd).astype(BF16)
        out_ref[pl.ds(half + 256 * m, 256)] = (even - odd).astype(BF16)


def pixel_kernel(x_ref, beam_ref, table_ref, out_ref):
    blocks, rows, _ = x_ref.shape
    half = beam_ref.shape[1] // 2
    share = out_ref.shape[2]
    even = jnp.concatenate([x_ref[b] for b in range(blocks // 2)], 1)
    odd = jnp.concatenate([x_ref[b] for b in range(blocks // 2, blocks)], 1)
    for part in range(half // share):
        lanes = pl.ds(share * part, share)
        by_even = dot(even, table_ref[0, lanes, :], NT)
        by_odd = dot(odd, table_ref[1, lanes, :], NT)
        out_ref[part] = (beam_ref[:, lanes] * (by_even + by_odd)).astype(BF16)
        late = pl.ds(half + share * part, share)
        out_ref[part + half // share] = (beam_ref[:, late] * (by_even - by_odd)).astype(BF16)


def sum_kernel(points, me_ref, starts_ref, terms_ref, mine_ref, theirs_ref):
    pointings, rows, share = terms_ref.shape
    ptg, core = me_ref[0], me_ref[1]
    lane = lax.broadcasted_iota(jnp.int32, (rows, share), 1)
    for ref, side in ((mine_ref, core), (theirs_ref, 1 - core)):
        for turn in range(2):
            lap = 2 * side + jnp.where(ptg % 2 == turn, 0, 1)
            column = lane + (lap * points + ptg * share)
            total = jnp.zeros((rows, share), F32)
            for p in range(pointings):
                inside = (column >= starts_ref[p]) & (column < starts_ref[p] + points)
                total += jnp.where(inside, terms_ref[p].astype(F32), 0.0)
            ref[turn] = total.astype(BF16)


def call(kernel, outs, specs, *args, scratch=(), flops=0, moved=4 << 20, limit=48):
    return pl.pallas_call(
        kernel,
        out_shape=outs,
        in_specs=specs,
        out_specs=jax.tree.map(lambda _: VMEM, outs),
        scratch_shapes=list(scratch),
        compiler_params=pltpu.CompilerParams(vmem_limit_bytes=limit << 20),
        cost_estimate=pl.CostEstimate(flops=flops, bytes_accessed=moved, transcendentals=0),
    )(*args)


def shape(*dims, dtype=BF16):
    return jax.ShapeDtypeStruct(dims, dtype)


def shards(image, beam, counts, offsets):
    points = counts.shape[1]
    devices = lax.axis_size("img")
    pointings = lax.axis_size("ptg")
    rows = points // devices
    tile = image.shape[1]
    me = lax.axis_index("img").astype(jnp.int32)
    ptg = lax.axis_index("ptg").astype(jnp.int32)
    start = offsets[0]
    place = me.reshape(1)

    tiles = lax.all_to_all(image, "img", split_axis=0, concat_axis=0, tiled=True)
    tiles = tiles.reshape(devices, rows, tile)

    starts = jnp.where(jnp.arange(pointings) == ptg, start, 0)
    for bit in (1, 2, 4):
        starts = starts + lax.ppermute(starts, "ptg", [(p, p ^ bit) for p in range(pointings)])

    choice = bf16(lane_choice(counts.shape[2]))
    choice = jnp.where(me < devices // 2, choice[0], choice[1])
    first_lane = np.zeros((16, 128), np.float32)
    first_lane[0, 0] = 1
    own, send, edge = call(
        choose_kernel,
        (shape(points, 128), shape(points // 2, 128), shape(points // 128, 128)),
        [VMEM] * 3,
        counts[0],
        choice,
        bf16(first_lane),
        flops=points * 128 * 512,
    )
    got = lax.ppermute(send, "img", [(i, devices - 1 - i) for i in range(devices)])
    edge = lax.ppermute(
        edge,
        "img",
        [(i, (devices - i) % (devices // 2)) for i in range(devices // 2, devices)],
    )
    direct, negated = row_choice()
    weight = call(
        weight_kernel,
        shape(points, 128),
        [SMEM] + [VMEM] * 6,
        place,
        own,
        got,
        edge,
        bf16(np.eye(128)),
        bf16(direct),
        bf16(negated),
        scratch=[pltpu.VMEM((points, 128), BF16), pltpu.VMEM((points, 128), F32)],
        flops=points * 128 * 1024,
    )

    twice = jnp.concatenate([beam[0], beam[0]], 1)
    turned = lax.dynamic_slice_in_dim(twice, (points - start % points) % points, points, 1)
    row_table = bf16(row_tables(points, devices))
    spectrum = call(
        row_kernel,
        shape(devices, rows, 128),
        [SMEM] + [VMEM] * 3,
        start.reshape(1),
        tiles,
        turned,
        row_table,
        flops=rows * points * points,
    )
    col = lax.all_to_all(spectrum, "img", split_axis=0, concat_axis=0, tiled=True)
    back = call(
        column_kernel,
        shape(points, 128),
        [SMEM] + [VMEM] * 8,
        place,
        col.reshape(points, 128),
        weight,
        *[bf16(t) for t in column_tables(points)],
        scratch=[pltpu.VMEM((2, points // 2, 128), BF16)] * 2,
        flops=8 * points * points * 128 // 2,
        moved=16 << 20,
    )
    lines = lax.all_to_all(
        back.reshape(devices, rows, 128), "img", split_axis=0, concat_axis=0, tiled=True
    )
    share = points // pointings
    contribution = call(
        pixel_kernel,
        shape(pointings, rows, share),
        [VMEM] * 3,
        lines,
        turned,
        row_table,
        flops=rows * points * points,
    )
    terms = lax.all_to_all(contribution, "ptg", split_axis=0, concat_axis=0, tiled=True)
    mine, theirs = call(
        functools.partial(sum_kernel, points),
        (shape(2, rows, share), shape(2, rows, share)),
        [SMEM, SMEM, VMEM],
        jnp.stack([ptg, me % 2]),
        starts,
        terms,
        moved=1 << 20,
    )
    other = lax.ppermute(theirs, "img", [(i, i ^ 1) for i in range(devices)])
    per_lap = points // tile
    halves = tile // share
    received = []
    for turn in range(2):
        pairs = []
        for q in range(pointings):
            for i in range(devices):
                lap = 2 * (i % 2) + (turn ^ (q % 2))
                pairs.append((q * devices + i, (i // 2) * devices + per_lap * lap + q // halves))
        block = jnp.concatenate([mine[turn], other[turn]], 0)
        received.append(lax.ppermute(block, ("ptg", "img"), pairs))
    lap = me // per_lap
    out = jnp.where(
        lap % 2 == 1,
        jnp.concatenate([received[1], received[0]], 1),
        jnp.concatenate([received[0], received[1]], 1),
    ).astype(F32)
    flipped = jnp.concatenate([out[rows:], out[:rows]], 0)
    return jnp.where(lap >= 2, flipped, out)


def solution(mesh):
    return jax.shard_map(
        shards,
        mesh=mesh,
        in_specs=(P(None, "img"), P("ptg", "img", None), P("ptg", None, "img"), P("ptg")),
        out_specs=P("ptg", "img"),
        check_vma=False,
    )
```

```python
import functools

import numpy as np

import jax
import jax.numpy as jnp
from jax import lax
from jax.experimental import pallas as pl
from jax.experimental.pallas import tpu as pltpu
from jax.sharding import PartitionSpec as P

F32, BF16 = jnp.float32, jnp.bfloat16
NT = (((1,), (1,)), ((), ()))
NN = (((1,), (0,)), ((), ()))
VMEM = pl.BlockSpec(memory_space=pltpu.VMEM)
SMEM = pl.BlockSpec(memory_space=pltpu.SMEM)


def dot(a, b, dims=NN):
    return lax.dot_general(a, b, dims, preferred_element_type=F32)


def row_tables(points, devices):
    half, lanes = points // 2, points // devices
    index = np.arange(half)
    turn = 2.0 * np.pi / points * np.arange(points)
    cos_of, sin_of = np.cos(turn), -np.sin(turn)
    made = []
    for odd in (0, 1):
        blocks = np.arange(devices // 2)
        if odd:
            blocks = blocks[::-1]
        freq = lanes * blocks[:, None] + 2 * np.arange(lanes // 2)[None, :] + odd
        phase = index[:, None, None] * freq[None] % points
        imag = sin_of[phase]
        if not odd:
            imag[:, 0, 0] = cos_of[index * half % points]
        made.append(np.concatenate([cos_of[phase], imag], axis=2).reshape(half, half))
    return np.stack(made)


def column_tables(points):
    half = points // 2
    index = np.arange(half)
    turn = 2.0 * np.pi / points * np.arange(points)
    cos_of, sin_of = np.cos(turn), -np.sin(turn)
    even = index[:, None] * (2 * index[None, :]) % points
    odd = index[:, None] * (2 * index[None, :] + 1) % points
    return [
        cos_of[even].T,
        sin_of[even].T,
        cos_of[odd].T,
        sin_of[odd].T,
        cos_of[odd],
        sin_of[odd],
    ]


def bf16(table):
    return jnp.asarray(np.asarray(table, np.float32).astype(jnp.bfloat16))


def lane_choice(lanes):
    half = lanes // 2
    k = np.arange(half)
    chosen = np.zeros((2, lanes, 2, 2, half), np.float32)
    for copy in (0, 1):
        chosen[0, 2 * k, 0, copy, k] = 1
        chosen[0, 2 * k + 1, 1, copy, k] = 1
        chosen[1, lanes - 1 - 2 * k, 0, copy, k] = 1
        chosen[1, lanes - 2 * k[1:], 1, copy, k[1:]] = 1
    return chosen.reshape(2, lanes, 4 * half)


def row_choice():
    k = np.arange(128)
    direct, negated = np.zeros((256, 256), np.float32), np.zeros((256, 256), np.float32)
    direct[k, 2 * k] = 1
    direct[128 + k, 2 * k + 1] = 1
    negated[k[1:], 256 - 2 * k[1:]] = 1
    negated[128 + k, 255 - 2 * k] = 1
    return direct, negated


def choose_kernel(counts_ref, choice_ref, first_ref, own_ref, send_ref, edge_ref):
    points = counts_ref.shape[0]
    lane = lax.broadcasted_iota(jnp.int32, (256, 128), 1)
    for b in range(points // 512):
        low = counts_ref[pl.ds(256 * b, 256)].astype(F32).astype(BF16)
        high = counts_ref[pl.ds(256 * b + points // 2, 256)].astype(F32).astype(BF16)
        got_low, got_high = dot(low, choice_ref[...]), dot(high, choice_ref[...])
        own_ref[pl.ds(256 * b, 256)] = got_low[:, :128].astype(BF16)
        own_ref[pl.ds(256 * b + points // 2, 256)] = got_high[:, :128].astype(BF16)
        send_ref[pl.ds(256 * b, 256)] = jnp.where(
            lane < 64, got_low[:, 128:], got_high[:, 128:]
        ).astype(BF16)
    edges = []
    for b in range(points // 128):
        block = counts_ref[pl.ds(128 * b, 128)].astype(F32).astype(BF16)
        edges.append(dot(first_ref[...], block, NT)[:1])
    edge_ref[...] = jnp.concatenate(edges, 0).astype(BF16)


def weight_kernel(me_ref, own_ref, got_ref, edge_ref, eye_ref, direct_ref, negated_ref, out_ref, plus, minus):
    points = own_ref.shape[0]
    me = me_ref[0]
    low, zero = me < 8, me == 0
    edge = dot(eye_ref[...], edge_ref[...], NT)
    lane = lax.broadcasted_iota(jnp.int32, (128, 128), 1)
    for b in range(points // 128):
        rows = pl.ds(128 * b, 128)
        own = own_ref[rows].astype(F32)
        packed = got_ref[pl.ds(128 * b % (points // 2), 128)].astype(F32)
        moved = pltpu.roll(packed, 64, 1)
        in_left = 128 * b < points // 2
        got = jnp.where((lane < 64) == in_left, packed, moved)
        column = jnp.broadcast_to(edge[:, b : b + 1], (128, 128))
        straight = jnp.where(low, own, got)
        mirrored = jnp.where(low, got, own)
        first = jnp.where(zero, jnp.where(lane == 0, own, column), column)
        mirrored = jnp.where(low & (lane % 64 == 0), first, mirrored)
        straight = jnp.where(zero & (lane == 64), column, straight)
        plus[rows] = straight.astype(BF16)
        minus[rows] = mirrored
    blocks = points // 256
    row = lax.broadcasted_iota(jnp.int32, (256, 128), 0)
    wide = lax.broadcasted_iota(jnp.int32, (256, 128), 1)
    scale = jnp.where(zero & (wide % 64 == 0), 0.5, 1.0)
    for b in range(blocks):
        taken = dot(direct_ref[...], plus[pl.ds(256 * b, 256)])
        taken += dot(negated_ref[...], minus[pl.ds(256 * (blocks - 1 - b), 256)].astype(BF16))
        wrapped = minus[pl.ds(256 * ((blocks - b) % blocks), 1)]
        taken = scale * (taken + jnp.where(row == 0, wrapped, 0.0))
        out_ref[pl.ds(128 * b, 128)] = taken[:128].astype(BF16)
        out_ref[pl.ds(points // 2 + 128 * b, 128)] = taken[128:].astype(BF16)


def row_kernel(start_ref, tiles_ref, beam_ref, table_ref, out_ref):
    tiles, rows, wide = tiles_ref.shape
    points = beam_ref.shape[1]
    start = start_ref[0]
    per_lap = points // wide
    lane = lax.broadcasted_iota(jnp.int32, (rows, wide), 1)
    beamed = []
    for block in range(per_lap):
        window = jnp.zeros((rows, wide), F32)
        for lap in range(tiles // per_lap):
            column = lane + (lap * points + block * wide)
            inside = (column >= start) & (column < start + points)
            window = jnp.where(inside, tiles_ref[lap * per_lap + block].astype(F32), window)
        beamed.append(window * beam_ref[:, pl.ds(block * wide, wide)])
    left = jnp.concatenate(beamed[: per_lap // 2], 1)
    right = jnp.concatenate(beamed[per_lap // 2 :], 1)
    blocks = out_ref.shape[0] // 2
    for odd in (0, 1):
        folded = (left - right if odd else left + right).astype(BF16)
        for part in range(blocks // 2):
            spectrum = dot(folded, table_ref[odd, :, pl.ds(256 * part, 256)]).astype(BF16)
            out_ref[odd * blocks + 2 * part] = spectrum[:, :128]
            out_ref[odd * blocks + 2 * part + 1] = spectrum[:, 128:]


def column_kernel(me_ref, x_ref, weight_ref, c0, s0, c1, s1, c1t, s1t, out_ref, upper, lower):
    points = x_ref.shape[0]
    half = points // 2
    scale = 1.0 / float(points * points)
    lane = lax.broadcasted_iota(jnp.int32, (256, 128), 1)
    sign = jnp.where(lane < 64, -1.0, 1.0)
    packed = (me_ref[0] == 0) & (lane % 64 == 0)
    first, second = x_ref[:half].astype(F32), x_ref[half:].astype(F32)
    for odd in (0, 1):
        folded = (first - second if odd else first + second).astype(BF16)
        for m in range(half // 256):
            rows = pl.ds(256 * m, 256)
            by_cos = dot((c1 if odd else c0)[rows], folded)
            by_sin = dot((s1 if odd else s0)[rows], folded)
            weight = weight_ref[pl.ds(odd * half + 256 * m, 256)].astype(F32) * scale
            up = weight * (by_cos + jnp.where(packed, 0.0, sign * pltpu.roll(by_sin, 64, 1)))
            down = jnp.where(packed, weight * by_sin, -sign * pltpu.roll(up, 64, 1))
            upper[odd, rows] = up.astype(BF16)
            lower[odd, rows] = down.astype(BF16)
    for m in range(half // 256):
        rows = pl.ds(256 * m, 256)
        even = dot(c0[rows], upper[0]) + dot(s0[rows], lower[0])
        odd = dot(c1t[rows], upper[1]) + dot(s1t[rows], lower[1])
        out_ref[rows] = (even + odd).astype(BF16)
        out_ref[pl.ds(half + 256 * m, 256)] = (even - odd).astype(BF16)


def pixel_kernel(x_ref, beam_ref, table_ref, out_ref):
    blocks, rows, _ = x_ref.shape
    half = beam_ref.shape[1] // 2
    share = out_ref.shape[2]
    even = jnp.concatenate([x_ref[b] for b in range(blocks // 2)], 1)
    odd = jnp.concatenate([x_ref[b] for b in range(blocks // 2, blocks)], 1)
    for part in range(half // share):
        lanes = pl.ds(share * part, share)
        by_even = dot(even, table_ref[0, lanes, :], NT)
        by_odd = dot(odd, table_ref[1, lanes, :], NT)
        out_ref[part] = (beam_ref[:, lanes] * (by_even + by_odd)).astype(BF16)
        late = pl.ds(half + share * part, share)
        out_ref[part + half // share] = (beam_ref[:, late] * (by_even - by_odd)).astype(BF16)


def sum_kernel(points, me_ref, starts_ref, terms_ref, mine_ref, theirs_ref):
    pointings, rows, share = terms_ref.shape
    ptg, core = me_ref[0], me_ref[1]
    lane = lax.broadcasted_iota(jnp.int32, (rows, share), 1)
    for ref, side in ((mine_ref, core), (theirs_ref, 1 - core)):
        for turn in range(2):
            lap = 2 * side + jnp.where(ptg % 2 == turn, 0, 1)
            column = lane + (lap * points + ptg * share)
            total = jnp.zeros((rows, share), F32)
            for p in range(pointings):
                inside = (column >= starts_ref[p]) & (column < starts_ref[p] + points)
                total += jnp.where(inside, terms_ref[p].astype(F32), 0.0)
            ref[turn] = total.astype(BF16)


def call(kernel, outs, specs, *args, scratch=(), flops=0, moved=4 << 20, limit=16):
    return pl.pallas_call(
        kernel,
        out_shape=outs,
        in_specs=specs,
        out_specs=jax.tree.map(lambda _: VMEM, outs),
        scratch_shapes=list(scratch),
        compiler_params=pltpu.CompilerParams(vmem_limit_bytes=limit << 20),
        cost_estimate=pl.CostEstimate(flops=flops, bytes_accessed=moved, transcendentals=0),
    )(*args)


def shape(*dims, dtype=BF16):
    return jax.ShapeDtypeStruct(dims, dtype)


def shards(image, beam, counts, offsets):
    points = counts.shape[1]
    devices = lax.axis_size("img")
    pointings = lax.axis_size("ptg")
    rows = points // devices
    tile = image.shape[1]
    me = lax.axis_index("img").astype(jnp.int32)
    ptg = lax.axis_index("ptg").astype(jnp.int32)
    start = offsets[0]
    place = me.reshape(1)

    tiles = lax.all_to_all(image, "img", split_axis=0, concat_axis=0, tiled=True)
    tiles = tiles.reshape(devices, rows, tile)

    starts = jnp.where(jnp.arange(pointings) == ptg, start, 0)
    for bit in (1, 2, 4):
        starts = starts + lax.ppermute(starts, "ptg", [(p, p ^ bit) for p in range(pointings)])

    choice = bf16(lane_choice(counts.shape[2]))
    choice = jnp.where(me < devices // 2, choice[0], choice[1])
    first_lane = np.zeros((16, 128), np.float32)
    first_lane[0, 0] = 1
    own, send, edge = call(
        choose_kernel,
        (shape(points, 128), shape(points // 2, 128), shape(points // 128, 128)),
        [VMEM] * 3,
        counts[0],
        choice,
        bf16(first_lane),
        flops=points * 128 * 512,
    )
    got = lax.ppermute(send, "img", [(i, devices - 1 - i) for i in range(devices)])
    edge = lax.ppermute(
        edge,
        "img",
        [(i, (devices - i) % (devices // 2)) for i in range(devices // 2, devices)],
    )
    direct, negated = row_choice()
    weight = call(
        weight_kernel,
        shape(points, 128),
        [SMEM] + [VMEM] * 6,
        place,
        own,
        got,
        edge,
        bf16(np.eye(128)),
        bf16(direct),
        bf16(negated),
        scratch=[pltpu.VMEM((points, 128), BF16), pltpu.VMEM((points, 128), F32)],
        flops=points * 128 * 1024,
    )

    twice = jnp.concatenate([beam[0], beam[0]], 1)
    turned = lax.dynamic_slice_in_dim(twice, (points - start % points) % points, points, 1)
    row_table = bf16(row_tables(points, devices))
    tiles, weight, starts = lax.optimization_barrier((tiles, weight, starts))
    spectrum = call(
        row_kernel,
        shape(devices, rows, 128),
        [SMEM] + [VMEM] * 3,
        start.reshape(1),
        tiles,
        turned,
        row_table,
        flops=rows * points * points,
    )
    col = lax.all_to_all(spectrum, "img", split_axis=0, concat_axis=0, tiled=True)
    back = call(
        column_kernel,
        shape(points, 128),
        [SMEM] + [VMEM] * 8,
        place,
        col.reshape(points, 128),
        weight,
        *[bf16(t) for t in column_tables(points)],
        scratch=[pltpu.VMEM((2, points // 2, 128), BF16)] * 2,
        flops=8 * points * points * 128 // 2,
        moved=16 << 20,
        limit=24,
    )
    lines = lax.all_to_all(
        back.reshape(devices, rows, 128), "img", split_axis=0, concat_axis=0, tiled=True
    )
    share = points // pointings
    contribution = call(
        pixel_kernel,
        shape(pointings, rows, share),
        [VMEM] * 3,
        lines,
        turned,
        row_table,
        flops=rows * points * points,
    )
    terms = lax.all_to_all(contribution, "ptg", split_axis=0, concat_axis=0, tiled=True)
    mine, theirs = call(
        functools.partial(sum_kernel, points),
        (shape(2, rows, share), shape(2, rows, share)),
        [SMEM, SMEM, VMEM],
        jnp.stack([ptg, me % 2]),
        starts,
        terms,
        moved=1 << 20,
    )
    other = lax.ppermute(theirs, "img", [(i, i ^ 1) for i in range(devices)])
    per_lap = points // tile
    halves = tile // share
    received = []
    for turn in range(2):
        pairs = []
        for q in range(pointings):
            for i in range(devices):
                lap = 2 * (i % 2) + (turn ^ (q % 2))
                pairs.append((q * devices + i, (i // 2) * devices + per_lap * lap + q // halves))
        block = jnp.concatenate([mine[turn], other[turn]], 0)
        received.append(lax.ppermute(block, ("ptg", "img"), pairs))
    lap = me // per_lap
    out = jnp.where(
        lap % 2 == 1,
        jnp.concatenate([received[1], received[0]], 1),
        jnp.concatenate([received[0], received[1]], 1),
    ).astype(F32)
    flipped = jnp.concatenate([out[rows:], out[:rows]], 0)
    return jnp.where(lap >= 2, flipped, out)


def solution(mesh):
    return jax.shard_map(
        shards,
        mesh=mesh,
        in_specs=(P(None, "img"), P("ptg", "img", None), P("ptg", None, "img"), P("ptg")),
        out_specs=P("ptg", "img"),
        check_vma=False,
    )
```

```python
import functools

import numpy as np

import jax
import jax.numpy as jnp
from jax import lax
from jax.experimental import pallas as pl
from jax.experimental.pallas import tpu as pltpu
from jax.sharding import Mesh, PartitionSpec as P

F32, BF16 = jnp.float32, jnp.bfloat16
NT = (((1,), (1,)), ((), ()))
NN = (((1,), (0,)), ((), ()))
VMEM = pl.BlockSpec(memory_space=pltpu.VMEM)
HBM = pl.BlockSpec(memory_space=pltpu.HBM)
SMEM = pl.BlockSpec(memory_space=pltpu.SMEM)


def dot(a, b, dims=NN):
    return lax.dot_general(a, b, dims, preferred_element_type=F32)


def row_tables(points, devices):
    half, lanes = points // 2, points // devices
    index = np.arange(half)
    turn = 2.0 * np.pi / points * np.arange(points)
    cos_of, sin_of = np.cos(turn), -np.sin(turn)
    made = []
    for odd in (0, 1):
        blocks = np.arange(devices // 2)
        if odd:
            blocks = blocks[::-1]
        freq = lanes * blocks[:, None] + 2 * np.arange(lanes // 2)[None, :] + odd
        phase = index[:, None, None] * freq[None] % points
        imag = sin_of[phase]
        if not odd:
            imag[:, 0, 0] = cos_of[index * half % points]
        made.append(np.concatenate([cos_of[phase], imag], axis=2).reshape(half, half))
    return np.stack(made)


def column_tables(points):
    half = points // 2
    index = np.arange(half)
    turn = 2.0 * np.pi / points * np.arange(points)
    cos_of, sin_of = np.cos(turn), -np.sin(turn)
    even = index[:, None] * (2 * index[None, :]) % points
    odd = index[:, None] * (2 * index[None, :] + 1) % points
    return [
        cos_of[even].T,
        sin_of[even].T,
        cos_of[odd].T,
        sin_of[odd].T,
        cos_of[odd],
        sin_of[odd],
    ]


def bf16(table):
    return jnp.asarray(np.asarray(table, np.float32).astype(jnp.bfloat16))


def lane_choice(lanes):
    half = lanes // 2
    k = np.arange(half)
    chosen = np.zeros((2, lanes, 2, 2, half), np.float32)
    for copy in (0, 1):
        chosen[0, 2 * k, 0, copy, k] = 1
        chosen[0, 2 * k + 1, 1, copy, k] = 1
        chosen[1, lanes - 1 - 2 * k, 0, copy, k] = 1
        chosen[1, lanes - 2 * k[1:], 1, copy, k[1:]] = 1
    return chosen.reshape(2, lanes, 4 * half)


def row_choice():
    k = np.arange(128)
    direct, negated = np.zeros((256, 256), np.float32), np.zeros((256, 256), np.float32)
    direct[k, 2 * k] = 1
    direct[128 + k, 2 * k + 1] = 1
    negated[k[1:], 256 - 2 * k[1:]] = 1
    negated[128 + k, 255 - 2 * k] = 1
    return direct, negated


def choose_kernel(counts_ref, choice_ref, first_ref, own_ref, send_ref, edge_ref):
    points = counts_ref.shape[0]
    lane = lax.broadcasted_iota(jnp.int32, (256, 128), 1)
    for b in range(points // 512):
        low = counts_ref[pl.ds(256 * b, 256)].astype(F32).astype(BF16)
        high = counts_ref[pl.ds(256 * b + points // 2, 256)].astype(F32).astype(BF16)
        got_low, got_high = dot(low, choice_ref[...]), dot(high, choice_ref[...])
        own_ref[pl.ds(256 * b, 256)] = got_low[:, :128].astype(BF16)
        own_ref[pl.ds(256 * b + points // 2, 256)] = got_high[:, :128].astype(BF16)
        send_ref[pl.ds(256 * b, 256)] = jnp.where(
            lane < 64, got_low[:, 128:], got_high[:, 128:]
        ).astype(BF16)
    edges = []
    for b in range(points // 128):
        block = counts_ref[pl.ds(128 * b, 128)].astype(F32).astype(BF16)
        edges.append(dot(first_ref[...], block, NT)[:1])
    edge_ref[...] = jnp.concatenate(edges, 0).astype(BF16)


def weight_kernel(me_ref, own_ref, got_ref, edge_ref, eye_ref, direct_ref, negated_ref, out_ref, plus, minus):
    points = own_ref.shape[0]
    me = me_ref[0]
    low, zero = me < 8, me == 0
    edge = dot(eye_ref[...], edge_ref[...], NT)
    lane = lax.broadcasted_iota(jnp.int32, (128, 128), 1)
    for b in range(points // 128):
        rows = pl.ds(128 * b, 128)
        own = own_ref[rows].astype(F32)
        packed = got_ref[pl.ds(128 * b % (points // 2), 128)].astype(F32)
        moved = pltpu.roll(packed, 64, 1)
        in_left = 128 * b < points // 2
        got = jnp.where((lane < 64) == in_left, packed, moved)
        column = jnp.broadcast_to(edge[:, b : b + 1], (128, 128))
        straight = jnp.where(low, own, got)
        mirrored = jnp.where(low, got, own)
        first = jnp.where(zero, jnp.where(lane == 0, own, column), column)
        mirrored = jnp.where(low & (lane % 64 == 0), first, mirrored)
        straight = jnp.where(zero & (lane == 64), column, straight)
        plus[rows] = straight.astype(BF16)
        minus[rows] = mirrored
    blocks = points // 256
    row = lax.broadcasted_iota(jnp.int32, (256, 128), 0)
    wide = lax.broadcasted_iota(jnp.int32, (256, 128), 1)
    scale = jnp.where(zero & (wide % 64 == 0), 0.5, 1.0)
    for b in range(blocks):
        taken = dot(direct_ref[...], plus[pl.ds(256 * b, 256)])
        taken += dot(negated_ref[...], minus[pl.ds(256 * (blocks - 1 - b), 256)].astype(BF16))
        wrapped = minus[pl.ds(256 * ((blocks - b) % blocks), 1)]
        taken = scale * (taken + jnp.where(row == 0, wrapped, 0.0))
        out_ref[pl.ds(128 * b, 128)] = taken[:128].astype(BF16)
        out_ref[pl.ds(points // 2 + 128 * b, 128)] = taken[128:].astype(BF16)


class Stream:
    def __init__(self, pieces, sems, ahead=6):
        self.copies = [
            pltpu.make_async_copy(source, target, sems.at[n])
            for n, (source, target) in enumerate(pieces)
        ]
        self.ahead, self.taken = ahead, 0
        for copy in self.copies[:ahead]:
            copy.start()

    def take(self):
        self.copies[self.taken].wait()
        if self.taken + self.ahead < len(self.copies):
            self.copies[self.taken + self.ahead].start()
        self.taken += 1


def pick_kernel(points, place_ref, starts_ref, tiles_ref, out_ref):
    laps, parts, rows, wide = tiles_ref.shape
    lane = lax.broadcasted_iota(jnp.int32, (rows, wide), 1) + place_ref[0] * wide
    for part in range(parts):
        held = [tiles_ref[lap, part].astype(F32) for lap in range(laps)]
        for p in range(out_ref.shape[0]):
            start = starts_ref[p]
            window = jnp.zeros((rows, wide), F32)
            for lap in range(laps):
                column = lane + lap * points
                inside = (column >= start) & (column < start + points)
                window = jnp.where(inside, held[lap], window)
            out_ref[p, part] = window.astype(BF16)


def row_kernel(window_ref, beam_ref, source_ref, out_ref, table_ref, sems):
    shares, parts, rows, wide = window_ref.shape
    blocks = out_ref.shape[0] // 2
    places = [(odd, pl.ds(256 * part, 256)) for odd in (0, 1) for part in range(blocks // 2)]
    stream = Stream(
        [(source_ref.at[odd, :, lanes], table_ref.at[odd, :, lanes]) for odd, lanes in places],
        sems,
    )
    beamed = []
    for part in range(parts):
        window = jnp.concatenate([window_ref[q, part] for q in range(shares)], 0)
        beamed.append(window.astype(F32) * beam_ref[:, pl.ds(part * wide, wide)])
    left = jnp.concatenate(beamed[: parts // 2], 1)
    right = jnp.concatenate(beamed[parts // 2 :], 1)
    for odd in (0, 1):
        folded = (left - right if odd else left + right).astype(BF16)
        for part in range(blocks // 2):
            stream.take()
            spectrum = dot(folded, table_ref[odd, :, pl.ds(256 * part, 256)]).astype(BF16)
            out_ref[odd * blocks + 2 * part] = spectrum[:, :128]
            out_ref[odd * blocks + 2 * part + 1] = spectrum[:, 128:]


def column_kernel(me_ref, x_ref, weight_ref, source_ref, out_ref, upper, lower, table_ref, sems):
    c0, s0, c1, s1, c1t, s1t = (table_ref.at[t] for t in range(6))
    points = x_ref.shape[0]
    half = points // 2
    places = [
        (t, pl.ds(256 * m, 256))
        for pair in (0, 2, 4)
        for m in range(half // 256)
        for t in (pair, pair + 1)
    ]
    stream = Stream(
        [(source_ref.at[t, rows], table_ref.at[t, rows]) for t, rows in places], sems
    )
    scale = 1.0 / float(points * points)
    lane = lax.broadcasted_iota(jnp.int32, (256, 128), 1)
    sign = jnp.where(lane < 64, -1.0, 1.0)
    packed = (me_ref[0] == 0) & (lane % 64 == 0)
    first, second = x_ref[:half].astype(F32), x_ref[half:].astype(F32)
    for odd in (0, 1):
        folded = (first - second if odd else first + second).astype(BF16)
        for m in range(half // 256):
            rows = pl.ds(256 * m, 256)
            stream.take()
            stream.take()
            by_cos = dot((c1 if odd else c0)[rows, :], folded)
            by_sin = dot((s1 if odd else s0)[rows, :], folded)
            weight = weight_ref[pl.ds(odd * half + 256 * m, 256)].astype(F32) * scale
            up = weight * (by_cos + jnp.where(packed, 0.0, sign * pltpu.roll(by_sin, 64, 1)))
            down = jnp.where(packed, weight * by_sin, -sign * pltpu.roll(up, 64, 1))
            upper[odd, rows] = up.astype(BF16)
            lower[odd, rows] = down.astype(BF16)
    for m in range(half // 256):
        rows = pl.ds(256 * m, 256)
        stream.take()
        stream.take()
        even = dot(c0[rows, :], upper[0]) + dot(s0[rows, :], lower[0])
        odd = dot(c1t[rows, :], upper[1]) + dot(s1t[rows, :], lower[1])
        out_ref[rows] = (even + odd).astype(BF16)
        out_ref[pl.ds(half + 256 * m, 256)] = (even - odd).astype(BF16)


def pixel_kernel(x_ref, beam_ref, source_ref, out_ref, table_ref, sems):
    blocks, rows, _ = x_ref.shape
    half = beam_ref.shape[1] // 2
    share = out_ref.shape[2]
    places = [(odd, pl.ds(share * part, share)) for part in range(half // share) for odd in (0, 1)]
    stream = Stream(
        [(source_ref.at[odd, lanes], table_ref.at[odd, lanes]) for odd, lanes in places], sems
    )
    even = jnp.concatenate([x_ref[b] for b in range(blocks // 2)], 1)
    odd = jnp.concatenate([x_ref[b] for b in range(blocks // 2, blocks)], 1)
    for part in range(half // share):
        lanes = pl.ds(share * part, share)
        stream.take()
        stream.take()
        by_even = dot(even, table_ref[0, lanes, :], NT)
        by_odd = dot(odd, table_ref[1, lanes, :], NT)
        out_ref[part] = (beam_ref[:, lanes] * (by_even + by_odd)).astype(BF16)
        late = pl.ds(half + share * part, share)
        out_ref[part + half // share] = (beam_ref[:, late] * (by_even - by_odd)).astype(BF16)


def sum_kernel(points, me_ref, starts_ref, terms_ref, mine_ref, theirs_ref):
    pointings, rows, share = terms_ref.shape
    ptg, core = me_ref[0], me_ref[1]
    lane = lax.broadcasted_iota(jnp.int32, (rows, share), 1)
    for ref, side in ((mine_ref, core), (theirs_ref, 1 - core)):
        for turn in range(2):
            lap = 2 * side + jnp.where(ptg % 2 == turn, 0, 1)
            column = lane + (lap * points + ptg * share)
            total = jnp.zeros((rows, share), F32)
            for p in range(pointings):
                inside = (column >= starts_ref[p]) & (column < starts_ref[p] + points)
                total += jnp.where(inside, terms_ref[p].astype(F32), 0.0)
            ref[turn] = total.astype(BF16)


def call(kernel, outs, specs, *args, scratch=(), flops=0, moved=4 << 20, limit=16):
    return pl.pallas_call(
        kernel,
        out_shape=outs,
        in_specs=specs,
        out_specs=jax.tree.map(lambda _: VMEM, outs),
        scratch_shapes=list(scratch),
        compiler_params=pltpu.CompilerParams(vmem_limit_bytes=limit << 20),
        cost_estimate=pl.CostEstimate(flops=flops, bytes_accessed=moved, transcendentals=0),
    )(*args)


def shape(*dims, dtype=BF16):
    return jax.ShapeDtypeStruct(dims, dtype)


IMG = ("s", "b")


def shards(image, beam, counts, offsets):
    points = counts.shape[1]
    laps, parts = lax.axis_size("s"), lax.axis_size("b")
    devices = laps * parts
    pointings = lax.axis_size("ptg")
    rows = points // devices
    tile = image.shape[1]
    me = lax.axis_index(IMG).astype(jnp.int32)
    ptg = lax.axis_index("ptg").astype(jnp.int32)
    start = offsets[0]
    place = me.reshape(1)

    starts = jnp.where(jnp.arange(pointings) == ptg, start, 0)
    near = [
        lax.ppermute(starts, "ptg", [(p, p ^ bit) for p in range(pointings)]) for bit in (1, 2, 3)
    ]
    starts = starts + near[0] + near[1] + near[2]
    starts = starts + lax.ppermute(starts, "ptg", [(p, p ^ 4) for p in range(pointings)])

    share_rows = rows // pointings
    shares = image.reshape(laps, parts, pointings, share_rows, tile)
    shares = lax.dynamic_index_in_dim(shares, ptg, 2, keepdims=False)
    shares = lax.all_to_all(shares, "s", split_axis=0, concat_axis=0, tiled=True)

    choice = bf16(lane_choice(counts.shape[2]))
    choice = jnp.where(me < devices // 2, choice[0], choice[1])
    first_lane = np.zeros((16, 128), np.float32)
    first_lane[0, 0] = 1
    own, send, edge = call(
        choose_kernel,
        (shape(points, 128), shape(points // 2, 128), shape(points // 128, 128)),
        [VMEM] * 3,
        counts[0],
        choice,
        bf16(first_lane),
        flops=points * 128 * 512,
    )
    got = lax.ppermute(send, IMG, [(i, devices - 1 - i) for i in range(devices)])
    edge = lax.ppermute(
        edge,
        IMG,
        [(i, (devices - i) % (devices // 2)) for i in range(devices // 2, devices)],
    )
    direct, negated = row_choice()
    weight = call(
        weight_kernel,
        shape(points, 128),
        [SMEM] + [VMEM] * 6,
        place,
        own,
        got,
        edge,
        bf16(np.eye(128)),
        bf16(direct),
        bf16(negated),
        scratch=[pltpu.VMEM((points, 128), BF16), pltpu.VMEM((points, 128), F32)],
        flops=points * 128 * 1024,
    )

    twice = jnp.concatenate([beam[0], beam[0]], 1)
    turned = lax.dynamic_slice_in_dim(twice, (points - start % points) % points, points, 1)
    picked = call(
        functools.partial(pick_kernel, points),
        shape(pointings, parts, share_rows, tile),
        [SMEM, SMEM, VMEM],
        lax.axis_index("b").astype(jnp.int32).reshape(1),
        starts,
        shares,
        moved=1 << 20,
    )
    window = lax.all_to_all(
        picked.reshape(pointings * parts, share_rows, tile),
        ("ptg", "b"),
        split_axis=0,
        concat_axis=0,
        tiled=True,
    ).reshape(pointings, parts, share_rows, tile)
    window, weight, turned = lax.optimization_barrier((window, weight, turned))
    row_table = bf16(row_tables(points, devices))
    table_scratch = lambda tables, pieces: [
        pltpu.VMEM((tables, points // 2, points // 2), BF16),
        pltpu.SemaphoreType.DMA((pieces,)),
    ]
    spectrum = call(
        row_kernel,
        shape(devices, rows, 128),
        [VMEM, VMEM, HBM],
        window,
        turned,
        row_table,
        scratch=table_scratch(2, 8),
        flops=rows * points * points,
    )
    col = lax.all_to_all(spectrum, IMG, split_axis=0, concat_axis=0, tiled=True)
    back = call(
        column_kernel,
        shape(points, 128),
        [SMEM, VMEM, VMEM, HBM],
        place,
        col.reshape(points, 128),
        weight,
        bf16(np.stack(column_tables(points))),
        scratch=[pltpu.VMEM((2, points // 2, 128), BF16)] * 2 + table_scratch(6, 24),
        flops=8 * points * points * 128 // 2,
        moved=16 << 20,
        limit=28,
    )
    lines = lax.all_to_all(
        back.reshape(devices, rows, 128), IMG, split_axis=0, concat_axis=0, tiled=True
    )
    share = points // pointings
    contribution = call(
        pixel_kernel,
        shape(pointings, rows, share),
        [VMEM, VMEM, HBM],
        lines,
        turned,
        row_table,
        scratch=table_scratch(2, 8),
        flops=rows * points * points,
    )
    terms = lax.all_to_all(contribution, "ptg", split_axis=0, concat_axis=0, tiled=True)
    mine, theirs = call(
        functools.partial(sum_kernel, points),
        (shape(2, rows, share), shape(2, rows, share)),
        [SMEM, SMEM, VMEM],
        jnp.stack([ptg, me % 2]),
        starts,
        terms,
        moved=1 << 20,
    )
    other = lax.ppermute(theirs, IMG, [(i, i ^ 1) for i in range(devices)])
    per_lap = parts
    halves = tile // share
    received = []
    for turn in range(2):
        pairs = []
        for q in range(pointings):
            for i in range(devices):
                lap = 2 * (i % 2) + (turn ^ (q % 2))
                pairs.append((q * devices + i, (i // 2) * devices + per_lap * lap + q // halves))
        block = jnp.concatenate([mine[turn], other[turn]], 0)
        received.append(lax.ppermute(block, ("ptg", *IMG), pairs))
    lap = me // per_lap
    out = jnp.where(
        lap % 2 == 1,
        jnp.concatenate([received[1], received[0]], 1),
        jnp.concatenate([received[0], received[1]], 1),
    ).astype(F32)
    flipped = jnp.concatenate([out[rows:], out[:rows]], 0)
    return jnp.where(lap >= 2, flipped, out)


def solution(mesh):
    pointings, devices = mesh.devices.shape
    split = Mesh(mesh.devices.reshape(pointings, 4, devices // 4), ("ptg", *IMG))
    return jax.shard_map(
        shards,
        mesh=split,
        in_specs=(P(None, IMG), P("ptg", IMG, None), P("ptg", None, IMG), P("ptg")),
        out_specs=P("ptg", IMG),
        check_vma=False,
    )
```

```python
import functools

import numpy as np

import jax
import jax.numpy as jnp
from jax import lax
from jax.experimental import pallas as pl
from jax.experimental.pallas import tpu as pltpu
from jax.sharding import Mesh, PartitionSpec as P

F32, BF16 = jnp.float32, jnp.bfloat16
NT = (((1,), (1,)), ((), ()))
NN = (((1,), (0,)), ((), ()))
VMEM = pl.BlockSpec(memory_space=pltpu.VMEM)
HBM = pl.BlockSpec(memory_space=pltpu.HBM)
SMEM = pl.BlockSpec(memory_space=pltpu.SMEM)


def dot(a, b, dims=NN):
    return lax.dot_general(a, b, dims, preferred_element_type=F32)


def row_tables(points, devices):
    half, lanes = points // 2, points // devices
    index = np.arange(half)
    turn = 2.0 * np.pi / points * np.arange(points)
    cos_of, sin_of = np.cos(turn), -np.sin(turn)
    made = []
    for odd in (0, 1):
        blocks = np.arange(devices // 2)
        if odd:
            blocks = blocks[::-1]
        freq = lanes * blocks[:, None] + 2 * np.arange(lanes // 2)[None, :] + odd
        phase = index[:, None, None] * freq[None] % points
        imag = sin_of[phase]
        if not odd:
            imag[:, 0, 0] = cos_of[index * half % points]
        made.append(np.concatenate([cos_of[phase], imag], axis=2).reshape(half, half))
    return np.stack(made)


def column_tables(points):
    half = points // 2
    index = np.arange(half)
    turn = 2.0 * np.pi / points * np.arange(points)
    cos_of, sin_of = np.cos(turn), -np.sin(turn)
    even = index[:, None] * (2 * index[None, :]) % points
    odd = index[:, None] * (2 * index[None, :] + 1) % points
    return [
        cos_of[even].T,
        sin_of[even].T,
        cos_of[odd].T,
        sin_of[odd].T,
        cos_of[odd],
        sin_of[odd],
    ]


def bf16(table):
    return jnp.asarray(np.asarray(table, np.float32).astype(jnp.bfloat16))


def ones_where(condition):
    return jnp.where(condition, 1.0, 0.0).astype(BF16)


def grid(rows, lanes):
    index = lambda axis: lax.broadcasted_iota(jnp.int32, (rows, lanes), axis)
    return index(0), index(1)


def choose_kernel(me_ref, counts_ref, own_ref, send_ref, edge_ref):
    points = counts_ref.shape[0]
    source, target = grid(128, 256)
    k, sent = target % 64, target // 128
    choice = ones_where(source == jnp.where(me_ref[0] < 8, 2 * k, 127 - 2 * k) + sent)
    unit_row, unit_lane = grid(16, 128)
    first = ones_where((unit_row == 0) & (unit_lane == 0))
    lane = lax.broadcasted_iota(jnp.int32, (256, 128), 1)
    for b in range(points // 512):
        low = counts_ref[pl.ds(256 * b, 256)].astype(F32).astype(BF16)
        high = counts_ref[pl.ds(256 * b + points // 2, 256)].astype(F32).astype(BF16)
        got_low, got_high = dot(low, choice), dot(high, choice)
        own_ref[pl.ds(256 * b, 256)] = got_low[:, :128].astype(BF16)
        own_ref[pl.ds(256 * b + points // 2, 256)] = got_high[:, :128].astype(BF16)
        send_ref[pl.ds(256 * b, 256)] = jnp.where(
            lane < 64, got_low[:, 128:], got_high[:, 128:]
        ).astype(BF16)
    edges = []
    for b in range(points // 128):
        block = counts_ref[pl.ds(128 * b, 128)].astype(F32).astype(BF16)
        edges.append(dot(first, block, NT)[:1])
    edge_ref[...] = jnp.concatenate(edges, 0).astype(BF16)


def weight_kernel(me_ref, own_ref, got_ref, edge_ref, out_ref, plus, minus):
    points = own_ref.shape[0]
    target, source = grid(256, 256)
    k, odd = target % 128, target // 128
    direct = ones_where(source == 2 * k + odd)
    negated = ones_where(source == 256 - 2 * k - odd)
    row, column = grid(128, 128)
    eye = ones_where(row == column)
    me = me_ref[0]
    low, zero = me < 8, me == 0
    edge = dot(eye, edge_ref[...], NT)
    lane = lax.broadcasted_iota(jnp.int32, (128, 128), 1)
    for b in range(points // 128):
        rows = pl.ds(128 * b, 128)
        own = own_ref[rows].astype(F32)
        packed = got_ref[pl.ds(128 * b % (points // 2), 128)].astype(F32)
        moved = pltpu.roll(packed, 64, 1)
        in_left = 128 * b < points // 2
        got = jnp.where((lane < 64) == in_left, packed, moved)
        column = jnp.broadcast_to(edge[:, b : b + 1], (128, 128))
        straight = jnp.where(low, own, got)
        mirrored = jnp.where(low, got, own)
        first = jnp.where(zero, jnp.where(lane == 0, own, column), column)
        mirrored = jnp.where(low & (lane % 64 == 0), first, mirrored)
        straight = jnp.where(zero & (lane == 64), column, straight)
        plus[rows] = straight.astype(BF16)
        minus[rows] = mirrored
    blocks = points // 256
    row = lax.broadcasted_iota(jnp.int32, (256, 128), 0)
    wide = lax.broadcasted_iota(jnp.int32, (256, 128), 1)
    scale = jnp.where(zero & (wide % 64 == 0), 0.5, 1.0)
    for b in range(blocks):
        taken = dot(direct, plus[pl.ds(256 * b, 256)])
        taken += dot(negated, minus[pl.ds(256 * (blocks - 1 - b), 256)].astype(BF16))
        wrapped = minus[pl.ds(256 * ((blocks - b) % blocks), 1)]
        taken = scale * (taken + jnp.where(row == 0, wrapped, 0.0))
        out_ref[pl.ds(128 * b, 128)] = taken[:128].astype(BF16)
        out_ref[pl.ds(points // 2 + 128 * b, 128)] = taken[128:].astype(BF16)


class Stream:
    def __init__(self, pieces, sems, ahead=6):
        self.copies = [
            pltpu.make_async_copy(source, target, sems.at[n])
            for n, (source, target) in enumerate(pieces)
        ]
        self.ahead, self.taken = ahead, 0
        for copy in self.copies[:ahead]:
            copy.start()

    def take(self):
        self.copies[self.taken].wait()
        if self.taken + self.ahead < len(self.copies):
            self.copies[self.taken + self.ahead].start()
        self.taken += 1


def pick_kernel(points, place_ref, starts_ref, tiles_ref, out_ref):
    laps, parts, rows, wide = tiles_ref.shape
    lane = lax.broadcasted_iota(jnp.int32, (rows, wide), 1) + place_ref[0] * wide
    for part in range(parts):
        held = [tiles_ref[lap, part].astype(F32) for lap in range(laps)]
        for p in range(out_ref.shape[0]):
            start = starts_ref[p]
            window = jnp.zeros((rows, wide), F32)
            for lap in range(laps):
                column = lane + lap * points
                inside = (column >= start) & (column < start + points)
                window = jnp.where(inside, held[lap], window)
            out_ref[p, part] = window.astype(BF16)


def row_kernel(window_ref, beam_ref, source_ref, out_ref, table_ref, sems):
    shares, parts, rows, wide = window_ref.shape
    blocks = out_ref.shape[0] // 2
    stream = Stream([(source_ref.at[n], table_ref.at[n]) for n in range(blocks)], sems)
    beamed = []
    for part in range(parts):
        window = jnp.concatenate([window_ref[q, part] for q in range(shares)], 0)
        beamed.append(window.astype(F32) * beam_ref[:, pl.ds(part * wide, wide)])
    left = jnp.concatenate(beamed[: parts // 2], 1)
    right = jnp.concatenate(beamed[parts // 2 :], 1)
    for odd in (0, 1):
        folded = (left - right if odd else left + right).astype(BF16)
        for part in range(blocks // 2):
            stream.take()
            spectrum = dot(folded, table_ref[odd * blocks // 2 + part]).astype(BF16)
            out_ref[odd * blocks + 2 * part] = spectrum[:, :128]
            out_ref[odd * blocks + 2 * part + 1] = spectrum[:, 128:]


def column_kernel(me_ref, x_ref, weight_ref, source_ref, out_ref, upper, lower, table_ref, sems):
    c0, s0, c1, s1, c1t, s1t = (table_ref.at[t] for t in range(6))
    points = x_ref.shape[0]
    half = points // 2
    places = [
        (t, pl.ds(256 * m, 256))
        for pair in (0, 2, 4)
        for m in range(half // 256)
        for t in (pair, pair + 1)
    ]
    stream = Stream(
        [(source_ref.at[t, rows], table_ref.at[t, rows]) for t, rows in places], sems
    )
    scale = 1.0 / float(points * points)
    lane = lax.broadcasted_iota(jnp.int32, (256, 128), 1)
    sign = jnp.where(lane < 64, -1.0, 1.0)
    packed = (me_ref[0] == 0) & (lane % 64 == 0)
    first, second = x_ref[:half].astype(F32), x_ref[half:].astype(F32)
    for odd in (0, 1):
        folded = (first - second if odd else first + second).astype(BF16)
        for m in range(half // 256):
            rows = pl.ds(256 * m, 256)
            stream.take()
            stream.take()
            by_cos = dot((c1 if odd else c0)[rows, :], folded)
            by_sin = dot((s1 if odd else s0)[rows, :], folded)
            weight = weight_ref[pl.ds(odd * half + 256 * m, 256)].astype(F32) * scale
            up = weight * (by_cos + jnp.where(packed, 0.0, sign * pltpu.roll(by_sin, 64, 1)))
            down = jnp.where(packed, weight * by_sin, -sign * pltpu.roll(up, 64, 1))
            upper[odd, rows] = up.astype(BF16)
            lower[odd, rows] = down.astype(BF16)
    for m in range(half // 256):
        rows = pl.ds(256 * m, 256)
        stream.take()
        stream.take()
        even = dot(c0[rows, :], upper[0]) + dot(s0[rows, :], lower[0])
        odd = dot(c1t[rows, :], upper[1]) + dot(s1t[rows, :], lower[1])
        out_ref[rows] = (even + odd).astype(BF16)
        out_ref[pl.ds(half + 256 * m, 256)] = (even - odd).astype(BF16)


def pixel_kernel(x_ref, beam_ref, table_ref, out_ref):
    blocks, rows, _ = x_ref.shape
    half = beam_ref.shape[1] // 2
    share = out_ref.shape[2]
    even = jnp.concatenate([x_ref[b] for b in range(blocks // 2)], 1)
    odd = jnp.concatenate([x_ref[b] for b in range(blocks // 2, blocks)], 1)
    for part in range(half // share):
        lanes = pl.ds(share * part, share)
        by_even = dot(even, table_ref[0, lanes, :], NT)
        by_odd = dot(odd, table_ref[1, lanes, :], NT)
        out_ref[part] = (beam_ref[:, lanes] * (by_even + by_odd)).astype(BF16)
        late = pl.ds(half + share * part, share)
        out_ref[part + half // share] = (beam_ref[:, late] * (by_even - by_odd)).astype(BF16)


def sum_kernel(points, me_ref, starts_ref, terms_ref, mine_ref, theirs_ref):
    pointings, rows, share = terms_ref.shape
    ptg, core = me_ref[0], me_ref[1]
    lane = lax.broadcasted_iota(jnp.int32, (rows, share), 1)
    for ref, side in ((mine_ref, core), (theirs_ref, 1 - core)):
        for turn in range(2):
            lap = 2 * side + jnp.where(ptg % 2 == turn, 0, 1)
            column = lane + (lap * points + ptg * share)
            total = jnp.zeros((rows, share), F32)
            for p in range(pointings):
                inside = (column >= starts_ref[p]) & (column < starts_ref[p] + points)
                total += jnp.where(inside, terms_ref[p].astype(F32), 0.0)
            ref[turn] = total.astype(BF16)


def call(kernel, outs, specs, *args, scratch=(), flops=0, moved=4 << 20, limit=16):
    return pl.pallas_call(
        kernel,
        out_shape=outs,
        in_specs=specs,
        out_specs=jax.tree.map(lambda _: VMEM, outs),
        scratch_shapes=list(scratch),
        compiler_params=pltpu.CompilerParams(vmem_limit_bytes=limit << 20),
        cost_estimate=pl.CostEstimate(flops=flops, bytes_accessed=moved, transcendentals=0),
    )(*args)


def shape(*dims, dtype=BF16):
    return jax.ShapeDtypeStruct(dims, dtype)


IMG = ("s", "b")


def shards(image, beam, counts, offsets):
    points = counts.shape[1]
    laps, parts = lax.axis_size("s"), lax.axis_size("b")
    devices = laps * parts
    pointings = lax.axis_size("ptg")
    rows = points // devices
    tile = image.shape[1]
    me = lax.axis_index(IMG).astype(jnp.int32)
    ptg = lax.axis_index("ptg").astype(jnp.int32)
    start = offsets[0]
    place = me.reshape(1)

    starts = jnp.where(jnp.arange(pointings) == ptg, start, 0)
    share_rows = rows // pointings
    shares = image.reshape(laps, parts, pointings, share_rows, tile)
    shares = lax.dynamic_index_in_dim(shares, ptg, 2, keepdims=False)
    own, send, edge = call(
        choose_kernel,
        (shape(points, 128), shape(points // 2, 128), shape(points // 128, 128)),
        [SMEM, VMEM],
        place,
        counts[0],
        flops=points * 128 * 512,
    )
    shares, send, edge, starts = lax.optimization_barrier((shares, send, edge, starts))
    shares = lax.all_to_all(shares, "s", split_axis=0, concat_axis=0, tiled=True)
    near = [
        lax.ppermute(starts, "ptg", [(p, p ^ bit) for p in range(pointings)]) for bit in (1, 2, 3)
    ]
    starts = starts + near[0] + near[1] + near[2]
    starts = starts + lax.ppermute(starts, "ptg", [(p, p ^ 4) for p in range(pointings)])
    got = lax.ppermute(send, IMG, [(i, devices - 1 - i) for i in range(devices)])
    edge = lax.ppermute(
        edge,
        IMG,
        [(i, (devices - i) % (devices // 2)) for i in range(devices // 2, devices)],
    )
    weight = call(
        weight_kernel,
        shape(points, 128),
        [SMEM] + [VMEM] * 3,
        place,
        own,
        got,
        edge,
        scratch=[pltpu.VMEM((points, 128), BF16), pltpu.VMEM((points, 128), F32)],
        flops=points * 128 * 1024,
    )

    twice = jnp.concatenate([beam[0], beam[0]], 1)
    turned = lax.dynamic_slice_in_dim(twice, (points - start % points) % points, points, 1)
    picked = call(
        functools.partial(pick_kernel, points),
        shape(pointings, parts, share_rows, tile),
        [SMEM, SMEM, VMEM],
        lax.axis_index("b").astype(jnp.int32).reshape(1),
        starts,
        shares,
        moved=1 << 20,
    )
    window = lax.all_to_all(
        picked.reshape(pointings * parts, share_rows, tile),
        ("ptg", "b"),
        split_axis=0,
        concat_axis=0,
        tiled=True,
    ).reshape(pointings, parts, share_rows, tile)
    window, weight, turned = lax.optimization_barrier((window, weight, turned))
    row_table = row_tables(points, devices)
    pieces = row_table.reshape(2, points // 2, -1, 256).transpose(0, 2, 1, 3)
    pieces = bf16(pieces.reshape(-1, points // 2, 256))
    spectrum = call(
        row_kernel,
        shape(devices, rows, 128),
        [VMEM, VMEM, HBM],
        window,
        turned,
        pieces,
        scratch=[pltpu.VMEM(pieces.shape, BF16), pltpu.SemaphoreType.DMA((pieces.shape[0],))],
        flops=rows * points * points,
        limit=60,
    )
    col = lax.all_to_all(spectrum, IMG, split_axis=0, concat_axis=0, tiled=True)
    back = call(
        column_kernel,
        shape(points, 128),
        [SMEM, VMEM, VMEM, HBM],
        place,
        col.reshape(points, 128),
        weight,
        bf16(np.stack(column_tables(points))),
        scratch=[pltpu.VMEM((2, points // 2, 128), BF16)] * 2
        + [pltpu.VMEM((6, points // 2, points // 2), BF16), pltpu.SemaphoreType.DMA((24,))],
        flops=8 * points * points * 128 // 2,
        moved=16 << 20,
        limit=60,
    )
    lines = lax.all_to_all(
        back.reshape(devices, rows, 128), IMG, split_axis=0, concat_axis=0, tiled=True
    )
    share = points // pointings
    contribution = call(
        pixel_kernel,
        shape(pointings, rows, share),
        [VMEM] * 3,
        lines,
        turned,
        bf16(row_table),
        flops=rows * points * points,
    )
    terms = lax.all_to_all(contribution, "ptg", split_axis=0, concat_axis=0, tiled=True)
    mine, theirs = call(
        functools.partial(sum_kernel, points),
        (shape(2, rows, share), shape(2, rows, share)),
        [SMEM, SMEM, VMEM],
        jnp.stack([ptg, me % 2]),
        starts,
        terms,
        moved=1 << 20,
    )
    other = lax.ppermute(theirs, IMG, [(i, i ^ 1) for i in range(devices)])
    per_lap = parts
    halves = tile // share
    received = []
    for turn in range(2):
        pairs = []
        for q in range(pointings):
            for i in range(devices):
                lap = 2 * (i % 2) + (turn ^ (q % 2))
                pairs.append((q * devices + i, (i // 2) * devices + per_lap * lap + q // halves))
        block = jnp.concatenate([mine[turn], other[turn]], 0)
        received.append(lax.ppermute(block, ("ptg", *IMG), pairs))
    lap = me // per_lap
    out = jnp.where(
        lap % 2 == 1,
        jnp.concatenate([received[1], received[0]], 1),
        jnp.concatenate([received[0], received[1]], 1),
    ).astype(F32)
    flipped = jnp.concatenate([out[rows:], out[:rows]], 0)
    return jnp.where(lap >= 2, flipped, out)


def solution(mesh):
    pointings, devices = mesh.devices.shape
    split = Mesh(mesh.devices.reshape(pointings, 4, devices // 4), ("ptg", *IMG))
    return jax.shard_map(
        shards,
        mesh=split,
        in_specs=(P(None, IMG), P("ptg", IMG, None), P("ptg", None, IMG), P("ptg")),
        out_specs=P("ptg", IMG),
        check_vma=False,
    )
```

```python
import functools

import numpy as np

import jax
import jax.numpy as jnp
from jax import lax
from jax.experimental import pallas as pl
from jax.experimental.pallas import tpu as pltpu
from jax.sharding import Mesh, PartitionSpec as P

F32, BF16 = jnp.float32, jnp.bfloat16
NT = (((1,), (1,)), ((), ()))
NN = (((1,), (0,)), ((), ()))
VMEM = pl.BlockSpec(memory_space=pltpu.VMEM)
SMEM = pl.BlockSpec(memory_space=pltpu.SMEM)


def dot(a, b, dims=NN):
    return lax.dot_general(a, b, dims, preferred_element_type=F32)


def row_table(points, devices):
    half, lanes = points // 2, points // devices
    index = np.arange(half)
    turn = 2.0 * np.pi / points * np.arange(points)
    cos_of, sin_of = np.cos(turn), -np.sin(turn)
    freq = lanes * np.arange(devices // 2)[:, None] + 2 * np.arange(lanes // 2)[None, :]
    phase = index[:, None, None] * freq[None] % points
    imag = sin_of[phase]
    imag[:, 0, 0] = cos_of[index * half % points]
    return np.concatenate([cos_of[phase], imag], axis=2).reshape(half, half)


def row_turn(points):
    angle = 2.0 * np.pi / points * np.arange(points // 2)
    return np.stack([np.cos(angle), np.sin(angle)] * 4).astype(np.float32)


def column_table(points):
    quarter = points // 4
    index = np.arange(quarter)
    angle = 2.0 * np.pi / quarter * (index[:, None] * index[None, :] % quarter)
    return np.concatenate([np.cos(angle), -np.sin(angle)])


def column_turn(points):
    angle = 2.0 * np.pi / points * np.arange(points // 4)[:, None] * np.arange(4)[None, :]
    made = np.zeros((points // 4, 128), np.float32)
    made[:, :4], made[:, 4:8] = np.cos(angle), np.sin(angle)
    return made


def bf16(table):
    return jnp.asarray(np.asarray(table, np.float32).astype(jnp.bfloat16))


def ones_where(condition):
    return jnp.where(condition, 1.0, 0.0).astype(BF16)


def grid(rows, lanes):
    index = lambda axis: lax.broadcasted_iota(jnp.int32, (rows, lanes), axis)
    return index(0), index(1)


def choose_kernel(me_ref, counts_ref, own_ref, send_ref, edge_ref):
    points = counts_ref.shape[0]
    source, target = grid(128, 256)
    k, sent = target % 64, target // 128
    choice = ones_where(source == jnp.where(me_ref[0] < 8, 2 * k, 127 - 2 * k) + sent)
    unit_row, unit_lane = grid(16, 128)
    first = ones_where((unit_row == 0) & (unit_lane == 0))
    lane = lax.broadcasted_iota(jnp.int32, (256, 128), 1)
    for b in range(points // 512):
        low = counts_ref[pl.ds(256 * b, 256)].astype(F32).astype(BF16)
        high = counts_ref[pl.ds(256 * b + points // 2, 256)].astype(F32).astype(BF16)
        got_low, got_high = dot(low, choice), dot(high, choice)
        own_ref[pl.ds(256 * b, 256)] = got_low[:, :128].astype(BF16)
        own_ref[pl.ds(256 * b + points // 2, 256)] = got_high[:, :128].astype(BF16)
        send_ref[pl.ds(256 * b, 256)] = jnp.where(
            lane < 64, got_low[:, 128:], got_high[:, 128:]
        ).astype(BF16)
    edges = []
    for b in range(points // 128):
        block = counts_ref[pl.ds(128 * b, 128)].astype(F32).astype(BF16)
        edges.append(dot(first, block, NT)[:1])
    edge_ref[...] = jnp.concatenate(edges, 0).astype(BF16)


def weight_kernel(me_ref, own_ref, got_ref, edge_ref, out_ref, plus, minus):
    points = own_ref.shape[0]
    target, source = grid(256, 256)
    index = 4 * (target % 64) + target // 64
    direct = ones_where(source == index)
    negated = ones_where(source == 256 - index)
    row, column = grid(128, 128)
    eye = ones_where(row == column)
    me = me_ref[0]
    low, zero = me < 8, me == 0
    edge = dot(eye, edge_ref[...], NT)
    lane = lax.broadcasted_iota(jnp.int32, (128, 128), 1)
    for b in range(points // 128):
        rows = pl.ds(128 * b, 128)
        own = own_ref[rows].astype(F32)
        packed = got_ref[pl.ds(128 * b % (points // 2), 128)].astype(F32)
        moved = pltpu.roll(packed, 64, 1)
        in_left = 128 * b < points // 2
        got = jnp.where((lane < 64) == in_left, packed, moved)
        column = jnp.broadcast_to(edge[:, b : b + 1], (128, 128))
        straight = jnp.where(low, own, got)
        mirrored = jnp.where(low, got, own)
        first = jnp.where(zero, jnp.where(lane == 0, own, column), column)
        mirrored = jnp.where(low & (lane % 64 == 0), first, mirrored)
        straight = jnp.where(zero & (lane == 64), column, straight)
        plus[rows] = straight.astype(BF16)
        minus[rows] = mirrored
    blocks = points // 256
    row = lax.broadcasted_iota(jnp.int32, (256, 128), 0)
    wide = lax.broadcasted_iota(jnp.int32, (256, 128), 1)
    scale = jnp.where(zero & (wide % 64 == 0), 0.5, 1.0)
    for b in range(blocks):
        taken = dot(direct, plus[pl.ds(256 * b, 256)])
        taken += dot(negated, minus[pl.ds(256 * (blocks - 1 - b), 256)].astype(BF16))
        wrapped = minus[pl.ds(256 * ((blocks - b) % blocks), 1)]
        taken = scale * (taken + jnp.where(row == 0, wrapped, 0.0))
        for r in range(4):
            out_ref[pl.ds(r * points // 4 + 64 * b, 64)] = taken[64 * r : 64 * r + 64].astype(BF16)


def pick_kernel(points, place_ref, starts_ref, tiles_ref, out_ref):
    laps, parts, rows, wide = tiles_ref.shape
    lane = lax.broadcasted_iota(jnp.int32, (rows, wide), 1) + place_ref[0] * wide
    for part in range(parts):
        held = [tiles_ref[lap, part].astype(F32) for lap in range(laps)]
        for p in range(out_ref.shape[0]):
            start = starts_ref[p]
            window = jnp.zeros((rows, wide), F32)
            for lap in range(laps):
                column = lane + lap * points
                inside = (column >= start) & (column < start + points)
                window = jnp.where(inside, held[lap], window)
            out_ref[p, part] = window.astype(BF16)


def row_kernel(window_ref, beam_ref, table_ref, turn_ref, out_ref):
    shares, parts, _, wide = window_ref.shape
    rows = out_ref.shape[1]
    beamed = []
    for part in range(parts):
        window = jnp.concatenate([window_ref[q, part] for q in range(shares)], 0)
        beamed.append(window.astype(F32) * beam_ref[:, pl.ds(part * wide, wide)])
    left = jnp.concatenate(beamed[: parts // 2], 1)
    right = jnp.concatenate(beamed[parts // 2 :], 1)
    minus = left - right
    folded = [left + right, minus * turn_ref[0:1], minus * turn_ref[1:2]]
    folded = jnp.concatenate([t.astype(BF16) for t in folded], 0)
    last = out_ref.shape[0] - 1
    lane = lax.broadcasted_iota(jnp.int32, (rows, 128), 1)
    for part in range(table_ref.shape[1] // 256):
        got = dot(folded, table_ref[:, pl.ds(256 * part, 256)])
        for n in (0, 1):
            block = 2 * part + n
            even, by_cos, by_sin = (
                got[rows * t : rows * (t + 1), 128 * n : 128 * (n + 1)] for t in range(3)
            )
            if block == 0:
                by_cos = jnp.where(lane == 64, 0.0, by_cos)
                by_sin = jnp.where(lane == 64, 0.0, by_sin)
            moved = pltpu.roll(by_sin, 64, 1)
            out_ref[block] = even.astype(BF16)
            out_ref[last - block] = jnp.where(lane < 64, by_cos + moved, by_cos - moved).astype(BF16)


def column_kernel(me_ref, x_ref, weight_ref, table_ref, turn_ref, out_ref, both):
    points = x_ref.shape[0]
    quarter = points // 4
    scale = 1.0 / float(points * points)
    lane = lax.broadcasted_iota(jnp.int32, (256, 128), 1)
    sign = jnp.where(lane < 64, -1.0, 1.0)
    packed = (me_ref[0] == 0) & (lane % 64 == 0)
    turns = lambda r, rows: (
        jnp.broadcast_to(turn_ref[rows, r : r + 1], (256, 128)),
        jnp.broadcast_to(turn_ref[rows, 4 + r : 5 + r], (256, 128)),
    )
    for m in range(quarter // 256):
        rows = pl.ds(256 * m, 256)
        x = [x_ref[pl.ds(quarter * t + 256 * m, 256)].astype(F32) for t in range(4)]
        even, p, odd, q = x[0] + x[2], x[0] - x[2], x[1] + x[3], x[1] - x[3]
        c1, s1 = turns(1, rows)
        c2, s2 = turns(2, rows)
        c3, s3 = turns(3, rows)
        pairs = [
            (even + odd, jnp.zeros_like(even)),
            (p * c1 - q * s1, -(p * s1 + q * c1)),
            ((even - odd) * c2, -(even - odd) * s2),
            (p * c3 + q * s3, q * c3 - p * s3),
        ]
        for r in range(4):
            both[4 + r, rows, 0:128] = pairs[r][0].astype(BF16)
            both[4 + r, rows, 128:256] = pairs[r][1].astype(BF16)
    for r in range(4):
        for m in range(quarter // 256):
            rows, below = pl.ds(256 * m, 256), pl.ds(quarter + 256 * m, 256)
            wide = both[4 + r] if r else both[4, :, 0:128]
            by_c, by_s = dot(table_ref[rows], wide), dot(table_ref[below], wide)
            by_cos, by_sin = by_c[:, :128], by_s[:, :128]
            if r:
                by_cos, by_sin = by_cos - by_s[:, 128:], by_sin + by_c[:, 128:]
            weight = weight_ref[pl.ds(r * quarter + 256 * m, 256)].astype(F32) * scale
            up = weight * (by_cos + jnp.where(packed, 0.0, sign * pltpu.roll(by_sin, 64, 1)))
            down = jnp.where(packed, weight * by_sin, -sign * pltpu.roll(up, 64, 1))
            both[r, rows, 0:128] = up.astype(BF16)
            both[r, rows, 128:256] = down.astype(BF16)
    for m in range(quarter // 256):
        rows, below = pl.ds(256 * m, 256), pl.ds(quarter + 256 * m, 256)
        parts = []
        for r in range(4):
            by_c, by_s = dot(table_ref[rows], both[r]), dot(table_ref[below], both[r])
            parts.append((by_c[:, :128] + by_s[:, 128:], by_c[:, 128:] - by_s[:, :128]))
        c1, s1 = turns(1, rows)
        c2, s2 = turns(2, rows)
        c3, s3 = turns(3, rows)
        (g0, _), (g1, h1), (g2, h2), (g3, h3) = parts
        middle = c2 * g2 - s2 * h2
        p = c1 * g1 - s1 * h1 + c3 * g3 - s3 * h3
        q = s3 * g3 + c3 * h3 - s1 * g1 - c1 * h1
        plus, minus = g0 + middle, g0 - middle
        for t, value in enumerate((plus + p, minus + q, plus - p, minus - q)):
            out_ref[pl.ds(quarter * t + 256 * m, 256)] = value.astype(BF16)


def pixel_kernel(x_ref, beam_ref, table_ref, turn_ref, out_ref):
    blocks, rows, _ = x_ref.shape
    half = beam_ref.shape[1] // 2
    share = out_ref.shape[2]
    lane = lax.broadcasted_iota(jnp.int32, (rows, 128), 1)
    even = [x_ref[b] for b in range(blocks // 2)]
    straight, crossed = [], []
    for b in range(blocks // 2):
        odd = x_ref[blocks - 1 - b].astype(F32)
        moved = pltpu.roll(odd, 64, 1)
        turned = jnp.where(lane < 64, -moved, moved)
        if b == 0:
            odd = jnp.where(lane == 64, 0.0, odd)
            turned = jnp.where(lane == 64, 0.0, turned)
        straight.append(odd.astype(BF16))
        crossed.append(turned.astype(BF16))
    wide = [jnp.concatenate(part, 1) for part in (even, straight, crossed)]
    wide = jnp.concatenate(wide, 0)
    for part in range(half // share):
        lanes = pl.ds(share * part, share)
        got = dot(wide, table_ref[lanes, :], NT)
        by_even = got[:rows]
        by_odd = turn_ref[0:1, lanes] * got[rows : 2 * rows] + turn_ref[1:2, lanes] * got[2 * rows :]
        out_ref[part] = (beam_ref[:, lanes] * (by_even + by_odd)).astype(BF16)
        late = pl.ds(half + share * part, share)
        out_ref[part + half // share] = (beam_ref[:, late] * (by_even - by_odd)).astype(BF16)


def sum_kernel(points, me_ref, starts_ref, terms_ref, mine_ref, theirs_ref):
    pointings, rows, share = terms_ref.shape
    ptg, core = me_ref[0], me_ref[1]
    lane = lax.broadcasted_iota(jnp.int32, (rows, share), 1)
    for ref, side in ((mine_ref, core), (theirs_ref, 1 - core)):
        for turn in range(2):
            lap = 2 * side + jnp.where(ptg % 2 == turn, 0, 1)
            column = lane + (lap * points + ptg * share)
            total = jnp.zeros((rows, share), F32)
            for p in range(pointings):
                inside = (column >= starts_ref[p]) & (column < starts_ref[p] + points)
                total += jnp.where(inside, terms_ref[p].astype(F32), 0.0)
            ref[turn] = total.astype(BF16)


def call(kernel, outs, specs, *args, scratch=(), flops=0, moved=4 << 20, limit=16):
    return pl.pallas_call(
        kernel,
        out_shape=outs,
        in_specs=specs,
        out_specs=jax.tree.map(lambda _: VMEM, outs),
        scratch_shapes=list(scratch),
        compiler_params=pltpu.CompilerParams(vmem_limit_bytes=limit << 20),
        cost_estimate=pl.CostEstimate(flops=flops, bytes_accessed=moved, transcendentals=0),
    )(*args)


def shape(*dims, dtype=BF16):
    return jax.ShapeDtypeStruct(dims, dtype)


IMG = ("s", "b")


def shards(image, beam, counts, offsets):
    points = counts.shape[1]
    laps, parts = lax.axis_size("s"), lax.axis_size("b")
    devices = laps * parts
    pointings = lax.axis_size("ptg")
    rows = points // devices
    tile = image.shape[1]
    me = lax.axis_index(IMG).astype(jnp.int32)
    ptg = lax.axis_index("ptg").astype(jnp.int32)
    start = offsets[0]
    place = me.reshape(1)

    starts = jnp.where(jnp.arange(pointings) == ptg, start, 0)
    share_rows = rows // pointings
    shares = image.reshape(laps, parts, pointings, share_rows, tile)
    shares = lax.dynamic_index_in_dim(shares, ptg, 2, keepdims=False)
    own, send, edge = call(
        choose_kernel,
        (shape(points, 128), shape(points // 2, 128), shape(points // 128, 128)),
        [SMEM, VMEM],
        place,
        counts[0],
        flops=points * 128 * 512,
    )
    shares, send, edge, starts = lax.optimization_barrier((shares, send, edge, starts))
    shares = lax.all_to_all(shares, "s", split_axis=0, concat_axis=0, tiled=True)
    near = [
        lax.ppermute(starts, "ptg", [(p, p ^ bit) for p in range(pointings)]) for bit in (1, 2, 3)
    ]
    starts = starts + near[0] + near[1] + near[2]
    starts = starts + lax.ppermute(starts, "ptg", [(p, p ^ 4) for p in range(pointings)])
    got = lax.ppermute(send, IMG, [(i, devices - 1 - i) for i in range(devices)])
    edge = lax.ppermute(
        edge,
        IMG,
        [(i, (devices - i) % (devices // 2)) for i in range(devices // 2, devices)],
    )
    weight = call(
        weight_kernel,
        shape(points, 128),
        [SMEM] + [VMEM] * 3,
        place,
        own,
        got,
        edge,
        scratch=[pltpu.VMEM((points, 128), BF16), pltpu.VMEM((points, 128), F32)],
        flops=points * 128 * 1024,
    )

    twice = jnp.concatenate([beam[0], beam[0]], 1)
    turned = lax.dynamic_slice_in_dim(twice, (points - start % points) % points, points, 1)
    shares, got, edge = lax.optimization_barrier((shares, got, edge))
    picked = call(
        functools.partial(pick_kernel, points),
        shape(pointings, parts, share_rows, tile),
        [SMEM, SMEM, VMEM],
        lax.axis_index("b").astype(jnp.int32).reshape(1),
        starts,
        shares,
        moved=1 << 20,
    )
    window = lax.all_to_all(
        picked.reshape(pointings * parts, share_rows, tile),
        ("ptg", "b"),
        split_axis=0,
        concat_axis=0,
        tiled=True,
    ).reshape(pointings, parts, share_rows, tile)
    window, weight, turned = lax.optimization_barrier((window, weight, turned))
    across, turn = bf16(row_table(points, devices)), jnp.asarray(row_turn(points))
    spectrum = call(
        row_kernel,
        shape(devices, rows, 128),
        [VMEM] * 4,
        window,
        turned,
        across,
        turn,
        flops=rows * points * points,
    )
    col = lax.all_to_all(spectrum, IMG, split_axis=0, concat_axis=0, tiled=True)
    back = call(
        column_kernel,
        shape(points, 128),
        [SMEM] + [VMEM] * 4,
        place,
        col.reshape(points, 128),
        weight,
        bf16(column_table(points)),
        jnp.asarray(column_turn(points)),
        scratch=[pltpu.VMEM((8, points // 4, 256), BF16)],
        flops=4 * points * points * 128,
    )
    lines = lax.all_to_all(
        back.reshape(devices, rows, 128), IMG, split_axis=0, concat_axis=0, tiled=True
    )
    share = points // pointings
    contribution = call(
        pixel_kernel,
        shape(pointings, rows, share),
        [VMEM] * 4,
        lines,
        turned,
        across,
        turn,
        flops=rows * points * points,
    )
    terms = lax.all_to_all(contribution, "ptg", split_axis=0, concat_axis=0, tiled=True)
    mine, theirs = call(
        functools.partial(sum_kernel, points),
        (shape(2, rows, share), shape(2, rows, share)),
        [SMEM, SMEM, VMEM],
        jnp.stack([ptg, me % 2]),
        starts,
        terms,
        moved=1 << 20,
    )
    other = lax.ppermute(theirs, IMG, [(i, i ^ 1) for i in range(devices)])
    per_lap = parts
    halves = tile // share
    received = []
    for turn in range(2):
        pairs = []
        for q in range(pointings):
            for i in range(devices):
                lap = 2 * (i % 2) + (turn ^ (q % 2))
                pairs.append((q * devices + i, (i // 2) * devices + per_lap * lap + q // halves))
        block = jnp.concatenate([mine[turn], other[turn]], 0)
        received.append(lax.ppermute(block, ("ptg", *IMG), pairs))
    lap = me // per_lap
    out = jnp.where(
        lap % 2 == 1,
        jnp.concatenate([received[1], received[0]], 1),
        jnp.concatenate([received[0], received[1]], 1),
    ).astype(F32)
    flipped = jnp.concatenate([out[rows:], out[:rows]], 0)
    return jnp.where(lap >= 2, flipped, out)


def solution(mesh):
    pointings, devices = mesh.devices.shape
    split = Mesh(mesh.devices.reshape(pointings, 4, devices // 4), ("ptg", *IMG))
    return jax.shard_map(
        shards,
        mesh=split,
        in_specs=(P(None, IMG), P("ptg", IMG, None), P("ptg", None, IMG), P("ptg")),
        out_specs=P("ptg", IMG),
        check_vma=False,
    )
```

```python
import functools

import numpy as np

import jax
import jax.numpy as jnp
from jax import lax
from jax.experimental import pallas as pl
from jax.experimental.pallas import tpu as pltpu
from jax.sharding import Mesh, PartitionSpec as P

F32, BF16 = jnp.float32, jnp.bfloat16
NT = (((1,), (1,)), ((), ()))
NN = (((1,), (0,)), ((), ()))
VMEM = pl.BlockSpec(memory_space=pltpu.VMEM)
SMEM = pl.BlockSpec(memory_space=pltpu.SMEM)


def dot(a, b, dims=NN):
    return lax.dot_general(a, b, dims, preferred_element_type=F32)


def row_table(points, devices):
    half, lanes = points // 2, points // devices
    index = np.arange(half)
    turn = 2.0 * np.pi / points * np.arange(points)
    cos_of, sin_of = np.cos(turn), -np.sin(turn)
    freq = lanes * np.arange(devices // 2)[:, None] + 2 * np.arange(lanes // 2)[None, :]
    phase = index[:, None, None] * freq[None] % points
    imag = sin_of[phase]
    imag[:, 0, 0] = cos_of[index * half % points]
    return np.concatenate([cos_of[phase], imag], axis=2).reshape(half, half)


def row_turn(points):
    angle = 2.0 * np.pi / points * np.arange(points // 2)
    return np.stack([np.cos(angle), np.sin(angle)] * 4).astype(np.float32)


def column_table(points):
    quarter = points // 4
    index = np.arange(quarter)
    angle = 2.0 * np.pi / quarter * (index[:, None] * index[None, :] % quarter)
    return np.concatenate([np.cos(angle), -np.sin(angle)])


def column_turn(points):
    angle = 2.0 * np.pi / points * np.arange(points // 4)[:, None] * np.arange(4)[None, :]
    made = np.zeros((points // 4, 128), np.float32)
    made[:, :4], made[:, 4:8] = np.cos(angle), np.sin(angle)
    return made


def bf16(table):
    return jnp.asarray(np.asarray(table, np.float32).astype(jnp.bfloat16))


def ones_where(condition):
    return jnp.where(condition, 1.0, 0.0).astype(BF16)


def grid(rows, lanes):
    index = lambda axis: lax.broadcasted_iota(jnp.int32, (rows, lanes), axis)
    return index(0), index(1)


def choose_kernel(me_ref, counts_ref, _, own_ref, send_ref, edge_ref):
    points = counts_ref.shape[0]
    source, target = grid(128, 256)
    k, sent = target % 64, target // 128
    choice = ones_where(source == jnp.where(me_ref[0] < 8, 2 * k, 127 - 2 * k) + sent)
    unit_row, unit_lane = grid(16, 128)
    first = ones_where((unit_row == 0) & (unit_lane == 0))
    lane = lax.broadcasted_iota(jnp.int32, (256, 128), 1)
    for b in range(points // 512):
        low = counts_ref[pl.ds(256 * b, 256)].astype(F32).astype(BF16)
        high = counts_ref[pl.ds(256 * b + points // 2, 256)].astype(F32).astype(BF16)
        got_low, got_high = dot(low, choice), dot(high, choice)
        own_ref[pl.ds(256 * b, 256)] = got_low[:, :128].astype(BF16)
        own_ref[pl.ds(256 * b + points // 2, 256)] = got_high[:, :128].astype(BF16)
        send_ref[pl.ds(256 * b, 256)] = jnp.where(
            lane < 64, got_low[:, 128:], got_high[:, 128:]
        ).astype(BF16)
    edges = []
    for b in range(points // 128):
        block = counts_ref[pl.ds(128 * b, 128)].astype(F32).astype(BF16)
        edges.append(dot(first, block, NT)[:1])
    edge_ref[...] = jnp.concatenate(edges, 0).astype(BF16)


def weight_kernel(me_ref, own_ref, got_ref, edge_ref, out_ref, plus, minus):
    points = own_ref.shape[0]
    target, source = grid(256, 256)
    index = 4 * (target % 64) + target // 64
    direct = ones_where(source == index)
    negated = ones_where(source == 256 - index)
    row, column = grid(128, 128)
    eye = ones_where(row == column)
    me = me_ref[0]
    low, zero = me < 8, me == 0
    edge = dot(eye, edge_ref[...], NT)
    lane = lax.broadcasted_iota(jnp.int32, (128, 128), 1)
    for b in range(points // 128):
        rows = pl.ds(128 * b, 128)
        own = own_ref[rows].astype(F32)
        packed = got_ref[pl.ds(128 * b % (points // 2), 128)].astype(F32)
        moved = pltpu.roll(packed, 64, 1)
        in_left = 128 * b < points // 2
        got = jnp.where((lane < 64) == in_left, packed, moved)
        column = jnp.broadcast_to(edge[:, b : b + 1], (128, 128))
        straight = jnp.where(low, own, got)
        mirrored = jnp.where(low, got, own)
        first = jnp.where(zero, jnp.where(lane == 0, own, column), column)
        mirrored = jnp.where(low & (lane % 64 == 0), first, mirrored)
        straight = jnp.where(zero & (lane == 64), column, straight)
        plus[rows] = straight.astype(BF16)
        minus[rows] = mirrored
    blocks = points // 256
    row = lax.broadcasted_iota(jnp.int32, (256, 128), 0)
    wide = lax.broadcasted_iota(jnp.int32, (256, 128), 1)
    scale = jnp.where(zero & (wide % 64 == 0), 0.5, 1.0)
    for b in range(blocks):
        taken = dot(direct, plus[pl.ds(256 * b, 256)])
        taken += dot(negated, minus[pl.ds(256 * (blocks - 1 - b), 256)].astype(BF16))
        wrapped = minus[pl.ds(256 * ((blocks - b) % blocks), 1)]
        taken = scale * (taken + jnp.where(row == 0, wrapped, 0.0))
        for r in range(4):
            out_ref[pl.ds(r * points // 4 + 64 * b, 64)] = taken[64 * r : 64 * r + 64].astype(BF16)


def pick_kernel(points, place_ref, starts_ref, tiles_ref, out_ref):
    laps, parts, rows, wide = tiles_ref.shape
    lane = lax.broadcasted_iota(jnp.int32, (rows, wide), 1) + place_ref[0] * wide
    for part in range(parts):
        held = [tiles_ref[lap, part].astype(F32) for lap in range(laps)]
        for p in range(out_ref.shape[0]):
            start = starts_ref[p]
            window = jnp.zeros((rows, wide), F32)
            for lap in range(laps):
                column = lane + lap * points
                inside = (column >= start) & (column < start + points)
                window = jnp.where(inside, held[lap], window)
            out_ref[p, part] = window.astype(BF16)


def row_kernel(window_ref, beam_ref, table_ref, turn_ref, out_ref):
    shares, parts, _, wide = window_ref.shape
    rows = out_ref.shape[1]
    beamed = []
    for part in range(parts):
        window = jnp.concatenate([window_ref[q, part] for q in range(shares)], 0)
        beamed.append(window.astype(F32) * beam_ref[:, pl.ds(part * wide, wide)])
    left = jnp.concatenate(beamed[: parts // 2], 1)
    right = jnp.concatenate(beamed[parts // 2 :], 1)
    minus = left - right
    folded = [left + right, minus * turn_ref[0:1], minus * turn_ref[1:2]]
    folded = jnp.concatenate([t.astype(BF16) for t in folded], 0)
    last = out_ref.shape[0] - 1
    lane = lax.broadcasted_iota(jnp.int32, (rows, 128), 1)
    for part in range(table_ref.shape[1] // 256):
        got = dot(folded, table_ref[:, pl.ds(256 * part, 256)])
        for n in (0, 1):
            block = 2 * part + n
            even, by_cos, by_sin = (
                got[rows * t : rows * (t + 1), 128 * n : 128 * (n + 1)] for t in range(3)
            )
            if block == 0:
                by_cos = jnp.where(lane == 64, 0.0, by_cos)
                by_sin = jnp.where(lane == 64, 0.0, by_sin)
            moved = pltpu.roll(by_sin, 64, 1)
            out_ref[block] = even.astype(BF16)
            out_ref[last - block] = jnp.where(lane < 64, by_cos + moved, by_cos - moved).astype(BF16)


def column_kernel(me_ref, x_ref, weight_ref, table_ref, turn_ref, out_ref, both):
    points = x_ref.shape[0]
    quarter = points // 4
    scale = 1.0 / float(points * points)
    lane = lax.broadcasted_iota(jnp.int32, (256, 128), 1)
    sign = jnp.where(lane < 64, -1.0, 1.0)
    packed = (me_ref[0] == 0) & (lane % 64 == 0)
    turns = lambda r, rows: (
        jnp.broadcast_to(turn_ref[rows, r : r + 1], (256, 128)),
        jnp.broadcast_to(turn_ref[rows, 4 + r : 5 + r], (256, 128)),
    )
    for m in range(quarter // 256):
        rows = pl.ds(256 * m, 256)
        x = [x_ref[pl.ds(quarter * t + 256 * m, 256)].astype(F32) for t in range(4)]
        even, p, odd, q = x[0] + x[2], x[0] - x[2], x[1] + x[3], x[1] - x[3]
        c1, s1 = turns(1, rows)
        c2, s2 = turns(2, rows)
        c3, s3 = turns(3, rows)
        pairs = [
            (even + odd, jnp.zeros_like(even)),
            (p * c1 - q * s1, -(p * s1 + q * c1)),
            ((even - odd) * c2, -(even - odd) * s2),
            (p * c3 + q * s3, q * c3 - p * s3),
        ]
        for r in range(4):
            both[4 + r, rows, 0:128] = pairs[r][0].astype(BF16)
            both[4 + r, rows, 128:256] = pairs[r][1].astype(BF16)
    for r in range(4):
        for m in range(quarter // 256):
            rows, below = pl.ds(256 * m, 256), pl.ds(quarter + 256 * m, 256)
            wide = both[4 + r] if r else both[4, :, 0:128]
            by_c, by_s = dot(table_ref[rows], wide), dot(table_ref[below], wide)
            by_cos, by_sin = by_c[:, :128], by_s[:, :128]
            if r:
                by_cos, by_sin = by_cos - by_s[:, 128:], by_sin + by_c[:, 128:]
            weight = weight_ref[pl.ds(r * quarter + 256 * m, 256)].astype(F32) * scale
            up = weight * (by_cos + jnp.where(packed, 0.0, sign * pltpu.roll(by_sin, 64, 1)))
            down = jnp.where(packed, weight * by_sin, -sign * pltpu.roll(up, 64, 1))
            both[r, rows, 0:128] = up.astype(BF16)
            both[r, rows, 128:256] = down.astype(BF16)
    for m in range(quarter // 256):
        rows, below = pl.ds(256 * m, 256), pl.ds(quarter + 256 * m, 256)
        parts = []
        for r in range(4):
            by_c, by_s = dot(table_ref[rows], both[r]), dot(table_ref[below], both[r])
            parts.append((by_c[:, :128] + by_s[:, 128:], by_c[:, 128:] - by_s[:, :128]))
        c1, s1 = turns(1, rows)
        c2, s2 = turns(2, rows)
        c3, s3 = turns(3, rows)
        (g0, _), (g1, h1), (g2, h2), (g3, h3) = parts
        middle = c2 * g2 - s2 * h2
        p = c1 * g1 - s1 * h1 + c3 * g3 - s3 * h3
        q = s3 * g3 + c3 * h3 - s1 * g1 - c1 * h1
        plus, minus = g0 + middle, g0 - middle
        for t, value in enumerate((plus + p, minus + q, plus - p, minus - q)):
            out_ref[pl.ds(quarter * t + 256 * m, 256)] = value.astype(BF16)


def pixel_kernel(x_ref, beam_ref, table_ref, turn_ref, out_ref):
    blocks, rows, _ = x_ref.shape
    half = beam_ref.shape[1] // 2
    share = out_ref.shape[2]
    lane = lax.broadcasted_iota(jnp.int32, (rows, 128), 1)
    even = [x_ref[b] for b in range(blocks // 2)]
    straight, crossed = [], []
    for b in range(blocks // 2):
        odd = x_ref[blocks - 1 - b].astype(F32)
        moved = pltpu.roll(odd, 64, 1)
        turned = jnp.where(lane < 64, -moved, moved)
        if b == 0:
            odd = jnp.where(lane == 64, 0.0, odd)
            turned = jnp.where(lane == 64, 0.0, turned)
        straight.append(odd.astype(BF16))
        crossed.append(turned.astype(BF16))
    wide = [jnp.concatenate(part, 1) for part in (even, straight, crossed)]
    wide = jnp.concatenate(wide, 0)
    for part in range(half // share):
        lanes = pl.ds(share * part, share)
        got = dot(wide, table_ref[lanes, :], NT)
        by_even = got[:rows]
        by_odd = turn_ref[0:1, lanes] * got[rows : 2 * rows] + turn_ref[1:2, lanes] * got[2 * rows :]
        out_ref[part] = (beam_ref[:, lanes] * (by_even + by_odd)).astype(BF16)
        late = pl.ds(half + share * part, share)
        out_ref[part + half // share] = (beam_ref[:, late] * (by_even - by_odd)).astype(BF16)


def sum_kernel(points, me_ref, starts_ref, terms_ref, mine_ref, theirs_ref):
    pointings, rows, share = terms_ref.shape
    ptg, core = me_ref[0], me_ref[1]
    lane = lax.broadcasted_iota(jnp.int32, (rows, share), 1)
    for ref, side in ((mine_ref, core), (theirs_ref, 1 - core)):
        for turn in range(2):
            lap = 2 * side + jnp.where(ptg % 2 == turn, 0, 1)
            column = lane + (lap * points + ptg * share)
            total = jnp.zeros((rows, share), F32)
            for p in range(pointings):
                inside = (column >= starts_ref[p]) & (column < starts_ref[p] + points)
                total += jnp.where(inside, terms_ref[p].astype(F32), 0.0)
            ref[turn] = total.astype(BF16)


def call(kernel, outs, specs, *args, scratch=(), flops=0, moved=4 << 20, limit=16):
    return pl.pallas_call(
        kernel,
        out_shape=outs,
        in_specs=specs,
        out_specs=jax.tree.map(lambda _: VMEM, outs),
        scratch_shapes=list(scratch),
        compiler_params=pltpu.CompilerParams(vmem_limit_bytes=limit << 20),
        cost_estimate=pl.CostEstimate(flops=flops, bytes_accessed=moved, transcendentals=0),
    )(*args)


def shape(*dims, dtype=BF16):
    return jax.ShapeDtypeStruct(dims, dtype)


IMG = ("s", "b")


def shards(image, beam, counts, offsets):
    points = counts.shape[1]
    laps, parts = lax.axis_size("s"), lax.axis_size("b")
    devices = laps * parts
    pointings = lax.axis_size("ptg")
    rows = points // devices
    tile = image.shape[1]
    me = lax.axis_index(IMG).astype(jnp.int32)
    ptg = lax.axis_index("ptg").astype(jnp.int32)
    start = offsets[0]
    place = me.reshape(1)

    starts = jnp.where(jnp.arange(pointings) == ptg, start, 0)
    share_rows = rows // pointings
    shares = image.reshape(laps, parts, pointings, share_rows, tile)
    shares = lax.dynamic_index_in_dim(shares, ptg, 2, keepdims=False)
    across, turn = bf16(row_table(points, devices)), jnp.asarray(row_turn(points))
    own, send, edge = call(
        choose_kernel,
        (shape(points, 128), shape(points // 2, 128), shape(points // 128, 128)),
        [SMEM, VMEM, VMEM],
        place,
        counts[0],
        across,
        flops=points * 128 * 512,
    )
    shares = lax.all_to_all(shares, "s", split_axis=0, concat_axis=0, tiled=True)
    near = [
        lax.ppermute(starts, "ptg", [(p, p ^ bit) for p in range(pointings)]) for bit in (1, 2, 3)
    ]
    starts = starts + near[0] + near[1] + near[2]
    starts = starts + lax.ppermute(starts, "ptg", [(p, p ^ 4) for p in range(pointings)])
    twice = jnp.concatenate([beam[0], beam[0]], 1)
    turned = lax.dynamic_slice_in_dim(twice, (points - start % points) % points, points, 1)
    picked = call(
        functools.partial(pick_kernel, points),
        shape(pointings, parts, share_rows, tile),
        [SMEM, SMEM, VMEM],
        lax.axis_index("b").astype(jnp.int32).reshape(1),
        starts,
        shares,
        moved=1 << 20,
    )
    window = lax.all_to_all(
        picked.reshape(pointings * parts, share_rows, tile),
        ("ptg", "b"),
        split_axis=0,
        concat_axis=0,
        tiled=True,
    ).reshape(pointings, parts, share_rows, tile)
    window, turned, own, send, edge = lax.optimization_barrier((window, turned, own, send, edge))
    got = lax.ppermute(send, IMG, [(i, devices - 1 - i) for i in range(devices)])
    edge = lax.ppermute(
        edge,
        IMG,
        [(i, (devices - i) % (devices // 2)) for i in range(devices // 2, devices)],
    )
    weight = call(
        weight_kernel,
        shape(points, 128),
        [SMEM] + [VMEM] * 3,
        place,
        own,
        got,
        edge,
        scratch=[pltpu.VMEM((points, 128), BF16), pltpu.VMEM((points, 128), F32)],
        flops=points * 128 * 1024,
    )

    spectrum = call(
        row_kernel,
        shape(devices, rows, 128),
        [VMEM] * 4,
        window,
        turned,
        across,
        turn,
        flops=rows * points * points,
    )
    col = lax.all_to_all(spectrum, IMG, split_axis=0, concat_axis=0, tiled=True)
    back = call(
        column_kernel,
        shape(points, 128),
        [SMEM] + [VMEM] * 4,
        place,
        col.reshape(points, 128),
        weight,
        bf16(column_table(points)),
        jnp.asarray(column_turn(points)),
        scratch=[pltpu.VMEM((8, points // 4, 256), BF16)],
        flops=4 * points * points * 128,
    )
    lines = lax.all_to_all(
        back.reshape(devices, rows, 128), IMG, split_axis=0, concat_axis=0, tiled=True
    )
    share = points // pointings
    contribution = call(
        pixel_kernel,
        shape(pointings, rows, share),
        [VMEM] * 4,
        lines,
        turned,
        across,
        turn,
        flops=rows * points * points,
    )
    terms = lax.all_to_all(contribution, "ptg", split_axis=0, concat_axis=0, tiled=True)
    mine, theirs = call(
        functools.partial(sum_kernel, points),
        (shape(2, rows, share), shape(2, rows, share)),
        [SMEM, SMEM, VMEM],
        jnp.stack([ptg, me % 2]),
        starts,
        terms,
        moved=1 << 20,
    )
    other = lax.ppermute(theirs, IMG, [(i, i ^ 1) for i in range(devices)])
    per_lap = parts
    halves = tile // share
    received = []
    for turn in range(2):
        pairs = []
        for q in range(pointings):
            for i in range(devices):
                lap = 2 * (i % 2) + (turn ^ (q % 2))
                pairs.append((q * devices + i, (i // 2) * devices + per_lap * lap + q // halves))
        block = jnp.concatenate([mine[turn], other[turn]], 0)
        received.append(lax.ppermute(block, ("ptg", *IMG), pairs))
    lap = me // per_lap
    out = jnp.where(
        lap % 2 == 1,
        jnp.concatenate([received[1], received[0]], 1),
        jnp.concatenate([received[0], received[1]], 1),
    ).astype(F32)
    flipped = jnp.concatenate([out[rows:], out[:rows]], 0)
    return jnp.where(lap >= 2, flipped, out)


def solution(mesh):
    pointings, devices = mesh.devices.shape
    split = Mesh(mesh.devices.reshape(pointings, 4, devices // 4), ("ptg", *IMG))
    return jax.shard_map(
        shards,
        mesh=split,
        in_specs=(P(None, IMG), P("ptg", IMG, None), P("ptg", None, IMG), P("ptg")),
        out_specs=P("ptg", IMG),
        check_vma=False,
    )
```

```python
import functools

import numpy as np

import jax
import jax.numpy as jnp
from jax import lax
from jax.experimental import pallas as pl
from jax.experimental.pallas import tpu as pltpu
from jax.sharding import Mesh, PartitionSpec as P

F32, BF16 = jnp.float32, jnp.bfloat16
NT = (((1,), (1,)), ((), ()))
NN = (((1,), (0,)), ((), ()))
VMEM = pl.BlockSpec(memory_space=pltpu.VMEM)
SMEM = pl.BlockSpec(memory_space=pltpu.SMEM)


def dot(a, b, dims=NN):
    return lax.dot_general(a, b, dims, preferred_element_type=F32)


def row_table(points, devices):
    half, lanes = points // 2, points // devices
    index = np.arange(half)
    turn = 2.0 * np.pi / points * np.arange(points)
    cos_of, sin_of = np.cos(turn), -np.sin(turn)
    freq = lanes * np.arange(devices // 2)[:, None] + 2 * np.arange(lanes // 2)[None, :]
    phase = index[:, None, None] * freq[None] % points
    imag = sin_of[phase]
    imag[:, 0, 0] = cos_of[index * half % points]
    return np.concatenate([cos_of[phase], imag], axis=2).reshape(half, half)


def row_turn(points):
    angle = 2.0 * np.pi / points * np.arange(points // 2)
    return np.stack([np.cos(angle), np.sin(angle)] * 4).astype(np.float32)


def column_table(points):
    quarter = points // 4
    index = np.arange(quarter)
    angle = 2.0 * np.pi / quarter * (index[:, None] * index[None, :] % quarter)
    return np.concatenate([np.cos(angle), -np.sin(angle)])


def column_turn(points):
    angle = 2.0 * np.pi / points * np.arange(points // 4)[:, None] * np.arange(4)[None, :]
    made = np.zeros((points // 4, 128), np.float32)
    made[:, :4], made[:, 4:8] = np.cos(angle), np.sin(angle)
    return made


def bf16(table):
    return jnp.asarray(np.asarray(table, np.float32).astype(jnp.bfloat16))


def ones_where(condition):
    return jnp.where(condition, 1.0, 0.0).astype(BF16)


def grid(rows, lanes):
    index = lambda axis: lax.broadcasted_iota(jnp.int32, (rows, lanes), axis)
    return index(0), index(1)


def choose_kernel(me_ref, counts_ref, _, own_ref, send_ref, edge_ref):
    points = counts_ref.shape[0]
    source, target = grid(128, 256)
    k, sent = target % 64, target // 128
    choice = ones_where(source == jnp.where(me_ref[0] < 8, 2 * k, 127 - 2 * k) + sent)
    unit_row, unit_lane = grid(16, 128)
    first = ones_where((unit_row == 0) & (unit_lane == 0))
    lane = lax.broadcasted_iota(jnp.int32, (256, 128), 1)
    for b in range(points // 512):
        low = counts_ref[pl.ds(256 * b, 256)].astype(F32).astype(BF16)
        high = counts_ref[pl.ds(256 * b + points // 2, 256)].astype(F32).astype(BF16)
        got_low, got_high = dot(low, choice), dot(high, choice)
        own_ref[pl.ds(256 * b, 256)] = got_low[:, :128].astype(BF16)
        own_ref[pl.ds(256 * b + points // 2, 256)] = got_high[:, :128].astype(BF16)
        send_ref[pl.ds(256 * b, 256)] = jnp.where(
            lane < 64, got_low[:, 128:], got_high[:, 128:]
        ).astype(BF16)
    edges = []
    for b in range(points // 128):
        block = counts_ref[pl.ds(128 * b, 128)].astype(F32).astype(BF16)
        edges.append(dot(first, block, NT)[:1])
    edge_ref[...] = jnp.concatenate(edges, 0).astype(BF16)


def weight_kernel(me_ref, own_ref, got_ref, edge_ref, out_ref, plus, minus):
    points = own_ref.shape[0]
    target, source = grid(256, 256)
    index = 4 * (target % 64) + target // 64
    direct = ones_where(source == index)
    negated = ones_where(source == 256 - index)
    row, column = grid(128, 128)
    eye = ones_where(row == column)
    me = me_ref[0]
    low, zero = me < 8, me == 0
    edge = dot(eye, edge_ref[...], NT)
    lane = lax.broadcasted_iota(jnp.int32, (128, 128), 1)
    for b in range(points // 128):
        rows = pl.ds(128 * b, 128)
        own = own_ref[rows].astype(F32)
        packed = got_ref[pl.ds(128 * b % (points // 2), 128)].astype(F32)
        moved = pltpu.roll(packed, 64, 1)
        in_left = 128 * b < points // 2
        got = jnp.where((lane < 64) == in_left, packed, moved)
        column = jnp.broadcast_to(edge[:, b : b + 1], (128, 128))
        straight = jnp.where(low, own, got)
        mirrored = jnp.where(low, got, own)
        first = jnp.where(zero, jnp.where(lane == 0, own, column), column)
        mirrored = jnp.where(low & (lane % 64 == 0), first, mirrored)
        straight = jnp.where(zero & (lane == 64), column, straight)
        plus[rows] = straight.astype(BF16)
        minus[rows] = mirrored
    blocks = points // 256
    row = lax.broadcasted_iota(jnp.int32, (256, 128), 0)
    wide = lax.broadcasted_iota(jnp.int32, (256, 128), 1)
    scale = jnp.where(zero & (wide % 64 == 0), 0.5, 1.0)
    for b in range(blocks):
        taken = dot(direct, plus[pl.ds(256 * b, 256)])
        taken += dot(negated, minus[pl.ds(256 * (blocks - 1 - b), 256)].astype(BF16))
        wrapped = minus[pl.ds(256 * ((blocks - b) % blocks), 1)]
        taken = scale * (taken + jnp.where(row == 0, wrapped, 0.0))
        for r in range(4):
            out_ref[pl.ds(r * points // 4 + 64 * b, 64)] = taken[64 * r : 64 * r + 64].astype(BF16)


def pick_kernel(points, place_ref, starts_ref, tiles_ref, out_ref):
    laps, parts, rows, wide = tiles_ref.shape
    lane = lax.broadcasted_iota(jnp.int32, (rows, wide), 1) + place_ref[0] * wide
    for part in range(parts):
        held = [tiles_ref[lap, part].astype(F32) for lap in range(laps)]
        for p in range(out_ref.shape[0]):
            start = starts_ref[p]
            window = jnp.zeros((rows, wide), F32)
            for lap in range(laps):
                column = lane + lap * points
                inside = (column >= start) & (column < start + points)
                window = jnp.where(inside, held[lap], window)
            out_ref[p, part] = window.astype(BF16)


def row_kernel(window_ref, beam_ref, table_ref, turn_ref, out_ref):
    shares, parts, _, wide = window_ref.shape
    rows = out_ref.shape[1]
    beamed = []
    for part in range(parts):
        window = jnp.concatenate([window_ref[q, part] for q in range(shares)], 0)
        beamed.append(window.astype(F32) * beam_ref[:, pl.ds(part * wide, wide)])
    left = jnp.concatenate(beamed[: parts // 2], 1)
    right = jnp.concatenate(beamed[parts // 2 :], 1)
    minus = left - right
    folded = [left + right, minus * turn_ref[0:1], minus * turn_ref[1:2]]
    folded = jnp.concatenate([t.astype(BF16) for t in folded], 0)
    last = out_ref.shape[0] - 1
    lane = lax.broadcasted_iota(jnp.int32, (rows, 128), 1)
    for part in range(table_ref.shape[1] // 256):
        got = dot(folded, table_ref[:, pl.ds(256 * part, 256)])
        for n in (0, 1):
            block = 2 * part + n
            even, by_cos, by_sin = (
                got[rows * t : rows * (t + 1), 128 * n : 128 * (n + 1)] for t in range(3)
            )
            if block == 0:
                by_cos = jnp.where(lane == 64, 0.0, by_cos)
                by_sin = jnp.where(lane == 64, 0.0, by_sin)
            moved = pltpu.roll(by_sin, 64, 1)
            out_ref[block] = even.astype(BF16)
            out_ref[last - block] = jnp.where(lane < 64, by_cos + moved, by_cos - moved).astype(BF16)


def column_kernel(me_ref, x_ref, weight_ref, table_ref, turn_ref, out_ref, both):
    points = x_ref.shape[0]
    quarter = points // 4
    scale = 1.0 / float(points * points)
    lane = lax.broadcasted_iota(jnp.int32, (256, 128), 1)
    sign = jnp.where(lane < 64, -1.0, 1.0)
    packed = (me_ref[0] == 0) & (lane % 64 == 0)
    turns = lambda r, rows: (
        jnp.broadcast_to(turn_ref[rows, r : r + 1], (256, 128)),
        jnp.broadcast_to(turn_ref[rows, 4 + r : 5 + r], (256, 128)),
    )
    for m in range(quarter // 256):
        rows = pl.ds(256 * m, 256)
        x = [x_ref[pl.ds(quarter * t + 256 * m, 256)].astype(F32) for t in range(4)]
        even, p, odd, q = x[0] + x[2], x[0] - x[2], x[1] + x[3], x[1] - x[3]
        c1, s1 = turns(1, rows)
        c2, s2 = turns(2, rows)
        c3, s3 = turns(3, rows)
        pairs = [
            (even + odd, jnp.zeros_like(even)),
            (p * c1 - q * s1, -(p * s1 + q * c1)),
            ((even - odd) * c2, -(even - odd) * s2),
            (p * c3 + q * s3, q * c3 - p * s3),
        ]
        for r in range(4):
            both[4 + r, rows, 0:128] = pairs[r][0].astype(BF16)
            both[4 + r, rows, 128:256] = pairs[r][1].astype(BF16)
    for r in range(4):
        for m in range(quarter // 256):
            rows, below = pl.ds(256 * m, 256), pl.ds(quarter + 256 * m, 256)
            wide = both[4 + r] if r else both[4, :, 0:128]
            by_c, by_s = dot(table_ref[rows], wide), dot(table_ref[below], wide)
            by_cos, by_sin = by_c[:, :128], by_s[:, :128]
            if r:
                by_cos, by_sin = by_cos - by_s[:, 128:], by_sin + by_c[:, 128:]
            weight = weight_ref[pl.ds(r * quarter + 256 * m, 256)].astype(F32) * scale
            up = weight * (by_cos + jnp.where(packed, 0.0, sign * pltpu.roll(by_sin, 64, 1)))
            down = jnp.where(packed, weight * by_sin, -sign * pltpu.roll(up, 64, 1))
            both[r, rows, 0:128] = up.astype(BF16)
            both[r, rows, 128:256] = down.astype(BF16)
    for m in range(quarter // 256):
        rows, below = pl.ds(256 * m, 256), pl.ds(quarter + 256 * m, 256)
        parts = []
        for r in range(4):
            by_c, by_s = dot(table_ref[rows], both[r]), dot(table_ref[below], both[r])
            parts.append((by_c[:, :128] + by_s[:, 128:], by_c[:, 128:] - by_s[:, :128]))
        c1, s1 = turns(1, rows)
        c2, s2 = turns(2, rows)
        c3, s3 = turns(3, rows)
        (g0, _), (g1, h1), (g2, h2), (g3, h3) = parts
        middle = c2 * g2 - s2 * h2
        p = c1 * g1 - s1 * h1 + c3 * g3 - s3 * h3
        q = s3 * g3 + c3 * h3 - s1 * g1 - c1 * h1
        plus, minus = g0 + middle, g0 - middle
        for t, value in enumerate((plus + p, minus + q, plus - p, minus - q)):
            out_ref[pl.ds(quarter * t + 256 * m, 256)] = value.astype(BF16)


def pixel_kernel(x_ref, beam_ref, table_ref, turn_ref, out_ref):
    blocks, rows, _ = x_ref.shape
    half = beam_ref.shape[1] // 2
    share = out_ref.shape[2]
    lane = lax.broadcasted_iota(jnp.int32, (rows, 128), 1)
    even = [x_ref[b] for b in range(blocks // 2)]
    straight, crossed = [], []
    for b in range(blocks // 2):
        odd = x_ref[blocks - 1 - b].astype(F32)
        moved = pltpu.roll(odd, 64, 1)
        turned = jnp.where(lane < 64, -moved, moved)
        if b == 0:
            odd = jnp.where(lane == 64, 0.0, odd)
            turned = jnp.where(lane == 64, 0.0, turned)
        straight.append(odd.astype(BF16))
        crossed.append(turned.astype(BF16))
    wide = [jnp.concatenate(part, 1) for part in (even, straight, crossed)]
    wide = jnp.concatenate(wide, 0)
    for part in range(half // share):
        lanes = pl.ds(share * part, share)
        got = dot(wide, table_ref[lanes, :], NT)
        by_even = got[:rows]
        by_odd = turn_ref[0:1, lanes] * got[rows : 2 * rows] + turn_ref[1:2, lanes] * got[2 * rows :]
        out_ref[part] = (beam_ref[:, lanes] * (by_even + by_odd)).astype(BF16)
        late = pl.ds(half + share * part, share)
        out_ref[part + half // share] = (beam_ref[:, late] * (by_even - by_odd)).astype(BF16)


def sum_kernel(points, me_ref, starts_ref, terms_ref, mine_ref, theirs_ref):
    pointings, rows, share = terms_ref.shape
    ptg, core = me_ref[0], me_ref[1]
    lane = lax.broadcasted_iota(jnp.int32, (rows, share), 1)
    for ref, side in ((mine_ref, core), (theirs_ref, 1 - core)):
        for turn in range(2):
            lap = 2 * side + jnp.where(ptg % 2 == turn, 0, 1)
            column = lane + (lap * points + ptg * share)
            total = jnp.zeros((rows, share), F32)
            for p in range(pointings):
                inside = (column >= starts_ref[p]) & (column < starts_ref[p] + points)
                total += jnp.where(inside, terms_ref[p].astype(F32), 0.0)
            ref[turn] = total.astype(BF16)


def call(kernel, outs, specs, *args, scratch=(), flops=0, moved=4 << 20, limit=16):
    return pl.pallas_call(
        kernel,
        out_shape=outs,
        in_specs=specs,
        out_specs=jax.tree.map(lambda _: VMEM, outs),
        scratch_shapes=list(scratch),
        compiler_params=pltpu.CompilerParams(vmem_limit_bytes=limit << 20),
        cost_estimate=pl.CostEstimate(flops=flops, bytes_accessed=moved, transcendentals=0),
    )(*args)


def shape(*dims, dtype=BF16):
    return jax.ShapeDtypeStruct(dims, dtype)


IMG = ("s", "b")


def shards(image, beam, counts, offsets):
    points = counts.shape[1]
    laps, parts = lax.axis_size("s"), lax.axis_size("b")
    devices = laps * parts
    pointings = lax.axis_size("ptg")
    rows = points // devices
    tile = image.shape[1]
    me = lax.axis_index(IMG).astype(jnp.int32)
    ptg = lax.axis_index("ptg").astype(jnp.int32)
    start = offsets[0]
    place = me.reshape(1)

    starts = jnp.where(jnp.arange(pointings) == ptg, start, 0)
    share_rows = rows // pointings
    shares = image.reshape(laps, parts, pointings, share_rows, tile)
    shares = lax.dynamic_index_in_dim(shares, ptg, 2, keepdims=False)
    across, turn = bf16(row_table(points, devices)), jnp.asarray(row_turn(points))
    own, send, edge = call(
        choose_kernel,
        (shape(points, 128), shape(points // 2, 128), shape(points // 128, 128)),
        [SMEM, VMEM, VMEM],
        place,
        counts[0],
        across,
        flops=points * 128 * 512,
    )
    shares = lax.all_to_all(shares, "s", split_axis=0, concat_axis=0, tiled=True)
    near = [
        lax.ppermute(starts, "ptg", [(p, p ^ bit) for p in range(pointings)]) for bit in (1, 2, 3)
    ]
    starts = starts + near[0] + near[1] + near[2]
    starts = starts + lax.ppermute(starts, "ptg", [(p, p ^ 4) for p in range(pointings)])
    got = lax.ppermute(send, IMG, [(i, devices - 1 - i) for i in range(devices)])
    edge = lax.ppermute(
        edge,
        IMG,
        [(i, (devices - i) % (devices // 2)) for i in range(devices // 2, devices)],
    )
    twice = jnp.concatenate([beam[0], beam[0]], 1)
    turned = lax.dynamic_slice_in_dim(twice, (points - start % points) % points, points, 1)
    picked = call(
        functools.partial(pick_kernel, points),
        shape(pointings, parts, share_rows, tile),
        [SMEM, SMEM, VMEM],
        lax.axis_index("b").astype(jnp.int32).reshape(1),
        starts,
        shares,
        moved=1 << 20,
    )
    picked, got, edge = lax.optimization_barrier((picked, got, edge))
    window = lax.all_to_all(
        picked.reshape(pointings * parts, share_rows, tile),
        ("ptg", "b"),
        split_axis=0,
        concat_axis=0,
        tiled=True,
    ).reshape(pointings, parts, share_rows, tile)
    weight = call(
        weight_kernel,
        shape(points, 128),
        [SMEM] + [VMEM] * 3,
        place,
        own,
        got,
        edge,
        scratch=[pltpu.VMEM((points, 128), BF16), pltpu.VMEM((points, 128), F32)],
        flops=points * 128 * 1024,
    )
    window, weight, turned = lax.optimization_barrier((window, weight, turned))
    spectrum = call(
        row_kernel,
        shape(devices, rows, 128),
        [VMEM] * 4,
        window,
        turned,
        across,
        turn,
        flops=rows * points * points,
    )
    col = lax.all_to_all(spectrum, IMG, split_axis=0, concat_axis=0, tiled=True)
    back = call(
        column_kernel,
        shape(points, 128),
        [SMEM] + [VMEM] * 4,
        place,
        col.reshape(points, 128),
        weight,
        bf16(column_table(points)),
        jnp.asarray(column_turn(points)),
        scratch=[pltpu.VMEM((8, points // 4, 256), BF16)],
        flops=4 * points * points * 128,
    )
    lines = lax.all_to_all(
        back.reshape(devices, rows, 128), IMG, split_axis=0, concat_axis=0, tiled=True
    )
    share = points // pointings
    contribution = call(
        pixel_kernel,
        shape(pointings, rows, share),
        [VMEM] * 4,
        lines,
        turned,
        across,
        turn,
        flops=rows * points * points,
    )
    terms = lax.all_to_all(contribution, "ptg", split_axis=0, concat_axis=0, tiled=True)
    mine, theirs = call(
        functools.partial(sum_kernel, points),
        (shape(2, rows, share), shape(2, rows, share)),
        [SMEM, SMEM, VMEM],
        jnp.stack([ptg, me % 2]),
        starts,
        terms,
        moved=1 << 20,
    )
    other = lax.ppermute(theirs, IMG, [(i, i ^ 1) for i in range(devices)])
    per_lap = parts
    halves = tile // share
    received = []
    for turn in range(2):
        pairs = []
        for q in range(pointings):
            for i in range(devices):
                lap = 2 * (i % 2) + (turn ^ (q % 2))
                pairs.append((q * devices + i, (i // 2) * devices + per_lap * lap + q // halves))
        block = jnp.concatenate([mine[turn], other[turn]], 0)
        received.append(lax.ppermute(block, ("ptg", *IMG), pairs))
    lap = me // per_lap
    out = jnp.where(
        lap % 2 == 1,
        jnp.concatenate([received[1], received[0]], 1),
        jnp.concatenate([received[0], received[1]], 1),
    ).astype(F32)
    flipped = jnp.concatenate([out[rows:], out[:rows]], 0)
    return jnp.where(lap >= 2, flipped, out)


def solution(mesh):
    pointings, devices = mesh.devices.shape
    split = Mesh(mesh.devices.reshape(pointings, 4, devices // 4), ("ptg", *IMG))
    return jax.shard_map(
        shards,
        mesh=split,
        in_specs=(P(None, IMG), P("ptg", IMG, None), P("ptg", None, IMG), P("ptg")),
        out_specs=P("ptg", IMG),
        check_vma=False,
    )
```

```python
import functools

import numpy as np

import jax
import jax.numpy as jnp
from jax import lax
from jax.experimental import pallas as pl
from jax.experimental.pallas import tpu as pltpu
from jax.sharding import Mesh, PartitionSpec as P

F32, BF16 = jnp.float32, jnp.bfloat16
NT = (((1,), (1,)), ((), ()))
NN = (((1,), (0,)), ((), ()))
VMEM = pl.BlockSpec(memory_space=pltpu.VMEM)
SMEM = pl.BlockSpec(memory_space=pltpu.SMEM)


def dot(a, b, dims=NN):
    return lax.dot_general(a, b, dims, preferred_element_type=F32)


def half_table(points, devices):
    half, lanes = points // 2, points // devices
    index = np.arange(half)
    turn = 2.0 * np.pi / points * np.arange(points)
    cos_of, sin_of = np.cos(turn), -np.sin(turn)
    freq = lanes * np.arange(devices // 2)[:, None] + 2 * np.arange(lanes // 2)[None, :]
    phase = index[:, None, None] * freq[None] % points
    imag = sin_of[phase]
    imag[:, 0, 0] = cos_of[index * half % points]
    return np.concatenate([cos_of[phase], imag], axis=2).reshape(half, half)


def half_turn(points):
    angle = 2.0 * np.pi / points * np.arange(points // 2)
    made = np.zeros((points // 2, 128), np.float32)
    made[:, 0], made[:, 1] = np.cos(angle), np.sin(angle)
    return made


def quarter_table(points):
    quarter = points // 4
    index = np.arange(quarter)
    angle = 2.0 * np.pi / quarter * (index[:, None] * index[None, :] % quarter)
    return np.concatenate([np.cos(angle), -np.sin(angle)], 1)


def quarter_turn(points):
    angle = 2.0 * np.pi / points * np.arange(4)[:, None] * np.arange(points // 4)[None, :]
    return np.concatenate([np.cos(angle), np.sin(angle)]).astype(np.float32)


def bf16(table):
    return jnp.asarray(np.asarray(table, np.float32).astype(jnp.bfloat16))


def ones_where(condition):
    return jnp.where(condition, 1.0, 0.0).astype(BF16)


def grid(rows, lanes):
    index = lambda axis: lax.broadcasted_iota(jnp.int32, (rows, lanes), axis)
    return index(0), index(1)


def swap_rows(t):
    half = t.shape[0] // 2
    return jnp.concatenate([t[half:], t[:half]], 0)


def choose_kernel(counts_ref, out_ref):
    blocks = out_ref.shape[0]
    target, source = grid(128, 128)
    k, odd = target % 64, target // 64
    direct = ones_where(source == 2 * k + odd)
    negated = ones_where(source == 128 - 2 * k - odd)
    row, _ = grid(128, 128)
    for i in range(blocks // 2):
        part = lambda b: counts_ref[pl.ds(128 * b, 128)].astype(F32)
        kept = dot(direct, part(i).astype(BF16))
        mirrored = dot(negated, part(blocks - 1 - i).astype(BF16))
        wrapped = counts_ref[pl.ds(128 * (blocks - i if i else blocks // 2), 8)].astype(F32)[:1]
        mirrored = mirrored + jnp.where(row == 0, wrapped, 0.0)
        for side, m in ((0, i), (1, blocks - 1 - i)):
            out_ref[m, 0:64] = kept[64 * side : 64 * side + 64].astype(BF16)
            out_ref[m, 64:128] = mirrored[64 * side : 64 * side + 64].astype(BF16)


def weight_kernel(me_ref, got_ref, out_ref):
    zero = me_ref[0] == 0
    source, target = grid(512, 512)
    index = 4 * (target % 128) + target // 128
    direct, negated = ones_where(source == index), ones_where(source == 512 - index)
    row, lane = grid(64, 128)
    only = zero & (row == 0)
    wide_row, _ = grid(64, 512)
    group = lambda g: jnp.concatenate([got_ref[4 * g + n] for n in range(4)], 1)
    for g in range(4):
        here = dot(group(g), direct)
        there = dot(group(3 - g)[64:], negated)
        corner = jnp.where(lane == 0, got_ref[4 * ((4 - g) % 4), 64:128].astype(F32), 0.0)
        first = there[:, :128] + corner
        there = jnp.concatenate([first, there[:, 128:]], 1)
        above = here[:64] + jnp.where(zero & (wide_row == 0), 0.0, there)
        below = jnp.where(zero & (wide_row == 0), here[64:], above)
        for r in range(4):
            lanes = pl.ds(512 * r + 128 * g, 128)
            out_ref[0:64, lanes] = above[:, 128 * r : 128 * r + 128].astype(BF16)
            out_ref[64:128, lanes] = below[:, 128 * r : 128 * r + 128].astype(BF16)


def beam_kernel(start_ref, beam_ref, out_ref):
    rows, points = beam_ref.shape
    turned = pltpu.roll(beam_ref[...], lax.rem(start_ref[0], points), 1).astype(BF16)
    for s in range(4):
        for b in range(4):
            out_ref[4 * s + b] = turned[:, 512 * b + 128 * s : 512 * b + 128 * s + 128]


def pick_kernel(points, place_ref, starts_ref, tiles_ref, out_ref):
    laps, rows, wide = tiles_ref.shape
    lane = lax.broadcasted_iota(jnp.int32, (rows, wide), 1) + place_ref[0] * wide
    held = [tiles_ref[lap].astype(F32) for lap in range(laps)]
    for p in range(out_ref.shape[0]):
        ahead = lane - starts_ref[p]
        window = held[0]
        for lap in range(1, laps):
            column = ahead + lap * points
            window = jnp.where((column >= 0) & (column < points), held[lap], window)
        out_ref[p] = window.astype(BF16)


def half_kernel(window_ref, beam_ref, table_ref, turn_ref, out_ref):
    points = beam_ref.shape[0]
    half = points // 2
    blocks = out_ref.shape[0]
    beamed = window_ref[...].astype(F32) * beam_ref[...].astype(F32)
    left, right = beamed[:half], beamed[half:]
    minus = left - right
    cos_of = jnp.broadcast_to(turn_ref[:, 0:1], (half, 128))
    sin_of = jnp.broadcast_to(turn_ref[:, 1:2], (half, 128))
    folded = [left + right, minus * cos_of, minus * sin_of]
    folded = jnp.concatenate([t.astype(BF16) for t in folded], 1)
    row, _ = grid(128, 128)
    for part in range(half // 256):
        got = dot(table_ref[pl.ds(256 * part, 256), :], folded)
        for n in (0, 1):
            block = 2 * part + n
            even, by_cos, by_sin = (
                got[128 * n : 128 * (n + 1), 128 * t : 128 * (t + 1)] for t in range(3)
            )
            if block == 0:
                by_cos = jnp.where(row == 64, 0.0, by_cos)
                by_sin = jnp.where(row == 64, 0.0, by_sin)
            moved = swap_rows(by_sin)
            odd = jnp.where(row < 64, by_cos + moved, by_cos - moved)
            out_ref[block] = even.astype(BF16)
            out_ref[blocks - 1 - block] = odd.astype(BF16)


def middle_kernel(me_ref, x_ref, weight_ref, table_ref, turn_ref, out_ref, both):
    quarter = table_ref.shape[0]
    scale = 1.0 / float(16 * quarter * quarter)
    row, _ = grid(128, 256)
    sign = jnp.where(row < 64, -1.0, 1.0)
    packed = (me_ref[0] == 0) & (row % 64 == 0)
    x = []
    for t in range(4):
        x.append(jnp.concatenate([x_ref[4 * s + t] for s in range(4)], 1).astype(F32))
    even, p, odd, q = x[0] + x[2], x[0] - x[2], x[1] + x[3], x[1] - x[3]
    c1, c2, c3 = (turn_ref[r : r + 1] for r in (1, 2, 3))
    s1, s2, s3 = (turn_ref[4 + r : 5 + r] for r in (1, 2, 3))
    pairs = [
        (even + odd, None),
        (p * c1 - q * s1, -(p * s1 + q * c1)),
        ((even - odd) * c2, -(even - odd) * s2),
        (p * c3 + q * s3, q * c3 - p * s3),
    ]
    for r in range(4):
        g = pairs[r][0].astype(BF16)
        wide = jnp.concatenate([g, pairs[r][1].astype(BF16)], 0) if r else g
        for m in range(quarter // 256):
            lanes, beside = pl.ds(256 * m, 256), pl.ds(quarter + 256 * m, 256)
            by_c, by_s = dot(wide, table_ref[:, lanes]), dot(wide, table_ref[:, beside])
            by_cos, by_sin = by_c[:128], by_s[:128]
            if r:
                by_cos, by_sin = by_cos - by_s[128:], by_sin + by_c[128:]
            weight = weight_ref[:, pl.ds(r * quarter + 256 * m, 256)].astype(F32) * scale
            up = weight * (by_cos + jnp.where(packed, 0.0, sign * swap_rows(by_sin)))
            down = jnp.where(packed, weight * by_sin, -sign * swap_rows(up))
            both[r, 0:128, lanes] = up.astype(BF16)
            both[r, 128:256, lanes] = down.astype(BF16)
    for m in range(quarter // 256):
        lanes, beside = pl.ds(256 * m, 256), pl.ds(quarter + 256 * m, 256)
        parts = []
        for r in range(4):
            by_c, by_s = dot(both[r], table_ref[:, lanes]), dot(both[r], table_ref[:, beside])
            parts.append((by_c[:128] + by_s[128:], by_c[128:] - by_s[:128]))
        c1, c2, c3 = (turn_ref[r : r + 1, lanes] for r in (1, 2, 3))
        s1, s2, s3 = (turn_ref[4 + r : 5 + r, lanes] for r in (1, 2, 3))
        (g0, _), (g1, h1), (g2, h2), (g3, h3) = parts
        middle = c2 * g2 - s2 * h2
        p = c1 * g1 - s1 * h1 + c3 * g3 - s3 * h3
        q = s3 * g3 + c3 * h3 - s1 * g1 - c1 * h1
        plus, minus = g0 + middle, g0 - middle
        for t, value in enumerate((plus + p, minus + q, plus - p, minus - q)):
            for n in (0, 1):
                out_ref[4 * (2 * m + n) + t] = value[:, 128 * n : 128 * n + 128].astype(BF16)


def pixel_kernel(x_ref, beam_ref, table_ref, turn_ref, out_ref):
    blocks = x_ref.shape[0]
    half = beam_ref.shape[0] // 2
    share = out_ref.shape[1]
    row, _ = grid(128, 128)
    wide = []
    for b in range(blocks // 2):
        odd = x_ref[blocks - 1 - b].astype(F32)
        moved = swap_rows(odd)
        crossed = jnp.where(row < 64, -moved, moved)
        if b == 0:
            odd = jnp.where(row == 64, 0.0, odd)
            crossed = jnp.where(row == 64, 0.0, crossed)
        wide.append(jnp.concatenate([x_ref[b], odd.astype(BF16), crossed.astype(BF16)], 1))
    wide = jnp.concatenate(wide, 0)
    for part in range(half // share):
        rows, late = pl.ds(share * part, share), pl.ds(half + share * part, share)
        got = dot(table_ref[rows, :], wide)
        cos_of = jnp.broadcast_to(turn_ref[rows, 0:1], (share, 128))
        sin_of = jnp.broadcast_to(turn_ref[rows, 1:2], (share, 128))
        by_even = got[:, :128]
        by_odd = cos_of * got[:, 128:256] + sin_of * got[:, 256:]
        out_ref[part] = (beam_ref[rows, :].astype(F32) * (by_even + by_odd)).astype(BF16)
        out_ref[part + half // share] = (
            beam_ref[late, :].astype(F32) * (by_even - by_odd)
        ).astype(BF16)


def sum_kernel(points, place_ref, starts_ref, terms_ref, out_ref):
    pointings, rows, wide = terms_ref.shape
    lane = lax.broadcasted_iota(jnp.int32, (rows, wide), 1) + place_ref[0] * wide
    totals = [jnp.zeros((rows, wide), F32) for _ in range(out_ref.shape[0])]
    for p in range(pointings):
        term = terms_ref[p].astype(F32)
        ahead = lane - starts_ref[p]
        for lap in range(len(totals)):
            column = ahead + lap * points
            inside = (column >= 0) & (column < points)
            totals[lap] += jnp.where(inside, term, 0.0)
    for lap, total in enumerate(totals):
        out_ref[lap] = total.astype(BF16)


def call(kernel, outs, specs, *args, scratch=(), flops=0, moved=4 << 20, limit=16):
    return pl.pallas_call(
        kernel,
        out_shape=outs,
        in_specs=specs,
        out_specs=jax.tree.map(lambda _: VMEM, outs),
        scratch_shapes=list(scratch),
        compiler_params=pltpu.CompilerParams(vmem_limit_bytes=limit << 20),
        cost_estimate=pl.CostEstimate(flops=flops, bytes_accessed=moved, transcendentals=0),
    )(*args)


def shape(*dims, dtype=BF16):
    return jax.ShapeDtypeStruct(dims, dtype)


IMG = ("s", "b")


def swap(x, axes):
    return lax.all_to_all(x, axes, split_axis=0, concat_axis=0, tiled=True)


def shards(image, beam, counts, offsets):
    points = counts.shape[1]
    laps, parts = lax.axis_size("s"), lax.axis_size("b")
    devices = laps * parts
    pointings = lax.axis_size("ptg")
    rows = points // devices
    share = points // pointings
    tile = image.shape[1]
    lap, part = lax.axis_index("s").astype(jnp.int32), lax.axis_index("b").astype(jnp.int32)
    me = lax.axis_index(IMG).astype(jnp.int32).reshape(1)
    ptg = lax.axis_index("ptg").astype(jnp.int32)
    place = (laps * part + lap).reshape(1)

    starts = jnp.where(jnp.arange(pointings) == ptg, offsets[0], 0)
    near = [
        lax.ppermute(starts, "ptg", [(p, p ^ bit) for p in range(pointings)]) for bit in (1, 2, 3)
    ]
    starts = starts + near[0] + near[1] + near[2]
    starts = starts + lax.ppermute(starts, "ptg", [(p, p ^ 4) for p in range(pointings)])

    tiles = lax.dynamic_slice_in_dim(image, ptg * share, share, 0)
    tiles = tiles.reshape(share, laps, tile // laps).transpose(1, 0, 2)
    tiles = swap(tiles, "s")

    turned = call(
        beam_kernel, shape(devices, rows, 128), [SMEM, VMEM], offsets, beam[0], moved=2 << 20
    )
    turned = swap(turned, IMG).reshape(points, 128)
    chosen = call(
        choose_kernel,
        shape(devices, 128, counts.shape[2]),
        [VMEM],
        counts[0],
        flops=points * 128 * 256,
    )
    chosen = swap(chosen, IMG)

    picked = call(
        functools.partial(pick_kernel, points),
        shape(pointings, share, 128),
        [SMEM, SMEM, VMEM],
        place,
        starts,
        tiles,
        moved=1 << 20,
    )
    window = swap(picked, "ptg").reshape(points, 128)
    weight = call(
        weight_kernel,
        shape(128, points),
        [SMEM, VMEM],
        me,
        chosen,
        scratch=[],
        flops=points * 128 * 1024,
    )
    window, turned, weight = lax.optimization_barrier((window, turned, weight))
    table, turn = half_table(points, devices), jnp.asarray(half_turn(points))
    spectrum = call(
        half_kernel,
        shape(devices, 128, 128),
        [VMEM] * 4,
        window,
        turned,
        bf16(table.T),
        turn,
        flops=points * points * 128,
    )
    lines = call(
        middle_kernel,
        shape(devices, 128, 128),
        [SMEM] + [VMEM] * 4,
        me,
        swap(spectrum, IMG),
        weight,
        bf16(quarter_table(points)),
        jnp.asarray(quarter_turn(points)),
        scratch=[pltpu.VMEM((4, 256, points // 4), BF16)],
        flops=4 * points * points * 128,
    )
    contribution = call(
        pixel_kernel,
        shape(pointings, share, 128),
        [VMEM] * 4,
        swap(lines, IMG),
        turned,
        bf16(table),
        turn,
        flops=points * points * 128,
    )
    sums = call(
        functools.partial(sum_kernel, points),
        shape(laps, share, 128),
        [SMEM, SMEM, VMEM],
        place,
        starts,
        swap(contribution, "ptg"),
        moved=1 << 20,
    )
    sums = swap(sums, "s")
    return sums.transpose(1, 0, 2).reshape(share, tile).astype(F32)


def solution(mesh):
    pointings, devices = mesh.devices.shape
    split = Mesh(mesh.devices.reshape(pointings, 4, devices // 4), ("ptg", *IMG))
    return jax.shard_map(
        shards,
        mesh=split,
        in_specs=(P(None, IMG), P("ptg", IMG, None), P("ptg", None, IMG), P("ptg")),
        out_specs=P("ptg", IMG),
        check_vma=False,
    )
```

```python
import functools

import numpy as np

import jax
import jax.numpy as jnp
from jax import lax
from jax.experimental import pallas as pl
from jax.experimental.pallas import tpu as pltpu
from jax.sharding import Mesh, PartitionSpec as P

F32, BF16 = jnp.float32, jnp.bfloat16
NT = (((1,), (1,)), ((), ()))
NN = (((1,), (0,)), ((), ()))
VMEM = pl.BlockSpec(memory_space=pltpu.VMEM)
SMEM = pl.BlockSpec(memory_space=pltpu.SMEM)


def dot(a, b, dims=NN):
    return lax.dot_general(a, b, dims, preferred_element_type=F32)


def row_table(points, devices):
    half, lanes = points // 2, points // devices
    index = np.arange(half)
    turn = 2.0 * np.pi / points * np.arange(points)
    cos_of, sin_of = np.cos(turn), -np.sin(turn)
    freq = lanes * np.arange(devices // 2)[:, None] + 2 * np.arange(lanes // 2)[None, :]
    phase = index[:, None, None] * freq[None] % points
    imag = sin_of[phase]
    imag[:, 0, 0] = cos_of[index * half % points]
    return np.concatenate([cos_of[phase], imag], axis=2).reshape(half, half)


def row_turn(points):
    angle = 2.0 * np.pi / points * np.arange(points // 2)
    return np.stack([np.cos(angle), np.sin(angle)] * 4).astype(np.float32)


def column_table(points):
    quarter = points // 4
    index = np.arange(quarter)
    angle = 2.0 * np.pi / quarter * (index[:, None] * index[None, :] % quarter)
    return np.concatenate([np.cos(angle), -np.sin(angle)])


def column_turn(points):
    angle = 2.0 * np.pi / points * np.arange(points // 4)[:, None] * np.arange(4)[None, :]
    made = np.zeros((points // 4, 128), np.float32)
    made[:, :4], made[:, 4:8] = np.cos(angle), np.sin(angle)
    return made


def bf16(table):
    return jnp.asarray(np.asarray(table, np.float32).astype(jnp.bfloat16))


def ones_where(condition):
    return jnp.where(condition, 1.0, 0.0).astype(BF16)


def grid(rows, lanes):
    index = lambda axis: lax.broadcasted_iota(jnp.int32, (rows, lanes), axis)
    return index(0), index(1)


def choose_kernel(me_ref, counts_ref, send_ref, edge_ref):
    points = counts_ref.shape[0]
    source, target = grid(128, 128)
    k = target % 64
    choice = ones_where(source == jnp.where(me_ref[0] < 8, 2 * k + 1, 128 - 2 * k))
    unit_row, unit_lane = grid(16, 128)
    first = ones_where((unit_row == 0) & (unit_lane == 0))
    lane = lax.broadcasted_iota(jnp.int32, (256, 128), 1)
    for b in range(points // 512):
        low = counts_ref[pl.ds(256 * b, 256)].astype(F32).astype(BF16)
        high = counts_ref[pl.ds(256 * b + points // 2, 256)].astype(F32).astype(BF16)
        got_low, got_high = dot(low, choice), dot(high, choice)
        send_ref[pl.ds(256 * b, 256)] = jnp.where(lane < 64, got_low, got_high).astype(BF16)
    edges = []
    for b in range(points // 128):
        block = counts_ref[pl.ds(128 * b, 128)].astype(F32).astype(BF16)
        edges.append(dot(first, block, NT)[:1])
    edge_ref[...] = jnp.concatenate(edges, 0).astype(BF16)


def weight_kernel(me_ref, counts_ref, got_ref, edge_ref, out_ref, plus, minus):
    points = counts_ref.shape[0]
    target, source = grid(256, 256)
    index = 4 * (target % 64) + target // 64
    direct = ones_where(source == index)
    negated = ones_where(source == 256 - index)
    row, column = grid(128, 128)
    eye = ones_where(row == column)
    me = me_ref[0]
    low, zero = me < 8, me == 0
    held, kept = grid(128, 128)
    kept = kept % 64
    choice = ones_where(held == jnp.where(low, 2 * kept, 127 - 2 * kept))
    edge = dot(eye, edge_ref[...], NT)
    lane = lax.broadcasted_iota(jnp.int32, (128, 128), 1)
    for b in range(points // 128):
        rows = pl.ds(128 * b, 128)
        own = dot(counts_ref[rows].astype(F32).astype(BF16), choice)
        packed = got_ref[pl.ds(128 * b % (points // 2), 128)].astype(F32)
        moved = pltpu.roll(packed, 64, 1)
        in_left = 128 * b < points // 2
        got = jnp.where((lane < 64) == in_left, packed, moved)
        column = jnp.broadcast_to(edge[:, b : b + 1], (128, 128))
        straight = jnp.where(low, own, got)
        mirrored = jnp.where(low, got, own)
        first = jnp.where(zero, jnp.where(lane == 0, own, column), column)
        mirrored = jnp.where(low & (lane % 64 == 0), first, mirrored)
        straight = jnp.where(zero & (lane == 64), column, straight)
        plus[rows] = straight.astype(BF16)
        minus[rows] = mirrored
    blocks = points // 256
    row = lax.broadcasted_iota(jnp.int32, (256, 128), 0)
    wide = lax.broadcasted_iota(jnp.int32, (256, 128), 1)
    scale = jnp.where(zero & (wide % 64 == 0), 0.5, 1.0)
    for b in range(blocks):
        taken = dot(direct, plus[pl.ds(256 * b, 256)])
        taken += dot(negated, minus[pl.ds(256 * (blocks - 1 - b), 256)].astype(BF16))
        wrapped = minus[pl.ds(256 * ((blocks - b) % blocks), 1)]
        taken = scale * (taken + jnp.where(row == 0, wrapped, 0.0))
        for r in range(4):
            out_ref[pl.ds(r * points // 4 + 64 * b, 64)] = taken[64 * r : 64 * r + 64].astype(BF16)


def cut_kernel(ptg_ref, image_ref, out_ref, sems):
    blocks, share, _ = out_ref.shape
    rows = image_ref.shape[0] // blocks
    copies = []
    for n in range(blocks):
        first = pl.multiple_of(rows * n + share * ptg_ref[0], share)
        copies.append(
            pltpu.make_async_copy(image_ref.at[pl.ds(first, share)], out_ref.at[n], sems.at[n])
        )
    for copy in copies:
        copy.start()
    for copy in copies:
        copy.wait()


def pick_kernel(points, place_ref, starts_ref, tiles_ref, out_ref):
    laps, parts, rows, wide = tiles_ref.shape
    lane = lax.broadcasted_iota(jnp.int32, (rows, wide), 1) + place_ref[0] * wide
    held = [[tiles_ref[lap, part].astype(F32) for part in range(parts)] for lap in range(laps)]
    for p in range(out_ref.shape[0]):
        ahead = lane - starts_ref[p]
        inside = []
        for lap in range(1, laps):
            column = ahead + lap * points
            inside.append((column >= 0) & (column < points))
        for part in range(parts):
            window = held[0][part]
            for lap in range(1, laps):
                window = jnp.where(inside[lap - 1], held[lap][part], window)
            out_ref[p, part] = window.astype(BF16)


def row_kernel(window_ref, beam_ref, table_ref, turn_ref, out_ref):
    shares, parts, _, wide = window_ref.shape
    rows = out_ref.shape[1]
    beamed = []
    for part in range(parts):
        window = jnp.concatenate([window_ref[q, part] for q in range(shares)], 0)
        beamed.append(window.astype(F32) * beam_ref[:, pl.ds(part * wide, wide)])
    left = jnp.concatenate(beamed[: parts // 2], 1)
    right = jnp.concatenate(beamed[parts // 2 :], 1)
    minus = left - right
    folded = [left + right, minus * turn_ref[0:1], minus * turn_ref[1:2]]
    folded = jnp.concatenate([t.astype(BF16) for t in folded], 0)
    last = out_ref.shape[0] - 1
    lane = lax.broadcasted_iota(jnp.int32, (rows, 128), 1)
    for part in range(table_ref.shape[1] // 256):
        got = dot(folded, table_ref[:, pl.ds(256 * part, 256)])
        for n in (0, 1):
            block = 2 * part + n
            even, by_cos, by_sin = (
                got[rows * t : rows * (t + 1), 128 * n : 128 * (n + 1)] for t in range(3)
            )
            if block == 0:
                by_cos = jnp.where(lane == 64, 0.0, by_cos)
                by_sin = jnp.where(lane == 64, 0.0, by_sin)
            moved = pltpu.roll(by_sin, 64, 1)
            out_ref[block] = even.astype(BF16)
            out_ref[last - block] = jnp.where(lane < 64, by_cos + moved, by_cos - moved).astype(BF16)


def column_kernel(me_ref, x_ref, weight_ref, table_ref, turn_ref, out_ref, both):
    points = x_ref.shape[0]
    quarter = points // 4
    scale = 1.0 / float(points * points)
    lane = lax.broadcasted_iota(jnp.int32, (256, 128), 1)
    sign = jnp.where(lane < 64, -1.0, 1.0)
    packed = (me_ref[0] == 0) & (lane % 64 == 0)
    turns = lambda r, rows: (
        jnp.broadcast_to(turn_ref[rows, r : r + 1], (256, 128)),
        jnp.broadcast_to(turn_ref[rows, 4 + r : 5 + r], (256, 128)),
    )
    for m in range(quarter // 256):
        rows = pl.ds(256 * m, 256)
        x = [x_ref[pl.ds(quarter * t + 256 * m, 256)].astype(F32) for t in range(4)]
        even, p, odd, q = x[0] + x[2], x[0] - x[2], x[1] + x[3], x[1] - x[3]
        c1, s1 = turns(1, rows)
        c2, s2 = turns(2, rows)
        c3, s3 = turns(3, rows)
        pairs = [
            (even + odd, jnp.zeros_like(even)),
            (p * c1 - q * s1, -(p * s1 + q * c1)),
            ((even - odd) * c2, -(even - odd) * s2),
            (p * c3 + q * s3, q * c3 - p * s3),
        ]
        for r in range(4):
            both[4 + r, rows, 0:128] = pairs[r][0].astype(BF16)
            both[4 + r, rows, 128:256] = pairs[r][1].astype(BF16)
    for r in range(4):
        for m in range(quarter // 256):
            rows, below = pl.ds(256 * m, 256), pl.ds(quarter + 256 * m, 256)
            wide = both[4 + r] if r else both[4, :, 0:128]
            by_c, by_s = dot(table_ref[rows], wide), dot(table_ref[below], wide)
            by_cos, by_sin = by_c[:, :128], by_s[:, :128]
            if r:
                by_cos, by_sin = by_cos - by_s[:, 128:], by_sin + by_c[:, 128:]
            weight = weight_ref[pl.ds(r * quarter + 256 * m, 256)].astype(F32) * scale
            up = weight * (by_cos + jnp.where(packed, 0.0, sign * pltpu.roll(by_sin, 64, 1)))
            down = jnp.where(packed, weight * by_sin, -sign * pltpu.roll(up, 64, 1))
            both[r, rows, 0:128] = up.astype(BF16)
            both[r, rows, 128:256] = down.astype(BF16)
    for m in range(quarter // 256):
        rows, below = pl.ds(256 * m, 256), pl.ds(quarter + 256 * m, 256)
        parts = []
        for r in range(4):
            by_c, by_s = dot(table_ref[rows], both[r]), dot(table_ref[below], both[r])
            parts.append((by_c[:, :128] + by_s[:, 128:], by_c[:, 128:] - by_s[:, :128]))
        c1, s1 = turns(1, rows)
        c2, s2 = turns(2, rows)
        c3, s3 = turns(3, rows)
        (g0, _), (g1, h1), (g2, h2), (g3, h3) = parts
        middle = c2 * g2 - s2 * h2
        p = c1 * g1 - s1 * h1 + c3 * g3 - s3 * h3
        q = s3 * g3 + c3 * h3 - s1 * g1 - c1 * h1
        plus, minus = g0 + middle, g0 - middle
        for t, value in enumerate((plus + p, minus + q, plus - p, minus - q)):
            out_ref[pl.ds(quarter * t + 256 * m, 256)] = value.astype(BF16)


def pixel_kernel(x_ref, beam_ref, table_ref, turn_ref, out_ref):
    blocks, rows, _ = x_ref.shape
    half = beam_ref.shape[1] // 2
    share = out_ref.shape[2]
    lane = lax.broadcasted_iota(jnp.int32, (rows, 128), 1)
    even = [x_ref[b] for b in range(blocks // 2)]
    straight, crossed = [], []
    for b in range(blocks // 2):
        odd = x_ref[blocks - 1 - b].astype(F32)
        moved = pltpu.roll(odd, 64, 1)
        turned = jnp.where(lane < 64, -moved, moved)
        if b == 0:
            odd = jnp.where(lane == 64, 0.0, odd)
            turned = jnp.where(lane == 64, 0.0, turned)
        straight.append(odd.astype(BF16))
        crossed.append(turned.astype(BF16))
    wide = [jnp.concatenate(part, 1) for part in (even, straight, crossed)]
    wide = jnp.concatenate(wide, 0)
    for part in range(half // share):
        lanes = pl.ds(share * part, share)
        got = dot(wide, table_ref[lanes, :], NT)
        by_even = got[:rows]
        by_odd = turn_ref[0:1, lanes] * got[rows : 2 * rows] + turn_ref[1:2, lanes] * got[2 * rows :]
        out_ref[part] = (beam_ref[:, lanes] * (by_even + by_odd)).astype(BF16)
        late = pl.ds(half + share * part, share)
        out_ref[part + half // share] = (beam_ref[:, late] * (by_even - by_odd)).astype(BF16)


def sum_kernel(points, me_ref, starts_ref, terms_ref, mine_ref, theirs_ref):
    pointings, rows, share = terms_ref.shape
    ptg, core = me_ref[0], me_ref[1]
    lane = lax.broadcasted_iota(jnp.int32, (rows, share), 1)
    for ref, side in ((mine_ref, core), (theirs_ref, 1 - core)):
        for turn in range(2):
            lap = 2 * side + jnp.where(ptg % 2 == turn, 0, 1)
            column = lane + (lap * points + ptg * share)
            total = jnp.zeros((rows, share), F32)
            for p in range(pointings):
                inside = (column >= starts_ref[p]) & (column < starts_ref[p] + points)
                total += jnp.where(inside, terms_ref[p].astype(F32), 0.0)
            ref[turn] = total.astype(BF16)


def call(kernel, outs, specs, *args, scratch=(), flops=0, moved=4 << 20, limit=16):
    return pl.pallas_call(
        kernel,
        out_shape=outs,
        in_specs=specs,
        out_specs=jax.tree.map(lambda _: VMEM, outs),
        scratch_shapes=list(scratch),
        compiler_params=pltpu.CompilerParams(vmem_limit_bytes=limit << 20),
        cost_estimate=pl.CostEstimate(flops=flops, bytes_accessed=moved, transcendentals=0),
    )(*args)


def shape(*dims, dtype=BF16):
    return jax.ShapeDtypeStruct(dims, dtype)


IMG = ("s", "b")


def shards(image, beam, counts, offsets):
    points = counts.shape[1]
    laps, parts = lax.axis_size("s"), lax.axis_size("b")
    devices = laps * parts
    pointings = lax.axis_size("ptg")
    rows = points // devices
    tile = image.shape[1]
    me = lax.axis_index(IMG).astype(jnp.int32)
    ptg = lax.axis_index("ptg").astype(jnp.int32)
    start = offsets[0]
    place = me.reshape(1)

    starts = jnp.where(jnp.arange(pointings) == ptg, start, 0)
    share_rows = rows // pointings
    shares = call(
        cut_kernel,
        shape(devices, share_rows, tile),
        [SMEM, pl.BlockSpec(memory_space=pl.ANY)],
        ptg.reshape(1),
        image,
        scratch=[pltpu.SemaphoreType.DMA((devices,))],
        moved=1 << 19,
        limit=60,
    ).reshape(laps, parts, share_rows, tile)
    send, edge = call(
        choose_kernel,
        (shape(points // 2, 128), shape(points // 128, 128)),
        [SMEM, VMEM],
        place,
        counts[0],
        flops=points * 128 * 512,
    )
    shares, send = lax.optimization_barrier((shares, send))
    shares = lax.all_to_all(shares, "s", split_axis=0, concat_axis=0, tiled=True)
    near = [
        lax.ppermute(starts, "ptg", [(p, p ^ bit) for p in range(pointings)]) for bit in (1, 2, 3)
    ]
    starts = starts + near[0] + near[1] + near[2]
    starts = starts + lax.ppermute(starts, "ptg", [(p, p ^ 4) for p in range(pointings)])
    got = lax.ppermute(send, IMG, [(i, devices - 1 - i) for i in range(devices)])
    edge = lax.ppermute(
        edge,
        IMG,
        [(i, (devices - i) % (devices // 2)) for i in range(devices // 2, devices)],
    )
    weight = call(
        weight_kernel,
        shape(points, 128),
        [SMEM] + [VMEM] * 3,
        place,
        counts[0],
        got,
        edge,
        scratch=[pltpu.VMEM((points, 128), BF16), pltpu.VMEM((points, 128), F32)],
        flops=points * 128 * 1024,
    )

    twice = jnp.concatenate([beam[0], beam[0]], 1)
    turned = lax.dynamic_slice_in_dim(twice, (points - start % points) % points, points, 1)
    shares, got = lax.optimization_barrier((shares, got))
    picked = call(
        functools.partial(pick_kernel, points),
        shape(pointings, parts, share_rows, tile),
        [SMEM, SMEM, VMEM],
        lax.axis_index("b").astype(jnp.int32).reshape(1),
        starts,
        shares,
        moved=1 << 20,
    )
    window = lax.all_to_all(
        picked.reshape(pointings * parts, share_rows, tile),
        ("ptg", "b"),
        split_axis=0,
        concat_axis=0,
        tiled=True,
    ).reshape(pointings, parts, share_rows, tile)
    seat = jnp.stack([ptg, me % 2])
    window, weight, turned, seat, starts = lax.optimization_barrier(
        (window, weight, turned, seat, starts)
    )
    across, turn = bf16(row_table(points, devices)), jnp.asarray(row_turn(points))
    spectrum = call(
        row_kernel,
        shape(devices, rows, 128),
        [VMEM] * 4,
        window,
        turned,
        across,
        turn,
        flops=rows * points * points,
    )
    col = lax.all_to_all(spectrum, IMG, split_axis=0, concat_axis=0, tiled=True)
    back = call(
        column_kernel,
        shape(points, 128),
        [SMEM] + [VMEM] * 4,
        place,
        col.reshape(points, 128),
        weight,
        bf16(column_table(points)),
        jnp.asarray(column_turn(points)),
        scratch=[pltpu.VMEM((8, points // 4, 256), BF16)],
        flops=4 * points * points * 128,
    )
    lines = lax.all_to_all(
        back.reshape(devices, rows, 128), IMG, split_axis=0, concat_axis=0, tiled=True
    )
    share = points // pointings
    contribution = call(
        pixel_kernel,
        shape(pointings, rows, share),
        [VMEM] * 4,
        lines,
        turned,
        across,
        turn,
        flops=rows * points * points,
    )
    terms = lax.all_to_all(contribution, "ptg", split_axis=0, concat_axis=0, tiled=True)
    mine, theirs = call(
        functools.partial(sum_kernel, points),
        (shape(2, rows, share), shape(2, rows, share)),
        [SMEM, SMEM, VMEM],
        seat,
        starts,
        terms,
        moved=1 << 20,
    )
    other = lax.ppermute(theirs, IMG, [(i, i ^ 1) for i in range(devices)])
    per_lap = parts
    halves = tile // share
    received = []
    for turn in range(2):
        pairs = []
        for q in range(pointings):
            for i in range(devices):
                lap = 2 * (i % 2) + (turn ^ (q % 2))
                pairs.append((q * devices + i, (i // 2) * devices + per_lap * lap + q // halves))
        block = jnp.concatenate([mine[turn], other[turn]], 0)
        received.append(lax.ppermute(block, ("ptg", *IMG), pairs))
    lap = me // per_lap
    out = jnp.where(
        lap % 2 == 1,
        jnp.concatenate([received[1], received[0]], 1),
        jnp.concatenate([received[0], received[1]], 1),
    ).astype(F32)
    flipped = jnp.concatenate([out[rows:], out[:rows]], 0)
    return jnp.where(lap >= 2, flipped, out)


def solution(mesh):
    pointings, devices = mesh.devices.shape
    split = Mesh(mesh.devices.reshape(pointings, 4, devices // 4), ("ptg", *IMG))
    return jax.shard_map(
        shards,
        mesh=split,
        in_specs=(P(None, IMG), P("ptg", IMG, None), P("ptg", None, IMG), P("ptg")),
        out_specs=P("ptg", IMG),
        check_vma=False,
    )
```

```python
import functools

import numpy as np

import jax
import jax.numpy as jnp
from jax import lax
from jax.experimental import pallas as pl
from jax.experimental.pallas import tpu as pltpu
from jax.sharding import Mesh, PartitionSpec as P

F32, BF16 = jnp.float32, jnp.bfloat16
NT = (((1,), (1,)), ((), ()))
NN = (((1,), (0,)), ((), ()))
VMEM = pl.BlockSpec(memory_space=pltpu.VMEM)
SMEM = pl.BlockSpec(memory_space=pltpu.SMEM)


def dot(a, b, dims=NN):
    return lax.dot_general(a, b, dims, preferred_element_type=F32)


def row_table(points, devices):
    half, lanes = points // 2, points // devices
    index = np.arange(half)
    turn = 2.0 * np.pi / points * np.arange(points)
    cos_of, sin_of = np.cos(turn), -np.sin(turn)
    freq = lanes * np.arange(devices // 2)[:, None] + 2 * np.arange(lanes // 2)[None, :]
    phase = index[:, None, None] * freq[None] % points
    imag = sin_of[phase]
    imag[:, 0, 0] = cos_of[index * half % points]
    return np.concatenate([cos_of[phase], imag], axis=2).reshape(half, half)


def row_turn(points):
    angle = 2.0 * np.pi / points * np.arange(points // 2)
    return np.stack([np.cos(angle), np.sin(angle)] * 4).astype(np.float32)


def column_table(points):
    quarter = points // 4
    index = np.arange(quarter)
    angle = 2.0 * np.pi / quarter * (index[:, None] * index[None, :] % quarter)
    return np.concatenate([np.cos(angle), -np.sin(angle)])


def column_turn(points):
    angle = 2.0 * np.pi / points * np.arange(points // 4)[:, None] * np.arange(4)[None, :]
    made = np.zeros((points // 4, 128), np.float32)
    made[:, :4], made[:, 4:8] = np.cos(angle), np.sin(angle)
    return made


def bf16(table):
    return jnp.asarray(np.asarray(table, np.float32).astype(jnp.bfloat16))


def ones_where(condition):
    return jnp.where(condition, 1.0, 0.0).astype(BF16)


def grid(rows, lanes):
    index = lambda axis: lax.broadcasted_iota(jnp.int32, (rows, lanes), axis)
    return index(0), index(1)


def choose_kernel(me_ref, counts_ref, send_ref, edge_ref):
    points = counts_ref.shape[0]
    source, target = grid(128, 128)
    k = target % 64
    choice = ones_where(source == jnp.where(me_ref[0] < 8, 2 * k + 1, 128 - 2 * k))
    unit_row, unit_lane = grid(16, 128)
    first = ones_where((unit_row == 0) & (unit_lane == 0))
    lane = lax.broadcasted_iota(jnp.int32, (256, 128), 1)
    for b in range(points // 512):
        low = counts_ref[pl.ds(256 * b, 256)].astype(F32).astype(BF16)
        high = counts_ref[pl.ds(256 * b + points // 2, 256)].astype(F32).astype(BF16)
        got_low, got_high = dot(low, choice), dot(high, choice)
        send_ref[pl.ds(256 * b, 256)] = jnp.where(lane < 64, got_low, got_high).astype(BF16)
    edges = []
    for b in range(points // 128):
        block = counts_ref[pl.ds(128 * b, 128)].astype(F32).astype(BF16)
        edges.append(dot(first, block, NT)[:1])
    edge_ref[...] = jnp.concatenate(edges, 0).astype(BF16)


def weight_kernel(me_ref, counts_ref, got_ref, edge_ref, out_ref, plus, minus):
    points = counts_ref.shape[0]
    target, source = grid(256, 256)
    index = 4 * (target % 64) + target // 64
    direct = ones_where(source == index)
    negated = ones_where(source == 256 - index)
    row, column = grid(128, 128)
    eye = ones_where(row == column)
    me = me_ref[0]
    low, zero = me < 8, me == 0
    held, kept = grid(128, 128)
    kept = kept % 64
    choice = ones_where(held == jnp.where(low, 2 * kept, 127 - 2 * kept))
    edge = dot(eye, edge_ref[...], NT)
    lane = lax.broadcasted_iota(jnp.int32, (128, 128), 1)
    for b in range(points // 128):
        rows = pl.ds(128 * b, 128)
        own = dot(counts_ref[rows].astype(F32).astype(BF16), choice)
        packed = got_ref[pl.ds(128 * b % (points // 2), 128)].astype(F32)
        moved = pltpu.roll(packed, 64, 1)
        in_left = 128 * b < points // 2
        got = jnp.where((lane < 64) == in_left, packed, moved)
        column = jnp.broadcast_to(edge[:, b : b + 1], (128, 128))
        straight = jnp.where(low, own, got)
        mirrored = jnp.where(low, got, own)
        first = jnp.where(zero, jnp.where(lane == 0, own, column), column)
        mirrored = jnp.where(low & (lane % 64 == 0), first, mirrored)
        straight = jnp.where(zero & (lane == 64), column, straight)
        plus[rows] = straight.astype(BF16)
        minus[rows] = mirrored
    blocks = points // 256
    row = lax.broadcasted_iota(jnp.int32, (256, 128), 0)
    wide = lax.broadcasted_iota(jnp.int32, (256, 128), 1)
    scale = jnp.where(zero & (wide % 64 == 0), 0.5, 1.0)
    for b in range(blocks):
        taken = dot(direct, plus[pl.ds(256 * b, 256)])
        taken += dot(negated, minus[pl.ds(256 * (blocks - 1 - b), 256)].astype(BF16))
        wrapped = minus[pl.ds(256 * ((blocks - b) % blocks), 1)]
        taken = scale * (taken + jnp.where(row == 0, wrapped, 0.0))
        for r in range(4):
            out_ref[pl.ds(r * points // 4 + 64 * b, 64)] = taken[64 * r : 64 * r + 64].astype(BF16)


def cut_kernel(ptg_ref, image_ref, out_ref, sems):
    blocks, share, _ = out_ref.shape
    rows = image_ref.shape[0] // blocks
    copies = []
    for n in range(blocks):
        first = pl.multiple_of(rows * n + share * ptg_ref[0], share)
        copies.append(
            pltpu.make_async_copy(image_ref.at[pl.ds(first, share)], out_ref.at[n], sems.at[n])
        )
    for copy in copies:
        copy.start()
    for copy in copies:
        copy.wait()


def pick_kernel(points, place_ref, starts_ref, tiles_ref, out_ref):
    laps, parts, rows, wide = tiles_ref.shape
    lane = lax.broadcasted_iota(jnp.int32, (rows, wide), 1) + place_ref[0] * wide
    held = [[tiles_ref[lap, part].astype(F32) for part in range(parts)] for lap in range(laps)]
    for p in range(out_ref.shape[0]):
        ahead = lane - starts_ref[p]
        inside = []
        for lap in range(1, laps):
            column = ahead + lap * points
            inside.append((column >= 0) & (column < points))
        for part in range(parts):
            window = held[0][part]
            for lap in range(1, laps):
                window = jnp.where(inside[lap - 1], held[lap][part], window)
            out_ref[p, part] = window.astype(BF16)


def row_kernel(window_ref, beam_ref, table_ref, turn_ref, out_ref):
    shares, parts, _, wide = window_ref.shape
    rows = out_ref.shape[1]
    beamed = []
    for part in range(parts):
        window = jnp.concatenate([window_ref[q, part] for q in range(shares)], 0)
        beamed.append(window.astype(F32) * beam_ref[:, pl.ds(part * wide, wide)])
    left = jnp.concatenate(beamed[: parts // 2], 1)
    right = jnp.concatenate(beamed[parts // 2 :], 1)
    minus = left - right
    folded = [left + right, minus * turn_ref[0:1], minus * turn_ref[1:2]]
    folded = jnp.concatenate([t.astype(BF16) for t in folded], 0)
    last = out_ref.shape[0] - 1
    lane = lax.broadcasted_iota(jnp.int32, (rows, 128), 1)
    for part in range(table_ref.shape[1] // 256):
        got = dot(folded, table_ref[:, pl.ds(256 * part, 256)])
        for n in (0, 1):
            block = 2 * part + n
            even, by_cos, by_sin = (
                got[rows * t : rows * (t + 1), 128 * n : 128 * (n + 1)] for t in range(3)
            )
            if block == 0:
                by_cos = jnp.where(lane == 64, 0.0, by_cos)
                by_sin = jnp.where(lane == 64, 0.0, by_sin)
            moved = pltpu.roll(by_sin, 64, 1)
            out_ref[block] = even.astype(BF16)
            out_ref[last - block] = jnp.where(lane < 64, by_cos + moved, by_cos - moved).astype(BF16)


def column_kernel(me_ref, x_ref, weight_ref, table_ref, turn_ref, out_ref, both):
    points = x_ref.shape[0]
    quarter = points // 4
    scale = 1.0 / float(points * points)
    lane = lax.broadcasted_iota(jnp.int32, (256, 128), 1)
    sign = jnp.where(lane < 64, -1.0, 1.0)
    packed = (me_ref[0] == 0) & (lane % 64 == 0)
    turns = lambda r, rows: (
        jnp.broadcast_to(turn_ref[rows, r : r + 1], (256, 128)),
        jnp.broadcast_to(turn_ref[rows, 4 + r : 5 + r], (256, 128)),
    )
    for m in range(quarter // 256):
        rows = pl.ds(256 * m, 256)
        x = [x_ref[pl.ds(quarter * t + 256 * m, 256)].astype(F32) for t in range(4)]
        even, p, odd, q = x[0] + x[2], x[0] - x[2], x[1] + x[3], x[1] - x[3]
        c1, s1 = turns(1, rows)
        c2, s2 = turns(2, rows)
        c3, s3 = turns(3, rows)
        pairs = [
            (even + odd, jnp.zeros_like(even)),
            (p * c1 - q * s1, -(p * s1 + q * c1)),
            ((even - odd) * c2, -(even - odd) * s2),
            (p * c3 + q * s3, q * c3 - p * s3),
        ]
        for r in range(4):
            both[4 + r, rows, 0:128] = pairs[r][0].astype(BF16)
            both[4 + r, rows, 128:256] = pairs[r][1].astype(BF16)
    for r in range(4):
        for m in range(quarter // 256):
            rows, below = pl.ds(256 * m, 256), pl.ds(quarter + 256 * m, 256)
            wide = both[4 + r] if r else both[4, :, 0:128]
            by_c, by_s = dot(table_ref[rows], wide), dot(table_ref[below], wide)
            by_cos, by_sin = by_c[:, :128], by_s[:, :128]
            if r:
                by_cos, by_sin = by_cos - by_s[:, 128:], by_sin + by_c[:, 128:]
            weight = weight_ref[pl.ds(r * quarter + 256 * m, 256)].astype(F32) * scale
            up = weight * (by_cos + jnp.where(packed, 0.0, sign * pltpu.roll(by_sin, 64, 1)))
            down = jnp.where(packed, weight * by_sin, -sign * pltpu.roll(up, 64, 1))
            both[r, rows, 0:128] = up.astype(BF16)
            both[r, rows, 128:256] = down.astype(BF16)
    for m in range(quarter // 256):
        rows, below = pl.ds(256 * m, 256), pl.ds(quarter + 256 * m, 256)
        parts = []
        for r in range(4):
            by_c, by_s = dot(table_ref[rows], both[r]), dot(table_ref[below], both[r])
            parts.append((by_c[:, :128] + by_s[:, 128:], by_c[:, 128:] - by_s[:, :128]))
        c1, s1 = turns(1, rows)
        c2, s2 = turns(2, rows)
        c3, s3 = turns(3, rows)
        (g0, _), (g1, h1), (g2, h2), (g3, h3) = parts
        middle = c2 * g2 - s2 * h2
        p = c1 * g1 - s1 * h1 + c3 * g3 - s3 * h3
        q = s3 * g3 + c3 * h3 - s1 * g1 - c1 * h1
        plus, minus = g0 + middle, g0 - middle
        for t, value in enumerate((plus + p, minus + q, plus - p, minus - q)):
            out_ref[pl.ds(quarter * t + 256 * m, 256)] = value.astype(BF16)


def pixel_kernel(x_ref, beam_ref, table_ref, turn_ref, out_ref):
    blocks, rows, _ = x_ref.shape
    half = beam_ref.shape[1] // 2
    share = out_ref.shape[2]
    lane = lax.broadcasted_iota(jnp.int32, (rows, 128), 1)
    even = [x_ref[b] for b in range(blocks // 2)]
    straight, crossed = [], []
    for b in range(blocks // 2):
        odd = x_ref[blocks - 1 - b].astype(F32)
        moved = pltpu.roll(odd, 64, 1)
        turned = jnp.where(lane < 64, -moved, moved)
        if b == 0:
            odd = jnp.where(lane == 64, 0.0, odd)
            turned = jnp.where(lane == 64, 0.0, turned)
        straight.append(odd.astype(BF16))
        crossed.append(turned.astype(BF16))
    wide = [jnp.concatenate(part, 1) for part in (even, straight, crossed)]
    wide = jnp.concatenate(wide, 0)
    for part in range(half // share):
        lanes = pl.ds(share * part, share)
        got = dot(wide, table_ref[lanes, :], NT)
        by_even = got[:rows]
        by_odd = turn_ref[0:1, lanes] * got[rows : 2 * rows] + turn_ref[1:2, lanes] * got[2 * rows :]
        out_ref[part] = (beam_ref[:, lanes] * (by_even + by_odd)).astype(BF16)
        late = pl.ds(half + share * part, share)
        out_ref[part + half // share] = (beam_ref[:, late] * (by_even - by_odd)).astype(BF16)


def sum_kernel(points, me_ref, starts_ref, terms_ref, mine_ref, theirs_ref):
    pointings, rows, share = terms_ref.shape
    ptg, core = me_ref[0], me_ref[1]
    lane = lax.broadcasted_iota(jnp.int32, (rows, share), 1)
    for ref, side in ((mine_ref, core), (theirs_ref, 1 - core)):
        for turn in range(2):
            lap = 2 * side + jnp.where(ptg % 2 == turn, 0, 1)
            column = lane + (lap * points + ptg * share)
            total = jnp.zeros((rows, share), F32)
            for p in range(pointings):
                inside = (column >= starts_ref[p]) & (column < starts_ref[p] + points)
                total += jnp.where(inside, terms_ref[p].astype(F32), 0.0)
            ref[turn] = total.astype(BF16)


def call(kernel, outs, specs, *args, scratch=(), flops=0, moved=4 << 20, limit=16):
    return pl.pallas_call(
        kernel,
        out_shape=outs,
        in_specs=specs,
        out_specs=jax.tree.map(lambda _: VMEM, outs),
        scratch_shapes=list(scratch),
        compiler_params=pltpu.CompilerParams(vmem_limit_bytes=limit << 20),
        cost_estimate=pl.CostEstimate(flops=flops, bytes_accessed=moved, transcendentals=0),
    )(*args)


def shape(*dims, dtype=BF16):
    return jax.ShapeDtypeStruct(dims, dtype)


IMG = ("s", "b")


def shards(image, beam, counts, offsets):
    points = counts.shape[1]
    laps, parts = lax.axis_size("s"), lax.axis_size("b")
    devices = laps * parts
    pointings = lax.axis_size("ptg")
    rows = points // devices
    tile = image.shape[1]
    me = lax.axis_index(IMG).astype(jnp.int32)
    ptg = lax.axis_index("ptg").astype(jnp.int32)
    start = offsets[0]
    place = me.reshape(1)

    starts = jnp.where(jnp.arange(pointings) == ptg, start, 0)
    share_rows = rows // pointings
    shares = call(
        cut_kernel,
        shape(devices, share_rows, tile),
        [SMEM, pl.BlockSpec(memory_space=pl.ANY)],
        ptg.reshape(1),
        image,
        scratch=[pltpu.SemaphoreType.DMA((devices,))],
        moved=1 << 19,
        limit=60,
    ).reshape(laps, parts, share_rows, tile)
    send, edge = call(
        choose_kernel,
        (shape(points // 2, 128), shape(points // 128, 128)),
        [SMEM, VMEM],
        place,
        counts[0],
        flops=points * 128 * 512,
    )
    shares, send = lax.optimization_barrier((shares, send))
    shares = lax.all_to_all(shares, "s", split_axis=0, concat_axis=0, tiled=True)
    near = [
        lax.ppermute(starts, "ptg", [(p, p ^ bit) for p in range(pointings)]) for bit in (1, 2, 3)
    ]
    starts = starts + near[0] + near[1] + near[2]
    starts = starts + lax.ppermute(starts, "ptg", [(p, p ^ 4) for p in range(pointings)])
    got = lax.ppermute(send, IMG, [(i, devices - 1 - i) for i in range(devices)])
    edge = lax.ppermute(
        edge,
        IMG,
        [(i, (devices - i) % (devices // 2)) for i in range(devices // 2, devices)],
    )
    weight = call(
        weight_kernel,
        shape(points, 128),
        [SMEM] + [VMEM] * 3,
        place,
        counts[0],
        got,
        edge,
        scratch=[pltpu.VMEM((points, 128), BF16), pltpu.VMEM((points, 128), F32)],
        flops=points * 128 * 1024,
    )

    twice = jnp.concatenate([beam[0], beam[0]], 1)
    turned = lax.dynamic_slice_in_dim(twice, (points - start % points) % points, points, 1)
    shares, got, edge = lax.optimization_barrier((shares, got, edge))
    picked = call(
        functools.partial(pick_kernel, points),
        shape(pointings, parts, share_rows, tile),
        [SMEM, SMEM, VMEM],
        lax.axis_index("b").astype(jnp.int32).reshape(1),
        starts,
        shares,
        moved=1 << 20,
    )
    window = lax.all_to_all(
        picked.reshape(pointings * parts, share_rows, tile),
        ("ptg", "b"),
        split_axis=0,
        concat_axis=0,
        tiled=True,
    ).reshape(pointings, parts, share_rows, tile)
    seat = jnp.stack([ptg, me % 2])
    window, weight, turned, seat, starts = lax.optimization_barrier(
        (window, weight, turned, seat, starts)
    )
    across, turn = bf16(row_table(points, devices)), jnp.asarray(row_turn(points))
    spectrum = call(
        row_kernel,
        shape(devices, rows, 128),
        [VMEM] * 4,
        window,
        turned,
        across,
        turn,
        flops=rows * points * points,
    )
    col = lax.all_to_all(spectrum, IMG, split_axis=0, concat_axis=0, tiled=True)
    back = call(
        column_kernel,
        shape(points, 128),
        [SMEM] + [VMEM] * 4,
        place,
        col.reshape(points, 128),
        weight,
        bf16(column_table(points)),
        jnp.asarray(column_turn(points)),
        scratch=[pltpu.VMEM((8, points // 4, 256), BF16)],
        flops=4 * points * points * 128,
    )
    lines = lax.all_to_all(
        back.reshape(devices, rows, 128), IMG, split_axis=0, concat_axis=0, tiled=True
    )
    share = points // pointings
    contribution = call(
        pixel_kernel,
        shape(pointings, rows, share),
        [VMEM] * 4,
        lines,
        turned,
        across,
        turn,
        flops=rows * points * points,
    )
    terms = lax.all_to_all(contribution, "ptg", split_axis=0, concat_axis=0, tiled=True)
    mine, theirs = call(
        functools.partial(sum_kernel, points),
        (shape(2, rows, share), shape(2, rows, share)),
        [SMEM, SMEM, VMEM],
        seat,
        starts,
        terms,
        moved=1 << 20,
    )
    other = lax.ppermute(theirs, IMG, [(i, i ^ 1) for i in range(devices)])
    per_lap = parts
    halves = tile // share
    received = []
    for turn in range(2):
        pairs = []
        for q in range(pointings):
            for i in range(devices):
                lap = 2 * (i % 2) + (turn ^ (q % 2))
                pairs.append((q * devices + i, (i // 2) * devices + per_lap * lap + q // halves))
        block = jnp.concatenate([mine[turn], other[turn]], 0)
        received.append(lax.ppermute(block, ("ptg", *IMG), pairs))
    lap = me // per_lap
    out = jnp.where(
        lap % 2 == 1,
        jnp.concatenate([received[1], received[0]], 1),
        jnp.concatenate([received[0], received[1]], 1),
    ).astype(F32)
    flipped = jnp.concatenate([out[rows:], out[:rows]], 0)
    return jnp.where(lap >= 2, flipped, out)


def solution(mesh):
    pointings, devices = mesh.devices.shape
    split = Mesh(mesh.devices.reshape(pointings, 4, devices // 4), ("ptg", *IMG))
    return jax.shard_map(
        shards,
        mesh=split,
        in_specs=(P(None, IMG), P("ptg", IMG, None), P("ptg", None, IMG), P("ptg")),
        out_specs=P("ptg", IMG),
        check_vma=False,
    )
```

```python
import functools

import numpy as np

import jax
import jax.numpy as jnp
from jax import lax
from jax.experimental import pallas as pl
from jax.experimental.pallas import tpu as pltpu
from jax.sharding import Mesh, PartitionSpec as P

F32, BF16 = jnp.float32, jnp.bfloat16
NT = (((1,), (1,)), ((), ()))
NN = (((1,), (0,)), ((), ()))
VMEM = pl.BlockSpec(memory_space=pltpu.VMEM)
SMEM = pl.BlockSpec(memory_space=pltpu.SMEM)


def dot(a, b, dims=NN):
    return lax.dot_general(a, b, dims, preferred_element_type=F32)


def row_table(points, devices):
    half, lanes = points // 2, points // devices
    index = np.arange(half)
    turn = 2.0 * np.pi / points * np.arange(points)
    cos_of, sin_of = np.cos(turn), -np.sin(turn)
    freq = lanes * np.arange(devices // 2)[:, None] + 2 * np.arange(lanes // 2)[None, :]
    phase = index[:, None, None] * freq[None] % points
    imag = sin_of[phase]
    imag[:, 0, 0] = cos_of[index * half % points]
    return np.concatenate([cos_of[phase], imag], axis=2).reshape(half, half)


def row_turn(points):
    angle = 2.0 * np.pi / points * np.arange(points // 2)
    return np.stack([np.cos(angle), np.sin(angle)] * 4).astype(np.float32)


def column_table(points):
    quarter = points // 4
    index = np.arange(quarter)
    angle = 2.0 * np.pi / quarter * (index[:, None] * index[None, :] % quarter)
    return np.concatenate([np.cos(angle), -np.sin(angle)])


def column_turn(points):
    angle = 2.0 * np.pi / points * np.arange(points // 4)[:, None] * np.arange(4)[None, :]
    made = np.zeros((points // 4, 128), np.float32)
    made[:, :4], made[:, 4:8] = np.cos(angle), np.sin(angle)
    return made


def bf16(table):
    return jnp.asarray(np.asarray(table, np.float32).astype(jnp.bfloat16))


def ones_where(condition):
    return jnp.where(condition, 1.0, 0.0).astype(BF16)


def grid(rows, lanes):
    index = lambda axis: lax.broadcasted_iota(jnp.int32, (rows, lanes), axis)
    return index(0), index(1)


def choose_kernel(me_ref, counts_ref, send_ref, edge_ref):
    points = counts_ref.shape[0]
    source, target = grid(128, 128)
    k = target % 64
    choice = ones_where(source == jnp.where(me_ref[0] < 8, 2 * k + 1, 128 - 2 * k))
    unit_row, unit_lane = grid(16, 128)
    first = ones_where((unit_row == 0) & (unit_lane == 0))
    lane = lax.broadcasted_iota(jnp.int32, (256, 128), 1)
    for b in range(points // 512):
        low = counts_ref[pl.ds(256 * b, 256)].astype(F32).astype(BF16)
        high = counts_ref[pl.ds(256 * b + points // 2, 256)].astype(F32).astype(BF16)
        got_low, got_high = dot(low, choice), dot(high, choice)
        send_ref[pl.ds(256 * b, 256)] = jnp.where(lane < 64, got_low, got_high).astype(BF16)
    edges = []
    for b in range(points // 128):
        block = counts_ref[pl.ds(128 * b, 128)].astype(F32).astype(BF16)
        edges.append(dot(first, block, NT)[:1])
    edge_ref[...] = jnp.concatenate(edges, 0).astype(BF16)


def weight_kernel(me_ref, counts_ref, got_ref, edge_ref, out_ref, plus, minus):
    points = counts_ref.shape[0]
    target, source = grid(256, 256)
    index = 4 * (target % 64) + target // 64
    direct = ones_where(source == index)
    negated = ones_where(source == 256 - index)
    row, column = grid(128, 128)
    eye = ones_where(row == column)
    me = me_ref[0]
    low, zero = me < 8, me == 0
    held, kept = grid(128, 128)
    kept = kept % 64
    choice = ones_where(held == jnp.where(low, 2 * kept, 127 - 2 * kept))
    edge = dot(eye, edge_ref[...], NT)
    lane = lax.broadcasted_iota(jnp.int32, (128, 128), 1)
    for b in range(points // 128):
        rows = pl.ds(128 * b, 128)
        own = dot(counts_ref[rows].astype(F32).astype(BF16), choice)
        packed = got_ref[pl.ds(128 * b % (points // 2), 128)].astype(F32)
        moved = pltpu.roll(packed, 64, 1)
        in_left = 128 * b < points // 2
        got = jnp.where((lane < 64) == in_left, packed, moved)
        column = jnp.broadcast_to(edge[:, b : b + 1], (128, 128))
        straight = jnp.where(low, own, got)
        mirrored = jnp.where(low, got, own)
        first = jnp.where(zero, jnp.where(lane == 0, own, column), column)
        mirrored = jnp.where(low & (lane % 64 == 0), first, mirrored)
        straight = jnp.where(zero & (lane == 64), column, straight)
        plus[rows] = straight.astype(BF16)
        minus[rows] = mirrored
    blocks = points // 256
    row = lax.broadcasted_iota(jnp.int32, (256, 128), 0)
    wide = lax.broadcasted_iota(jnp.int32, (256, 128), 1)
    scale = jnp.where(zero & (wide % 64 == 0), 0.5, 1.0)
    for b in range(blocks):
        taken = dot(direct, plus[pl.ds(256 * b, 256)])
        taken += dot(negated, minus[pl.ds(256 * (blocks - 1 - b), 256)].astype(BF16))
        wrapped = minus[pl.ds(256 * ((blocks - b) % blocks), 1)]
        taken = scale * (taken + jnp.where(row == 0, wrapped, 0.0))
        for r in range(4):
            out_ref[pl.ds(r * points // 4 + 64 * b, 64)] = taken[64 * r : 64 * r + 64].astype(BF16)


def cut_kernel(ptg_ref, image_ref, out_ref, sems):
    blocks, share, _ = out_ref.shape
    rows = image_ref.shape[0] // blocks
    copies = []
    for n in range(blocks):
        first = pl.multiple_of(rows * n + share * ptg_ref[0], share)
        copies.append(
            pltpu.make_async_copy(image_ref.at[pl.ds(first, share)], out_ref.at[n], sems.at[n])
        )
    for copy in copies:
        copy.start()
    for copy in copies:
        copy.wait()


def pick_kernel(points, place_ref, starts_ref, tiles_ref, out_ref):
    laps, parts, rows, wide = tiles_ref.shape
    lane = lax.broadcasted_iota(jnp.int32, (rows, wide), 1) + place_ref[0] * wide
    held = [[tiles_ref[lap, part].astype(F32) for part in range(parts)] for lap in range(laps)]
    for p in range(out_ref.shape[0]):
        ahead = lane - starts_ref[p]
        inside = []
        for lap in range(1, laps):
            column = ahead + lap * points
            inside.append((column >= 0) & (column < points))
        for part in range(parts):
            window = held[0][part]
            for lap in range(1, laps):
                window = jnp.where(inside[lap - 1], held[lap][part], window)
            out_ref[p, part] = window.astype(BF16)


def row_kernel(window_ref, beam_ref, table_ref, turn_ref, out_ref):
    shares, parts, _, wide = window_ref.shape
    rows = out_ref.shape[1]
    beamed = []
    for part in range(parts):
        window = jnp.concatenate([window_ref[q, part] for q in range(shares)], 0)
        beamed.append(window.astype(F32) * beam_ref[:, pl.ds(part * wide, wide)])
    left = jnp.concatenate(beamed[: parts // 2], 1)
    right = jnp.concatenate(beamed[parts // 2 :], 1)
    minus = left - right
    folded = [left + right, minus * turn_ref[0:1], minus * turn_ref[1:2]]
    folded = jnp.concatenate([t.astype(BF16) for t in folded], 0)
    last = out_ref.shape[0] - 1
    lane = lax.broadcasted_iota(jnp.int32, (rows, 128), 1)
    for part in range(table_ref.shape[1] // 256):
        got = dot(folded, table_ref[:, pl.ds(256 * part, 256)])
        for n in (0, 1):
            block = 2 * part + n
            even, by_cos, by_sin = (
                got[rows * t : rows * (t + 1), 128 * n : 128 * (n + 1)] for t in range(3)
            )
            if block == 0:
                by_cos = jnp.where(lane == 64, 0.0, by_cos)
                by_sin = jnp.where(lane == 64, 0.0, by_sin)
            moved = pltpu.roll(by_sin, 64, 1)
            out_ref[block] = even.astype(BF16)
            out_ref[last - block] = jnp.where(lane < 64, by_cos + moved, by_cos - moved).astype(BF16)


def column_kernel(me_ref, x_ref, weight_ref, table_ref, turn_ref, out_ref, both):
    points = x_ref.shape[0]
    quarter = points // 4
    scale = 1.0 / float(points * points)
    lane = lax.broadcasted_iota(jnp.int32, (256, 128), 1)
    sign = jnp.where(lane < 64, -1.0, 1.0)
    packed = (me_ref[0] == 0) & (lane % 64 == 0)
    turns = lambda r, rows: (
        jnp.broadcast_to(turn_ref[rows, r : r + 1], (256, 128)),
        jnp.broadcast_to(turn_ref[rows, 4 + r : 5 + r], (256, 128)),
    )
    for m in range(quarter // 256):
        rows = pl.ds(256 * m, 256)
        x = [x_ref[pl.ds(quarter * t + 256 * m, 256)].astype(F32) for t in range(4)]
        even, p, odd, q = x[0] + x[2], x[0] - x[2], x[1] + x[3], x[1] - x[3]
        c1, s1 = turns(1, rows)
        c2, s2 = turns(2, rows)
        c3, s3 = turns(3, rows)
        pairs = [
            (even + odd, jnp.zeros_like(even)),
            (p * c1 - q * s1, -(p * s1 + q * c1)),
            ((even - odd) * c2, -(even - odd) * s2),
            (p * c3 + q * s3, q * c3 - p * s3),
        ]
        for r in range(4):
            both[4 + r, rows, 0:128] = pairs[r][0].astype(BF16)
            both[4 + r, rows, 128:256] = pairs[r][1].astype(BF16)
    for r in range(4):
        for m in range(quarter // 256):
            rows, below = pl.ds(256 * m, 256), pl.ds(quarter + 256 * m, 256)
            wide = both[4 + r] if r else both[4, :, 0:128]
            by_c, by_s = dot(table_ref[rows], wide), dot(table_ref[below], wide)
            by_cos, by_sin = by_c[:, :128], by_s[:, :128]
            if r:
                by_cos, by_sin = by_cos - by_s[:, 128:], by_sin + by_c[:, 128:]
            weight = weight_ref[pl.ds(r * quarter + 256 * m, 256)].astype(F32) * scale
            up = weight * (by_cos + jnp.where(packed, 0.0, sign * pltpu.roll(by_sin, 64, 1)))
            down = jnp.where(packed, weight * by_sin, -sign * pltpu.roll(up, 64, 1))
            both[r, rows, 0:128] = up.astype(BF16)
            both[r, rows, 128:256] = down.astype(BF16)
    for m in range(quarter // 256):
        rows, below = pl.ds(256 * m, 256), pl.ds(quarter + 256 * m, 256)
        parts = []
        for r in range(4):
            by_c, by_s = dot(table_ref[rows], both[r]), dot(table_ref[below], both[r])
            parts.append((by_c[:, :128] + by_s[:, 128:], by_c[:, 128:] - by_s[:, :128]))
        c1, s1 = turns(1, rows)
        c2, s2 = turns(2, rows)
        c3, s3 = turns(3, rows)
        (g0, _), (g1, h1), (g2, h2), (g3, h3) = parts
        middle = c2 * g2 - s2 * h2
        p = c1 * g1 - s1 * h1 + c3 * g3 - s3 * h3
        q = s3 * g3 + c3 * h3 - s1 * g1 - c1 * h1
        plus, minus = g0 + middle, g0 - middle
        for t, value in enumerate((plus + p, minus + q, plus - p, minus - q)):
            out_ref[pl.ds(quarter * t + 256 * m, 256)] = value.astype(BF16)


def pixel_kernel(x_ref, beam_ref, table_ref, turn_ref, out_ref):
    blocks, rows, _ = x_ref.shape
    half = beam_ref.shape[1] // 2
    share = out_ref.shape[2]
    lane = lax.broadcasted_iota(jnp.int32, (rows, 128), 1)
    even = [x_ref[b] for b in range(blocks // 2)]
    straight, crossed = [], []
    for b in range(blocks // 2):
        odd = x_ref[blocks - 1 - b].astype(F32)
        moved = pltpu.roll(odd, 64, 1)
        turned = jnp.where(lane < 64, -moved, moved)
        if b == 0:
            odd = jnp.where(lane == 64, 0.0, odd)
            turned = jnp.where(lane == 64, 0.0, turned)
        straight.append(odd.astype(BF16))
        crossed.append(turned.astype(BF16))
    wide = [jnp.concatenate(part, 1) for part in (even, straight, crossed)]
    wide = jnp.concatenate(wide, 0)
    for part in range(half // share):
        lanes = pl.ds(share * part, share)
        got = dot(wide, table_ref[lanes, :], NT)
        by_even = got[:rows]
        by_odd = turn_ref[0:1, lanes] * got[rows : 2 * rows] + turn_ref[1:2, lanes] * got[2 * rows :]
        out_ref[part] = (beam_ref[:, lanes] * (by_even + by_odd)).astype(BF16)
        late = pl.ds(half + share * part, share)
        out_ref[part + half // share] = (beam_ref[:, late] * (by_even - by_odd)).astype(BF16)


def sum_kernel(points, me_ref, starts_ref, terms_ref, mine_ref, theirs_ref):
    pointings, rows, share = terms_ref.shape
    ptg, core = me_ref[0], me_ref[1]
    lane = lax.broadcasted_iota(jnp.int32, (rows, share), 1)
    for ref, side in ((mine_ref, core), (theirs_ref, 1 - core)):
        for turn in range(2):
            lap = 2 * side + jnp.where(ptg % 2 == turn, 0, 1)
            column = lane + (lap * points + ptg * share)
            total = jnp.zeros((rows, share), F32)
            for p in range(pointings):
                inside = (column >= starts_ref[p]) & (column < starts_ref[p] + points)
                total += jnp.where(inside, terms_ref[p].astype(F32), 0.0)
            ref[turn] = total.astype(BF16)


def call(kernel, outs, specs, *args, scratch=(), flops=0, moved=4 << 20, limit=16):
    return pl.pallas_call(
        kernel,
        out_shape=outs,
        in_specs=specs,
        out_specs=jax.tree.map(lambda _: VMEM, outs),
        scratch_shapes=list(scratch),
        compiler_params=pltpu.CompilerParams(vmem_limit_bytes=limit << 20),
        cost_estimate=pl.CostEstimate(flops=flops, bytes_accessed=moved, transcendentals=0),
    )(*args)


def shape(*dims, dtype=BF16):
    return jax.ShapeDtypeStruct(dims, dtype)


IMG = ("s", "b")


def shards(image, beam, counts, offsets):
    points = counts.shape[1]
    laps, parts = lax.axis_size("s"), lax.axis_size("b")
    devices = laps * parts
    pointings = lax.axis_size("ptg")
    rows = points // devices
    tile = image.shape[1]
    me = lax.axis_index(IMG).astype(jnp.int32)
    ptg = lax.axis_index("ptg").astype(jnp.int32)
    start = offsets[0]
    place = me.reshape(1)

    starts = jnp.where(jnp.arange(pointings) == ptg, start, 0)
    share_rows = rows // pointings
    shares = call(
        cut_kernel,
        shape(devices, share_rows, tile),
        [SMEM, pl.BlockSpec(memory_space=pl.ANY)],
        ptg.reshape(1),
        image,
        scratch=[pltpu.SemaphoreType.DMA((devices,))],
        moved=1 << 19,
        limit=60,
    ).reshape(laps, parts, share_rows, tile)
    send, edge = call(
        choose_kernel,
        (shape(points // 2, 128), shape(points // 128, 128)),
        [SMEM, VMEM],
        place,
        counts[0],
        flops=points * 128 * 512,
    )
    shares, send = lax.optimization_barrier((shares, send))
    shares = lax.all_to_all(shares, "s", split_axis=0, concat_axis=0, tiled=True)
    near = [
        lax.ppermute(starts, "ptg", [(p, p ^ bit) for p in range(pointings)]) for bit in (1, 2, 3)
    ]
    starts = starts + near[0] + near[1] + near[2]
    starts = starts + lax.ppermute(starts, "ptg", [(p, p ^ 4) for p in range(pointings)])
    got = lax.ppermute(send, IMG, [(i, devices - 1 - i) for i in range(devices)])
    edge = lax.ppermute(
        edge,
        IMG,
        [(i, (devices - i) % (devices // 2)) for i in range(devices // 2, devices)],
    )
    weight = call(
        weight_kernel,
        shape(points, 128),
        [SMEM] + [VMEM] * 3,
        place,
        counts[0],
        got,
        edge,
        scratch=[pltpu.VMEM((points, 128), BF16), pltpu.VMEM((points, 128), F32)],
        flops=points * 128 * 1024,
    )

    twice = jnp.concatenate([beam[0], beam[0]], 1)
    turned = lax.dynamic_slice_in_dim(twice, (points - start % points) % points, points, 1)
    picked = call(
        functools.partial(pick_kernel, points),
        shape(pointings, parts, share_rows, tile),
        [SMEM, SMEM, VMEM],
        lax.axis_index("b").astype(jnp.int32).reshape(1),
        starts,
        shares,
        moved=1 << 20,
    )
    picked, got, edge = lax.optimization_barrier((picked, got, edge))
    window = lax.all_to_all(
        picked.reshape(pointings * parts, share_rows, tile),
        ("ptg", "b"),
        split_axis=0,
        concat_axis=0,
        tiled=True,
    ).reshape(pointings, parts, share_rows, tile)
    seat = jnp.stack([ptg, me % 2])
    window, weight, turned, seat, starts = lax.optimization_barrier(
        (window, weight, turned, seat, starts)
    )
    across, turn = bf16(row_table(points, devices)), jnp.asarray(row_turn(points))
    spectrum = call(
        row_kernel,
        shape(devices, rows, 128),
        [VMEM] * 4,
        window,
        turned,
        across,
        turn,
        flops=rows * points * points,
    )
    col = lax.all_to_all(spectrum, IMG, split_axis=0, concat_axis=0, tiled=True)
    back = call(
        column_kernel,
        shape(points, 128),
        [SMEM] + [VMEM] * 4,
        place,
        col.reshape(points, 128),
        weight,
        bf16(column_table(points)),
        jnp.asarray(column_turn(points)),
        scratch=[pltpu.VMEM((8, points // 4, 256), BF16)],
        flops=4 * points * points * 128,
    )
    lines = lax.all_to_all(
        back.reshape(devices, rows, 128), IMG, split_axis=0, concat_axis=0, tiled=True
    )
    share = points // pointings
    contribution = call(
        pixel_kernel,
        shape(pointings, rows, share),
        [VMEM] * 4,
        lines,
        turned,
        across,
        turn,
        flops=rows * points * points,
    )
    terms = lax.all_to_all(contribution, "ptg", split_axis=0, concat_axis=0, tiled=True)
    mine, theirs = call(
        functools.partial(sum_kernel, points),
        (shape(2, rows, share), shape(2, rows, share)),
        [SMEM, SMEM, VMEM],
        seat,
        starts,
        terms,
        moved=1 << 20,
    )
    other = lax.ppermute(theirs, IMG, [(i, i ^ 1) for i in range(devices)])
    per_lap = parts
    halves = tile // share
    received = []
    for turn in range(2):
        pairs = []
        for q in range(pointings):
            for i in range(devices):
                lap = 2 * (i % 2) + (turn ^ (q % 2))
                pairs.append((q * devices + i, (i // 2) * devices + per_lap * lap + q // halves))
        block = jnp.concatenate([mine[turn], other[turn]], 0)
        received.append(lax.ppermute(block, ("ptg", *IMG), pairs))
    lap = me // per_lap
    out = jnp.where(
        lap % 2 == 1,
        jnp.concatenate([received[1], received[0]], 1),
        jnp.concatenate([received[0], received[1]], 1),
    ).astype(F32)
    flipped = jnp.concatenate([out[rows:], out[:rows]], 0)
    return jnp.where(lap >= 2, flipped, out)


def solution(mesh):
    pointings, devices = mesh.devices.shape
    split = Mesh(mesh.devices.reshape(pointings, 4, devices // 4), ("ptg", *IMG))
    return jax.shard_map(
        shards,
        mesh=split,
        in_specs=(P(None, IMG), P("ptg", IMG, None), P("ptg", None, IMG), P("ptg")),
        out_specs=P("ptg", IMG),
        check_vma=False,
    )
```
